32 devices in a mesh: section: 2 (over x), tensor: 2 (over y), ctx: 8 (over z, core).
Axes of the slice: x: 2, y: 2, z: 4, core: 2. Of those that a mesh axis runs over, the one named last changes fastest.
Arguments:
- block_input: bfloat16 [4, 1024, 1536], P(None, 'ctx'), may hold values from -6 to 6
- positions: int32 [4, 1024], P(None, 'ctx'), may hold values from 0 to 1023, as said below
- cotangent: bfloat16 [4, 1024, 1536], P(None, 'ctx'), may hold values from -6 to 6
- norm_attn: bfloat16 [2, 1536], P('section', 'ctx'), may hold values from 0.5 to 1.5
- w_qkv: bfloat16 [2, 1536, 2, 1024], P('section', 'ctx', 'tensor'), may hold values from -0.15625 to 0.15625
- b_qkv: bfloat16 [2, 2, 1024], P('section', 'tensor', 'ctx'), may hold values from -3 to 3
- w_out: bfloat16 [2, 2, 768, 1536], P('section', 'tensor', 'ctx'), may hold values from -3.5 to 3.5
- norm_mlp: bfloat16 [2, 1536], P('section', 'ctx'), may hold values from 0.5 to 1.5
- w_gate_up: bfloat16 [2, 1536, 2, 8960], P('section', 'ctx', None, 'tensor'), may hold values from -0.15625 to 0.15625
- w_down: bfloat16 [2, 8960, 1536], P('section', ('tensor', 'ctx')), may hold values from -0.125 to 0.125
Outputs:
- section_output: bfloat16 [2, 4, 1024, 1536], P('section', None, 'ctx')
- input_grad: bfloat16 [2, 4, 1024, 1536], P('section', None, 'ctx')
- grad_norm_attn: float32 [2, 1536], P('section', 'ctx')
- grad_w_qkv: float32 [2, 1536, 2, 1024], P('section', 'ctx', 'tensor')
- grad_b_qk: float32 [2, 2, 896], P('section', 'tensor', 'ctx')
- grad_b_v: float32 [2, 2, 128], P('section', 'tensor', 'ctx')
- grad_w_out: float32 [2, 2, 768, 1536], P('section', 'tensor', 'ctx')
- grad_norm_mlp: float32 [2, 1536], P('section', 'ctx')
- grad_w_gate_up: float32 [2, 1536, 2, 8960], P('section', 'ctx', None, 'tensor')
- grad_w_down: float32 [2, 8960, 1536], P('section', ('tensor', 'ctx'))
The draws below stay inside these ranges and needn't reach their ends.
Inputs may be any that keep to these rules, and one draw needn't show every extreme that they name: In every micro-batch each position of 0 to 1023 appears once; the 128 tokens of one index of ctx are two runs of 64 consecutive positions in rising order, sequence blocks b and 15 - b of size 64, with b differing between devices.
All inputs are finite; a program needn't handle non-finite values.
Results may differ from the reference program's by a relative error of at most 0.04.
Values may be sent and summed in bfloat16 or wider, within the bound.
A program may use at most 320 MiB of HBM per device.

```python
import math
import jax
import jax.numpy as jnp
from jax import lax

D = 1536
KVH = 2
HD = 128
FF = 8960
TOK_DEV = 128
MB = 4
LAYERS = 2
SEQ = 1024
QW = 768
GW = 1024


def draw_positions(key, part):
    half_size = TOK_DEV // 2
    span_count = SEQ // TOK_DEV
    sequences = []
    for micro_index in range(MB):
        shuffled = jax.random.permutation(jax.random.fold_in(key, 17 + micro_index), span_count)
        mirrored = 2 * span_count - 1 - shuffled
        blocks = jnp.stack([shuffled, mirrored], axis=1)
        offsets = jnp.arange(half_size, dtype=jnp.int32)
        tokens_pos = blocks[:, :, None] * half_size + offsets[None, None, :]
        sequences.append(tokens_pos.reshape(span_count * TOK_DEV))
    return jnp.stack(sequences).astype(jnp.int32)


def block_scale(key, shape, cuts, low, largest):
    gain, own = 1.0, jax.random.fold_in(key, 6)
    for dim, parts in cuts:
        draws = jnp.exp(jax.random.uniform(jax.random.fold_in(own, dim), (parts,), jnp.float32, low / len(cuts), largest / len(cuts)))
        gain = gain * jnp.repeat(draws, shape[dim] // parts).reshape([-1 if axis == dim else 1 for axis in range(len(shape))])
    return gain


def scatter_about(stream_key, shape, spread, most, shards=(), kind=jnp.bfloat16):
    values = jax.random.normal(stream_key, shape, jnp.float32) * spread
    if len(shards) > 0:
        values = block_scale(stream_key, shape, shards, -0.22, 0.18) * values
    return jnp.clip(values, min=-most, max=most).astype(kind)


def setup_inputs(seed: int = 0) -> dict:
    streams_of = jax.random.split(jax.random.key(seed), 11)
    block_input = scatter_about(streams_of[0], (MB, SEQ, D), 1.0, 6.0, ((1, 8),))
    positions = draw_positions(jax.random.fold_in(streams_of[10], 71), 0)
    cotangent = scatter_about(streams_of[2], (MB, SEQ, D), 1.0, 6.0, ((1, 8),))
    norm_attn = jnp.clip(1.0 + 0.1 * jax.random.normal(streams_of[3], (LAYERS, D), jnp.float32), 0.5, 1.5).astype(jnp.bfloat16)
    w_qkv = scatter_about(streams_of[4], (LAYERS, D, KVH, GW), D ** -0.5, 0.15625, ((0, 2), (1, 8), (2, 2)))
    b_qkv = scatter_about(streams_of[5], (LAYERS, KVH, GW), 0.5, 3.0, ((0, 2), (1, 2), (2, 8)))
    w_out = scatter_about(streams_of[6], (LAYERS, KVH, QW, D), (max(1, 4 * QW // SEQ)) ** -0.5, 3.5, ((0, 2), (1, 2), (2, 8)))
    norm_mlp = jnp.clip(1.0 + 0.1 * jax.random.normal(streams_of[7], (LAYERS, D), jnp.float32), 0.5, 1.5).astype(jnp.bfloat16)
    w_gate_up = scatter_about(streams_of[8], (LAYERS, D, 2, FF), D ** -0.5, 0.15625, ((0, 2), (1, 8), (3, 2)))
    w_down = scatter_about(streams_of[9], (LAYERS, FF, D), (FF // 4) ** -0.5, 0.125, ((0, 2), (1, 16)))
    return dict(block_input=block_input, positions=positions, cotangent=cotangent, norm_attn=norm_attn, w_qkv=w_qkv, b_qkv=b_qkv, w_out=w_out, norm_mlp=norm_mlp, w_gate_up=w_gate_up, w_down=w_down)


@jax.custom_vjp
def low(v):
    return lax.optimization_barrier(v.astype(jnp.bfloat16)).astype(jnp.float32)

@jax.custom_vjp
def low_back(v):
    return v

def low_keep(v):
    return (low(v), None)

def low_pass(kept, grad):
    return (grad,)

def back_keep(v):
    return (v, None)

def back_low(kept, grad):
    return (low(grad),)
low.defvjp(low_keep, low_pass)
low_back.defvjp(back_keep, back_low)
EPSILON = 1e-06
ROPE_BASE = 1000000.0
HIGHEST = lax.Precision.HIGHEST

def angles(positions, head_dim):
    half_dim = head_dim // 2
    frequency = ROPE_BASE ** (-(jnp.arange(half_dim, dtype=jnp.float32) * 2.0) / head_dim)
    phases = positions.astype(jnp.float32)[:, None] * frequency[None, :]
    phases = jnp.concatenate([phases, phases], axis=-1)
    return (jnp.cos(phases), jnp.sin(phases))

def rotate(values, cosine_table, sine_table):
    half_dim = values.shape[-1] // 2
    turned = jnp.concatenate([-values[..., half_dim:], values[..., :half_dim]], axis=-1)
    return values * cosine_table + turned * sine_table

def rms_norm(values, gain_row):
    return values * lax.rsqrt(lax.optimization_barrier(jnp.mean(values * values, axis=-1, keepdims=True)) + EPSILON) * gain_row

def attend(queries, key_part, value_part, positions):
    block_size = min(512, queries.shape[0])
    block_count = queries.shape[0] // block_size
    factor = 1.0 / math.sqrt(HD)

    def one_block(inputs):
        query_block, row_pos = inputs
        raw_scores = jnp.einsum('qgjd,kgd->gjqk', query_block, key_part, precision=HIGHEST)
        scores = low_back(raw_scores) * factor
        scores = jnp.where(row_pos[:, None] >= positions[None, :], scores, -1e+30)
        weights_low = low(jax.nn.softmax(scores, axis=-1))
        return jnp.einsum('gjqk,kgd->qgjd', weights_low, value_part, precision=HIGHEST)
    block_outs = lax.map(jax.checkpoint(one_block), (queries.reshape((block_count, block_size) + queries.shape[1:]), positions.reshape(block_count, block_size)))
    return block_outs.reshape(queries.shape)

def layer_pass(values, weights, positions):
    norm_attn, w_qkv, b_qkv, w_out, norm_mlp, w_gate_up, w_down = weights
    cosine_table, sine_table = angles(positions, HD)
    normed = low(rms_norm(values, norm_attn))
    mixed_proj = low_back(jnp.einsum('sd,dgc->sgc', normed, w_qkv, precision=HIGHEST) + b_qkv)
    queries = mixed_proj[..., :QW].reshape(SEQ, KVH, QW // HD, HD)
    queries = low(rotate(queries, cosine_table[:, None, None, :], sine_table[:, None, None, :]))
    key_part = low(rotate(mixed_proj[..., QW:QW + HD], cosine_table[:, None, :], sine_table[:, None, :]))
    value_part = low(mixed_proj[..., QW + HD:])
    attended = attend(queries, key_part, value_part, positions).reshape(SEQ, KVH, QW)
    attended = low(low_back(attended))
    middle = values + low_back(jnp.einsum('sgc,gcd->sd', attended, w_out, precision=HIGHEST))
    normed_mlp = low(rms_norm(middle, norm_mlp))
    gate_up = low_back(jnp.einsum('sd,dcf->scf', normed_mlp, w_gate_up, precision=HIGHEST))
    hidden = low(jax.nn.silu(gate_up[:, 0]) * gate_up[:, 1])
    return middle + low_back(jnp.dot(hidden, w_down, precision=HIGHEST))

def reference(block_input, positions, cotangent, norm_attn, w_qkv, b_qkv, w_out, norm_mlp, w_gate_up, w_down):
    params = tuple((weight.astype(jnp.float32) for weight in (norm_attn, w_qkv, b_qkv, w_out, norm_mlp, w_gate_up, w_down)))
    first_input = block_input.astype(jnp.float32)
    section_probe = jnp.zeros_like(first_input)

    def forward(first_input, section_probe, params):
        layer_zero = tuple((weight[0] for weight in params))
        layer_one = tuple((weight[1] for weight in params))
        first_outs = []
        final_outs = []
        for batch_index in range(MB):
            handed = low(layer_pass(first_input[batch_index], layer_zero, positions[batch_index]))
            final_out = layer_pass(low_back(handed) + section_probe[batch_index], layer_one, positions[batch_index])
            first_outs.append(handed)
            final_outs.append(final_out)
        return (jnp.stack(first_outs), jnp.stack(final_outs))
    (first_stack, final_stack), pullback = jax.vjp(forward, first_input, section_probe, params)
    grad_input, grad_probe, grad_params = pullback((jnp.zeros_like(first_stack), cotangent.astype(jnp.float32)))
    section_output = jnp.stack([first_stack, final_stack]).astype(jnp.bfloat16)
    input_grad = jnp.stack([grad_input, grad_probe]).astype(jnp.bfloat16)
    bias_grad = grad_params[2]
    return (section_output, input_grad, grad_params[0], grad_params[1], bias_grad[..., :QW + HD], bias_grad[..., QW + HD:], grad_params[3], grad_params[4], grad_params[5], grad_params[6])
```

```python
import functools
import math

import jax
import jax.numpy as jnp
from jax import lax
from jax.sharding import PartitionSpec as P

EPSILON = 1e-06
ROPE_BASE = 1000000.0
ROWS = (((0,), (0,)), ((), ()))
LAST = (((1,), (1,)), ((), ()))
F32 = jnp.float32
BF16 = jnp.bfloat16
SWAP = [(0, 1), (1, 0)]


def dot(a, b, dims=(((1,), (0,)), ((), ()))):
    return lax.dot_general(a, b, dims, preferred_element_type=F32)


def angles(positions, head_dim):
    half_dim = head_dim // 2
    frequency = ROPE_BASE ** (-(jnp.arange(half_dim, dtype=F32) * 2.0) / head_dim)
    phases = positions.astype(F32)[:, None] * frequency[None, :]
    phases = jnp.concatenate([phases, phases], axis=-1)
    return jnp.cos(phases), jnp.sin(phases)


def rotate(values, cosine, sine):
    half = values.shape[-1] // 2
    turned = jnp.concatenate([-values[..., half:], values[..., :half]], axis=-1)
    return values * cosine + turned * sine


def unrotate(grads, cosine, sine):
    half = grads.shape[-1] // 2
    twisted = grads * sine
    turned = jnp.concatenate([twisted[..., half:], -twisted[..., :half]], axis=-1)
    return grads * cosine + turned


def inverse_root(values):
    return lax.rsqrt(jnp.mean(values * values, axis=-1, keepdims=True) + EPSILON)


def norm_backward(values, root, gain, grad_normed):
    normal = values * root
    gain_grad = jnp.sum(grad_normed * normal, axis=0)
    scaled = grad_normed * gain
    mean = jnp.mean(scaled * normal, axis=-1, keepdims=True)
    return root * (scaled - normal * mean), gain_grad


def swap(value):
    return lax.ppermute(value, "section", SWAP)


def gather_ctx(value, axis):
    return lax.all_gather(value, "ctx", axis=axis, tiled=True)


def gather_tokens(rows):
    return lax.all_gather(rows, ("tensor", "ctx"), axis=0, tiled=True)


def scatter_tokens(rows):
    return lax.psum_scatter(rows, ("tensor", "ctx"), scatter_dimension=0, tiled=True).astype(F32)


def tensor_gather(rows):
    return lax.all_gather(rows, "tensor", axis=0, tiled=True)


def tensor_scatter(rows):
    return lax.psum_scatter(
        rows.astype(BF16), "tensor", scatter_dimension=0, tiled=True
    ).astype(F32)


def attend(queries, kv, query_pos, key_pos, head_dim):
    factor = 1.0 / math.sqrt(head_dim)
    keys, values = kv[..., :head_dim], kv[..., head_dim:]
    scores = jnp.einsum("bqhd,bkd->bhqk", queries, keys, preferred_element_type=F32)
    allowed = query_pos[:, None, :, None] >= key_pos[:, None, None, :]
    scores = jnp.where(allowed, scores * factor, -1e30)
    log_total = jax.nn.logsumexp(scores, axis=-1)
    probs = jnp.exp(scores - log_total[..., None]).astype(BF16)
    out = jnp.einsum("bhqk,bkd->bqhd", probs, values, preferred_element_type=F32)
    return out, log_total


def attend_backward(queries, kv, query_pos, key_pos, head_dim, log_total, grads, delta):
    factor = 1.0 / math.sqrt(head_dim)
    keys, values = kv[..., :head_dim], kv[..., head_dim:]
    scores = jnp.einsum("bqhd,bkd->bhqk", queries, keys, preferred_element_type=F32)
    allowed = query_pos[:, None, :, None] >= key_pos[:, None, None, :]
    scores = jnp.where(allowed, scores * factor, -1e30)
    probs = jnp.exp(scores - log_total[..., None])
    grad_probs = jnp.einsum("bqhd,bkd->bhqk", grads, values, preferred_element_type=F32)
    grad_scores = (probs * (grad_probs - delta[..., None]) * factor).astype(BF16)
    grad_q = jnp.einsum("bhqk,bkd->bqhd", grad_scores, keys, preferred_element_type=F32)
    grad_k = jnp.einsum("bhqk,bqhd->bkd", grad_scores, queries, preferred_element_type=F32)
    grad_v = jnp.einsum("bhqk,bqhd->bkd", probs.astype(BF16), grads, preferred_element_type=F32)
    return grad_q, jnp.concatenate([grad_k, grad_v], axis=-1)


def layer_forward(x_low, weights, tables):
    gain_attn, w_mixed, bias, w_project, gain_mlp, w_expand, w_reduce = weights
    cosine, sine, query_pos, key_pos, mine = tables
    count, width = x_low.shape
    query_width = w_project.shape[0]
    head_dim = (w_mixed.shape[1] - query_width) // 2
    heads = query_width // head_dim
    batch = query_pos.shape[0]
    tokens = count // batch
    x = x_low.astype(F32)
    root_attn = inverse_root(x)
    normed = (x * root_attn * gain_attn).astype(BF16)
    mixed = dot(normed, w_mixed) + bias
    queries = rotate(
        mixed[:, :query_width].reshape(count, heads, head_dim),
        cosine[:, None, :],
        sine[:, None, :],
    ).astype(BF16)
    queries = queries.reshape(batch, tokens, heads, head_dim)
    keys = rotate(mixed[:, query_width : query_width + head_dim], cosine, sine)
    kv = jnp.concatenate([keys, mixed[:, query_width + head_dim :]], axis=1).astype(BF16)
    kv = gather_ctx(kv.reshape(batch, tokens, 2 * head_dim), 1)
    attended_full, log_total = attend(queries, kv, query_pos, key_pos, head_dim)
    attended = attended_full.astype(BF16).reshape(count, query_width)
    x_mine = lax.dynamic_slice_in_dim(x, mine * tokens, tokens, 0)
    middle = x_mine + tensor_scatter(dot(attended, w_project))
    root_mlp = inverse_root(middle)
    normed_mlp = (middle * root_mlp * gain_mlp).astype(BF16)
    all_normed = gather_tokens(normed_mlp)
    gate = dot(all_normed, w_expand[0])
    up = dot(all_normed, w_expand[1])
    hidden = (jax.nn.silu(gate) * up).astype(BF16)
    result = middle + scatter_tokens(dot(hidden, w_reduce).astype(BF16))
    kept = (
        x_mine,
        lax.dynamic_slice_in_dim(root_attn, mine * tokens, tokens, 0),
        normed,
        queries,
        kv,
        attended_full,
        log_total,
        attended,
        middle,
        root_mlp,
        all_normed,
        gate,
        up,
        hidden,
    )
    return result.astype(BF16), kept


def layer_backward(grad_out, kept, weights, tables):
    gain_attn, w_mixed, bias, w_project, gain_mlp, w_expand, w_reduce = weights
    cosine, sine, query_pos, key_pos, mine = tables
    (
        x_mine,
        root_attn,
        normed,
        queries,
        kv,
        attended_full,
        log_total,
        attended,
        middle,
        root_mlp,
        all_normed,
        gate,
        up,
        hidden,
    ) = kept
    batch, tokens, heads, head_dim = queries.shape
    count = batch * tokens
    grad_mlp = gather_tokens(grad_out.astype(BF16))
    grad_hidden = dot(grad_mlp, w_reduce, LAST)
    sig = jax.nn.sigmoid(gate)
    grad_gate = (grad_hidden * up * sig * (1.0 + gate * (1.0 - sig))).astype(BF16)
    grad_up = (grad_hidden * (gate * sig)).astype(BF16)
    part = dot(grad_gate, w_expand[0], LAST) + dot(grad_up, w_expand[1], LAST)
    grad_normed_mlp = scatter_tokens(part.astype(BF16))
    d_reduce = dot(hidden, grad_mlp, ROWS)
    d_expand = jnp.stack([dot(all_normed, grad_gate, ROWS), dot(all_normed, grad_up, ROWS)])
    grad_middle, d_gain_mlp = norm_backward(middle, root_mlp, gain_mlp, grad_normed_mlp)
    grad_middle = grad_middle + grad_out
    grad_branch = tensor_gather(grad_middle.astype(BF16))
    d_project = dot(attended, grad_branch, ROWS)
    grad_attended = dot(grad_branch, w_project, LAST).astype(BF16)
    grad_attended = grad_attended.reshape(batch, tokens, heads, head_dim)
    delta = jnp.sum(grad_attended.astype(F32) * attended_full, axis=-1)
    grad_q, grad_kv = attend_backward(
        queries,
        kv,
        query_pos,
        key_pos,
        head_dim,
        log_total,
        grad_attended,
        jnp.swapaxes(delta, 1, 2),
    )
    grad_kv = lax.psum_scatter(
        grad_kv.astype(BF16), "ctx", scatter_dimension=1, tiled=True
    ).astype(F32)
    grad_kv = grad_kv.reshape(count, 2 * head_dim)
    grad_q = unrotate(
        grad_q.reshape(count, heads, head_dim), cosine[:, None, :], sine[:, None, :]
    )
    grad_k = unrotate(grad_kv[:, :head_dim], cosine, sine)
    grad_mixed = jnp.concatenate(
        [grad_q.reshape(count, heads * head_dim), grad_k, grad_kv[:, head_dim:]], axis=1
    ).astype(BF16)
    d_mixed = dot(normed, grad_mixed, ROWS)
    d_bias = jnp.sum(grad_mixed.astype(F32), axis=0)
    grad_normed = tensor_scatter(dot(grad_mixed, w_mixed, LAST))
    grad_x, d_gain_attn = norm_backward(x_mine, root_attn, gain_attn, grad_normed)
    grad_x = (grad_x + grad_middle).astype(BF16)
    return grad_x, (d_gain_attn, d_mixed, d_bias, d_project, d_gain_mlp, d_expand, d_reduce)


def shards(
    block_input, positions, cotangent, norm_attn, w_qkv, b_qkv, w_out, norm_mlp, w_gate_up, w_down
):
    section = lax.axis_index("section")
    tensor = lax.axis_index("tensor")
    ctx = lax.axis_index("ctx")
    ctx_size = lax.axis_size("ctx")
    first = section == 0
    micro, tokens, width = block_input.shape
    half = micro // 2
    head_dim = w_qkv.shape[3] - w_out.shape[2] * ctx_size
    head_dim = head_dim // 2
    slice_width = norm_attn.shape[1]
    slice_bias = b_qkv.shape[2]
    units = w_down.shape[1]

    def plane_part(value):
        return lax.dynamic_slice_in_dim(value, section * half, half, 0)

    def layers(own, other):
        return jnp.where(first, own, other), jnp.where(first, other, own)

    x = plane_part(block_input).reshape(half * tokens, width)
    pos_local = plane_part(positions)
    pos_all = gather_ctx(pos_local, 1)
    cosine, sine = angles(pos_local.reshape(-1), head_dim)
    tables = (cosine, sine, pos_local, pos_all, tensor)

    small = jnp.concatenate([norm_attn[0], norm_mlp[0], b_qkv[0, 0]])
    qkv, out = w_qkv[0, :, 0, :], w_out[0, 0]
    expand = jnp.transpose(
        w_gate_up[0].reshape(slice_width, 2, ctx_size, units), (2, 1, 0, 3)
    )
    expand = lax.all_to_all(expand, "ctx", split_axis=0, concat_axis=0, tiled=True)
    expand = jnp.transpose(expand, (1, 0, 2, 3)).reshape(2, width, units)
    small0, small1 = layers(small, swap(small))
    qkv0, qkv1 = layers(qkv, swap(qkv))
    out0, out1 = layers(out, swap(out))
    expand0, expand1 = layers(expand, swap(expand))
    down0, down1 = layers(w_down[0], swap(w_down[0]))

    def whole(small, qkv, out, expand, down):
        small = gather_ctx(small[None], 0)
        return (
            small[:, :slice_width].reshape(1, width),
            gather_ctx(qkv, 0),
            small[:, 2 * slice_width :].reshape(1, slice_bias * ctx_size),
            gather_ctx(out, 0),
            small[:, slice_width : 2 * slice_width].reshape(1, width),
            expand,
            down,
        )

    weights0 = whole(small0, qkv0, out0, expand0, down0)
    weights1 = whole(small1, qkv1, out1, expand1, down1)

    result0, kept0 = layer_forward(x, weights0, tables)
    x1 = tensor_gather(result0)
    result1, kept1 = layer_forward(x1, weights1, tables)
    out1_all = tensor_gather(result1)

    def exchange(layer0, layer1):
        kept_here = jnp.where(first, layer0, layer1)
        received = swap(jnp.where(first, layer1, layer0))
        low = jnp.where(first, kept_here, received)
        high = jnp.where(first, received, kept_here)
        both = jnp.concatenate([low, high], axis=0)
        return both.reshape(1, micro, tokens, width)

    section_output = exchange(x1, out1_all)

    seed = lax.dynamic_slice_in_dim(cotangent, section * half + tensor, 1, 0)[0].astype(F32)
    grad1, d1 = layer_backward(seed, kept1, weights1, tables)
    grad0, d0 = layer_backward(grad1.astype(F32), kept0, weights0, tables)
    input_grad = exchange(tensor_gather(grad0), tensor_gather(grad1))

    def to_owner(part0, part1):
        return jnp.where(first, part0, part1), jnp.where(first, part1, part0).astype(BF16)

    def over_section(part0, part1):
        own, other = to_owner(part0, part1)
        return own + swap(other).astype(F32)

    d_expand = over_section(d0[5], d1[5])
    d_expand = d_expand.astype(BF16).reshape(2, ctx_size, slice_width, units)
    d_expand = lax.all_to_all(
        jnp.transpose(d_expand, (1, 0, 2, 3)), "ctx", split_axis=0, concat_axis=0, tiled=True
    )
    d_expand = jnp.transpose(d_expand, (2, 1, 0, 3)).reshape(
        1, slice_width, 2, ctx_size * units
    ).astype(F32)
    d_reduce = over_section(d0[6], d1[6])

    def ctx_scatter(value):
        return lax.psum_scatter(
            value.astype(BF16), "ctx", scatter_dimension=0, tiled=True
        ).astype(F32)

    d_mixed = over_section(ctx_scatter(d0[1]), ctx_scatter(d1[1]))
    d_project = over_section(ctx_scatter(d0[3]), ctx_scatter(d1[3]))
    gains = jnp.stack([jnp.stack([d0[0], d0[4]]), jnp.stack([d1[0], d1[4]])])
    gains = lax.psum(gains, ("section", "tensor", "ctx"))
    gains = lax.dynamic_slice(
        gains, (section, 0, ctx * slice_width), (1, 2, slice_width)
    )
    biases = lax.psum(jnp.stack([d0[2], d1[2]]), ("section", "ctx"))
    biases = lax.dynamic_slice_in_dim(biases, section, 1, 0)
    split_at = biases.shape[1] - head_dim
    bias_qk = lax.dynamic_slice_in_dim(
        biases[:, :split_at], ctx * (split_at // ctx_size), split_at // ctx_size, 1
    )
    bias_v = lax.dynamic_slice_in_dim(
        biases[:, split_at:], ctx * (head_dim // ctx_size), head_dim // ctx_size, 1
    )
    return (
        section_output,
        input_grad,
        gains[:, 0],
        d_mixed[None, :, None, :],
        bias_qk[None],
        bias_v[None],
        d_project[None, None],
        gains[:, 1],
        d_expand,
        d_reduce[None],
    )


def solution(mesh):
    in_specs = (
        P(None, "ctx", None),
        P(None, "ctx"),
        P(None, "ctx", None),
        P("section", "ctx"),
        P("section", "ctx", "tensor", None),
        P("section", "tensor", "ctx"),
        P("section", "tensor", "ctx", None),
        P("section", "ctx"),
        P("section", "ctx", None, "tensor"),
        P("section", ("tensor", "ctx"), None),
    )
    out_specs = (
        P("section", None, "ctx", None),
        P("section", None, "ctx", None),
        P("section", "ctx"),
        P("section", "ctx", "tensor", None),
        P("section", "tensor", "ctx"),
        P("section", "tensor", "ctx"),
        P("section", "tensor", "ctx", None),
        P("section", "ctx"),
        P("section", "ctx", None, "tensor"),
        P("section", ("tensor", "ctx"), None),
    )
    return jax.shard_map(shards, mesh=mesh, in_specs=in_specs, out_specs=out_specs, check_vma=False)
```

```python
import functools
import functools
import math

import jax
import jax.numpy as jnp
from jax import lax
from jax.experimental import pallas as pl
from jax.experimental.pallas import tpu as pltpu
from jax.sharding import PartitionSpec as P

EPSILON = 1e-06
ROPE_BASE = 1000000.0
ROWS = (((0,), (0,)), ((), ()))
LAST = (((1,), (1,)), ((), ()))
F32 = jnp.float32
BF16 = jnp.bfloat16
SWAP = [(0, 1), (1, 0)]
MESH = pl.DeviceIdType.MESH
VMEM = pl.BlockSpec(memory_space=pltpu.VMEM)
HBM = pl.BlockSpec(memory_space=pl.ANY)


def dot(a, b, dims=(((1,), (0,)), ((), ()))):
    return lax.dot_general(a, b, dims, preferred_element_type=F32)


def angles(positions, head_dim):
    half_dim = head_dim // 2
    frequency = ROPE_BASE ** (-(jnp.arange(half_dim, dtype=F32) * 2.0) / head_dim)
    phases = positions.astype(F32)[:, None] * frequency[None, :]
    phases = jnp.concatenate([phases, phases], axis=-1)
    return jnp.cos(phases), jnp.sin(phases)


def rotate(values, cosine, sine):
    half = values.shape[-1] // 2
    turned = jnp.concatenate([-values[..., half:], values[..., :half]], axis=-1)
    return values * cosine + turned * sine


def unrotate(grads, cosine, sine):
    half = grads.shape[-1] // 2
    twisted = grads * sine
    turned = jnp.concatenate([twisted[..., half:], -twisted[..., :half]], axis=-1)
    return grads * cosine + turned


def inverse_root(values):
    return lax.rsqrt(jnp.mean(values * values, axis=-1, keepdims=True) + EPSILON)


def norm_backward(values, root, gain, grad_normed):
    normal = values * root
    gain_grad = jnp.sum(grad_normed * normal, axis=0)
    scaled = grad_normed * gain
    mean = jnp.mean(scaled * normal, axis=-1, keepdims=True)
    return root * (scaled - normal * mean), gain_grad


def swap(value):
    return lax.ppermute(value, "section", SWAP)


def gather_ctx(value, axis):
    return lax.all_gather(value, "ctx", axis=axis, tiled=True)


def gather_tokens(rows):
    return lax.all_gather(rows, ("ctx", "tensor"), axis=0, tiled=True)


def scatter_tokens(rows):
    return lax.psum_scatter(rows, ("ctx", "tensor"), scatter_dimension=0, tiled=True).astype(F32)


def tensor_gather(rows):
    return lax.all_gather(rows, "tensor", axis=0, tiled=True)


def tensor_scatter(rows):
    mine = lax.axis_index("tensor")
    tokens = rows.shape[0] // 2
    own = lax.dynamic_slice_in_dim(rows, mine * tokens, tokens, 0)
    other = lax.dynamic_slice_in_dim(rows, (1 - mine) * tokens, tokens, 0)
    return own + lax.ppermute(other.astype(BF16), "tensor", SWAP).astype(F32)


def greet_all(size, me):
    barrier = pltpu.get_barrier_semaphore()
    for step in range(1, size):
        pl.semaphore_signal(
            barrier, inc=1, device_id={"ctx": (me + step) % size}, device_id_type=MESH
        )
    there = 1 - lax.axis_index("section")
    pl.semaphore_signal(barrier, inc=1, device_id={"section": there}, device_id_type=MESH)
    pl.semaphore_wait(barrier, size)


def by_distance(size):
    return sorted(range(size), key=lambda step: min(step, size - step))


def share_kernel(size, from_ref, all_ref, send, recv, over_send, over_recv, local):
    me = lax.axis_index("ctx")
    section = lax.axis_index("section")
    greet_all(size, me)

    def copy(there, source):
        return remote(
            from_ref.at[:, there],
            all_ref.at[section, :, source],
            send.at[there],
            recv.at[source],
            {"ctx": there},
        )

    def over(block, source):
        return remote(
            block,
            all_ref.at[section, :, source],
            over_send.at[source],
            over_recv.at[source],
            {"section": 1 - section},
        )

    own = pltpu.make_async_copy(from_ref.at[:, me], all_ref.at[section, :, me], local)
    own.start()
    over(from_ref.at[:, me], me).start()
    order = by_distance(size)[1:]

    def pass_on(step):
        source = (me + size - step) % size
        copy(source, source).wait_recv()
        over(all_ref.at[section, :, source], source).start()
        copy((me + step) % size, me).wait_send()

    for index, step in enumerate(order):
        copy((me + step) % size, me).start()
        if index > 0:
            pass_on(order[index - 1])
    pass_on(order[-1])
    own.wait()
    for step in range(size):
        source = (me + step) % size
        over(all_ref.at[section, :, source], source).wait()


def share(blocks):
    size = blocks.shape[1]
    if size != 8:
        moved = lax.all_to_all(blocks, "ctx", split_axis=1, concat_axis=1, tiled=True)
        return lax.all_gather(moved, "section")
    dma = pltpu.SemaphoreType.DMA
    return pl.pallas_call(
        functools.partial(share_kernel, size),
        out_shape=jax.ShapeDtypeStruct((2,) + blocks.shape, blocks.dtype),
        in_specs=[HBM],
        out_specs=HBM,
        scratch_shapes=[dma((size,)), dma((size,)), dma((size,)), dma((size,)), dma],
        compiler_params=pltpu.CompilerParams(collective_id=5, has_side_effects=True),
        cost_estimate=pl.CostEstimate(flops=blocks.size, bytes_accessed=1024, transcendentals=0),
        name="share",
    )(blocks)


def collect_kernel(
    size, first_ref, second_ref, to_ref, own, other, send, recv, over_send, over_recv, local, store
):
    me = lax.axis_index("ctx")
    section = lax.axis_index("section")
    greet_all(size, me)
    order = by_distance(size)[::-1]

    def over(source_ref, at):
        return remote(
            source_ref.at[:, at], other.at[at], over_send.at[at], over_recv.at[at],
            {"section": 1 - section},
        )

    def load(source_ref, at):
        return pltpu.make_async_copy(source_ref.at[:, at], own.at[at], local.at[at])

    def copy(there, source):
        return remote(
            own.at[there], to_ref.at[:, source], send.at[there], recv.at[source], {"ctx": there}
        )

    def start(at):
        @pl.when(section == 0)
        def _():
            over(second_ref, at).start()
            load(first_ref, at).start()

        @pl.when(section == 1)
        def _():
            over(first_ref, at).start()
            load(second_ref, at).start()

    for index, step in enumerate(order):
        at = (me + step) % size
        if index == 0:
            start(at)
        if index + 1 < size:
            start((me + order[index + 1]) % size)
        over(first_ref, at).wait()
        load(first_ref, at).wait()
        own[at] = (own[at].astype(F32) + other[at].astype(F32)).astype(own.dtype)
        if step > 0:
            copy(at, me).start()
        else:
            mine = pltpu.make_async_copy(own.at[at], to_ref.at[:, me], store)
            mine.start()
            mine.wait()
    for step in order:
        at = (me + step) % size
        if step > 0:
            copy(at, at).wait_recv()
            copy(at, me).wait_send()


def collect(first, second, is_first):
    parts, size, rows, columns = first.shape
    if size != 8:
        received = lax.ppermute(jnp.where(is_first, second, first), "section", SWAP)
        total = jnp.where(is_first, first, second).astype(F32) + received.astype(F32)
        return lax.all_to_all(
            total.astype(BF16), "ctx", split_axis=1, concat_axis=1, tiled=True
        )
    dma = pltpu.SemaphoreType.DMA
    block = pltpu.VMEM((size, parts, rows, columns), first.dtype)
    return pl.pallas_call(
        functools.partial(collect_kernel, size),
        out_shape=jax.ShapeDtypeStruct(first.shape, first.dtype),
        in_specs=[HBM, HBM],
        out_specs=HBM,
        scratch_shapes=[block, block]
        + [dma((size,)), dma((size,)), dma((size,)), dma((size,)), dma((size,)), dma],
        compiler_params=pltpu.CompilerParams(
            collective_id=6, has_side_effects=True, vmem_limit_bytes=24 << 20
        ),
        cost_estimate=pl.CostEstimate(flops=first.size, bytes_accessed=1024, transcendentals=0),
        name="collect",
    )(first, second)


def remote(src, dst, send, recv, device):
    return pltpu.make_async_remote_copy(
        src_ref=src, dst_ref=dst, send_sem=send, recv_sem=recv, device_id=device, device_id_type=MESH
    )


def spread_kernel(chunk, piece, layer, planes, ins, outs, extra, own_ref, *refs):
    in_refs, refs = refs[:ins], refs[ins:]
    all_ref, sum_ref = refs[:2]
    out_refs, refs = refs[2 : 2 + outs], refs[2 + outs :]
    work_refs, refs = refs[:extra], refs[extra:]
    (expand_w, load_sem), refs = refs[:2], refs[2:]
    load = pltpu.make_async_copy(in_refs[0].at[layer], expand_w, load_sem)
    load.start()
    in_refs = (expand_w,) + in_refs[1:]
    (land, core_out, core_in, y_out, y_in, z_out, z_in, both, kept,
     zs, zr, ys, yr, cs, cr, rcs, rcr, rys, ryr, rzs, rzr, local) = refs
    tensor = lax.axis_index("tensor")
    ctx = lax.axis_index("ctx")
    plane, core = ctx // 2, ctx % 2
    rows = own_ref.shape[0]
    y_peer = {"tensor": 1 - tensor}
    core_peer = {"ctx": plane * 2 + 1 - core}

    barrier = pltpu.get_barrier_semaphore()
    pl.semaphore_signal(barrier, inc=1, device_id=y_peer, device_id_type=MESH)
    pl.semaphore_signal(barrier, inc=1, device_id=core_peer, device_id_type=MESH)
    for step in range(1, planes):
        there = (plane + step) % planes
        pl.semaphore_signal(barrier, inc=1, device_id={"ctx": there * 2 + core}, device_id_type=MESH)
    pl.semaphore_wait(barrier, planes + 1)

    def block(at, which_core, which_tensor):
        start = pl.multiple_of(((at * 2 + which_core) * 2 + which_tensor) * rows, rows)
        return land.at[pl.ds(start, rows)]

    def along(at, target, direction):
        ref = block(at, core, tensor)
        return remote(ref, ref, zs.at[at, direction], zr.at[at], {"ctx": target * 2 + core})

    def across(at, which_tensor):
        ref = block(at, core, which_tensor)
        return remote(ref, ref, ys.at[at], yr.at[at], y_peer)

    def beside(at, which_core, which_tensor, slot):
        ref = block(at, which_core, which_tensor)
        return remote(ref, ref, cs.at[at, slot], cr.at[at, slot], core_peer)

    start = pl.multiple_of(((plane * 2 + core) * 2 + tensor) * rows, rows)
    land[pl.ds(start, rows)] = own_ref[...]

    @pl.when(plane < planes - 1)
    def _():
        along(plane, plane + 1, 0).start()

    @pl.when(plane > 0)
    def _():
        along(plane, plane - 1, 1).start()

    across(plane, tensor).start()
    beside(plane, core, tensor, 0).start()

    def reduce_core(at):
        return remote(core_out.at[at], core_in.at[at], rcs.at[at], rcr.at[at], core_peer)

    def reduce_y(at):
        return remote(y_out.at[at], y_in.at[at], rys.at[at], ryr.at[at], y_peer)

    def reduce_z(at):
        return remote(z_out.at[at], z_in.at[plane], rzs.at[at], rzr.at[plane], {"ctx": at * 2 + core})

    def reduced_z(at):
        return remote(z_out.at[at], z_in.at[at], rzs.at[at], rzr.at[at], {"ctx": at * 2 + core})

    def save(at):
        span = pl.ds(pl.multiple_of(at * 4 * rows, 4 * rows), 4 * rows)
        return pltpu.make_async_copy(land.at[span], all_ref.at[span], local.at[at])

    def side_plane(distance, side):
        return plane + distance * (2 * side - 1)

    def inside(at):
        return jnp.logical_and(at >= 0, at < planes)

    def pass_on(distance, side):
        at = side_plane(distance, side)
        target = plane + 1 - 2 * side

        @pl.when(inside(at))
        def _():
            along(at, plane, 0).wait_recv()

            @pl.when(inside(target))
            def _():
                along(at, target, side).start()

            across(at, tensor).start()
            beside(at, core, tensor, 0).start()

    def pass_beside(distance, side):
        at = side_plane(distance, side)

        @pl.when(inside(at))
        def _():
            across(at, 1 - tensor).wait_recv()
            beside(at, core, 1 - tensor, 1).start()

    def step(index, carry):
        distance = (index + 1) // 2
        at = side_plane(distance, 1 - index % 2)

        @pl.when(jnp.logical_or(index == 0, index % 2 == 1))
        def _():
            pass_on(distance + 1, 0)
            pass_on(distance + 1, 1)

            @pl.when(distance > 0)
            def _():
                pass_beside(distance, 0)

            pass_beside(distance, 1)

        @pl.when(inside(at))
        def _():
            beside(at, 1 - core, tensor, 0).wait_recv()
            beside(at, 1 - core, 1 - tensor, 1).wait_recv()
            if piece is None:
                save(at).start()
            theirs = pl.multiple_of((at * 2 + 1 - core) * 2 * rows, 2 * rows)
            core_out[at] = chunk(land, theirs, 2 * rows, in_refs, out_refs, work_refs).astype(BF16)
            reduce_core(at).start()
            mine = pl.multiple_of((at * 2 + core) * 2 * rows, 2 * rows)
            both[...] = chunk(land, mine, 2 * rows, in_refs, out_refs, work_refs)
            reduce_core(at).wait_recv()
            both[...] += core_in[at].astype(F32)
            other = pl.multiple_of((1 - tensor) * rows, rows)
            own = pl.multiple_of(tensor * rows, rows)
            y_out[at] = both[pl.ds(other, rows)].astype(BF16)

            @pl.when(index > 0)
            def _():
                reduce_y(at).start()

            kept[at] = both[pl.ds(own, rows)]

        return carry

    load.wait()
    lax.fori_loop(0, 2 * planes - 1, step, 0)

    reduce_y(plane).start()

    def collect(index, count):
        at = side_plane((index + 2) // 2, index % 2)

        @pl.when(inside(at))
        def _():
            if piece is not None:
                piece(land, count, planes, in_refs, out_refs, work_refs)
            reduce_y(at).wait_recv()
            z_out[at] = (kept[at] + y_in[at].astype(F32)).astype(BF16)
            reduce_z(at).start()

        return count + inside(at).astype(jnp.int32)

    count = lax.fori_loop(0, 2 * planes - 2, collect, 0)
    if piece is not None:
        piece(land, count, planes, in_refs, out_refs, work_refs)
    reduce_y(plane).wait_recv()
    sum_ref[...] = kept[plane] + y_in[plane].astype(F32)

    def finish(index, carry):
        at = (plane + 1 + index) % planes
        reduced_z(at).wait_recv()
        sum_ref[...] += z_in[at].astype(F32)
        return carry

    lax.fori_loop(0, planes - 1, finish, 0)

    @pl.when(plane < planes - 1)
    def _():
        along(plane, plane + 1, 0).wait_send()

    @pl.when(plane > 0)
    def _():
        along(plane, plane - 1, 1).wait_send()

    def drain(index, carry):
        distance = (index + 1) // 2
        side = 1 - index % 2
        at = side_plane(distance, side)
        target = plane + 1 - 2 * side

        @pl.when(inside(at))
        def _():
            @pl.when(jnp.logical_and(index > 0, inside(target)))
            def _():
                along(at, target, side).wait_send()

            across(at, tensor).wait_send()
            beside(at, core, tensor, 0).wait_send()
            beside(at, core, 1 - tensor, 1).wait_send()
            if piece is None:
                save(at).wait()
            reduce_core(at).wait_send()
            reduce_y(at).wait_send()

            @pl.when(index > 0)
            def _():
                reduce_z(at).wait_send()

        return carry

    lax.fori_loop(0, 2 * planes - 1, drain, 0)


def spread(chunk, piece, own, inputs, layer, outputs, work, planes, ident, name):
    rows, width = own.shape
    count = planes * 4 * rows
    dma = pltpu.SemaphoreType.DMA
    shape = jax.ShapeDtypeStruct
    saved = (count, width) if piece is None else (16, width)
    outs = [shape(saved, BF16), shape((rows, width), F32)] + list(outputs)
    return pl.pallas_call(
        functools.partial(
            spread_kernel, chunk, piece, layer, planes, len(inputs), len(outputs), len(work)
        ),
        out_shape=outs,
        in_specs=[VMEM, HBM] + [VMEM] * (len(inputs) - 1),
        out_specs=[HBM, VMEM] + [VMEM] * len(outputs),
        scratch_shapes=list(work)
        + [
            pltpu.VMEM(inputs[0].shape[1:], BF16),
            pltpu.SemaphoreType.DMA,
            pltpu.VMEM((count, width), BF16),
            pltpu.VMEM((planes, 2 * rows, width), BF16),
            pltpu.VMEM((planes, 2 * rows, width), BF16),
            pltpu.VMEM((planes, rows, width), BF16),
            pltpu.VMEM((planes, rows, width), BF16),
            pltpu.VMEM((planes, rows, width), BF16),
            pltpu.VMEM((planes, rows, width), BF16),
            pltpu.VMEM((2 * rows, width), F32),
            pltpu.VMEM((planes, rows, width), F32),
            dma((planes, 2)), dma((planes,)), dma((planes,)), dma((planes,)), dma((planes, 2)), dma((planes, 2)),
            dma((planes,)), dma((planes,)), dma((planes,)), dma((planes,)), dma((planes,)), dma((planes,)), dma((planes,)),
        ],
        compiler_params=pltpu.CompilerParams(collective_id=ident + 10 * layer, has_side_effects=True, vmem_limit_bytes=62 << 20),
        cost_estimate=pl.CostEstimate(
            flops=count * width, bytes_accessed=count, transcendentals=0
        ),
        name=name,
    )(own, *inputs)


def mlp_chunk(land, start, rows, in_refs, out_refs, work_refs):
    expand_w, down_w = in_refs
    gate_slope, up_slope, hidden_ref = out_refs
    span = pl.ds(start, rows)
    x = land[span]
    gate = dot(x, expand_w[0])
    up = dot(x, expand_w[1])
    sig = jax.nn.sigmoid(gate)
    silu = gate * sig
    hidden = (silu * up).astype(BF16)
    gate_slope[span] = (up * sig * (1.0 + gate * (1.0 - sig))).astype(BF16)
    up_slope[span] = silu.astype(BF16)
    hidden_ref[span] = hidden
    return dot(hidden, down_w[...])


def mlp_back_chunk(land, start, rows, in_refs, out_refs, work_refs):
    expand_w, down_w, gate_slope, up_slope = in_refs[:4]
    gate_ref, up_ref = work_refs
    span = pl.ds(start, rows)
    grad_hidden = dot(land[span], down_w[...], LAST)
    grad_gate = (grad_hidden * gate_slope[span].astype(F32)).astype(BF16)
    grad_up = (grad_hidden * up_slope[span].astype(F32)).astype(BF16)
    gate_ref[span] = grad_gate
    up_ref[span] = grad_up
    return dot(grad_gate, expand_w[0], LAST) + dot(grad_up, expand_w[1], LAST)


def mlp_back_piece(land, index, pieces, in_refs, out_refs, work_refs):
    normed, hidden = in_refs[4:]
    gate_ref, up_ref = work_refs
    d_expand, d_down = out_refs
    size = d_expand.shape[1] // pieces
    span = pl.ds(pl.multiple_of(index * size, size), size)
    rows = normed[:, span]
    d_expand[0, span] = dot(rows, gate_ref[...], ROWS).astype(BF16)
    d_expand[1, span] = dot(rows, up_ref[...], ROWS).astype(BF16)
    d_down[:, span] = dot(hidden[...], land[:, span], ROWS).astype(BF16)


def mlp_forward(own, expand, layer, down_w, planes):
    count = planes * 4 * own.shape[0]
    shape = jax.ShapeDtypeStruct((count, down_w.shape[0]), BF16)
    return spread(
        mlp_chunk,
        None,
        own,
        (expand, down_w),
        layer,
        (shape,) * 3,
        (),
        planes,
        1,
        "mlp_forward",
    )


def mlp_backward(own, expand, layer, down_w, gate_slope, up_slope, normed, hidden, planes):
    d_expand = jax.ShapeDtypeStruct(expand.shape[1:], BF16)
    reduce = jax.ShapeDtypeStruct(down_w.shape, BF16)
    work = pltpu.VMEM(gate_slope.shape, BF16)
    return spread(
        mlp_back_chunk,
        mlp_back_piece,
        own,
        (expand, down_w, gate_slope, up_slope, normed, hidden),
        layer,
        (d_expand, reduce),
        (work, work),
        planes,
        2,
        "mlp_backward",
    )[1:]


def feed_forward(own, expand_layer, down_w):
    planes = lax.axis_size("ctx") // 2
    if planes == 4:
        return mlp_forward(own, *expand_layer, down_w, planes)
    expand = expand_layer[0][expand_layer[1]]
    rows = gather_tokens(own)
    gate, up = dot(rows, expand[0]), dot(rows, expand[1])
    sig = jax.nn.sigmoid(gate)
    silu = gate * sig
    hidden = (silu * up).astype(BF16)
    gate_slope = (up * sig * (1.0 + gate * (1.0 - sig))).astype(BF16)
    total = scatter_tokens(dot(hidden, down_w).astype(BF16))
    return rows, total, gate_slope, silu.astype(BF16), hidden


def feed_backward(own, expand_layer, down_w, gate_slope, up_slope, normed, hidden):
    planes = lax.axis_size("ctx") // 2
    if planes == 4:
        return mlp_backward(
            own, *expand_layer, down_w, gate_slope, up_slope, normed, hidden, planes
        )
    expand = expand_layer[0][expand_layer[1]]
    rows = gather_tokens(own)
    grad_hidden = dot(rows, down_w, LAST)
    grad_gate = (grad_hidden * gate_slope.astype(F32)).astype(BF16)
    grad_up = (grad_hidden * up_slope.astype(F32)).astype(BF16)
    part = dot(grad_gate, expand[0], LAST) + dot(grad_up, expand[1], LAST)
    return (
        scatter_tokens(part.astype(BF16)),
        jnp.stack([dot(normed, grad_gate, ROWS), dot(normed, grad_up, ROWS)]).astype(BF16),
        dot(hidden, rows, ROWS).astype(BF16),
    )


def greet_line(planes, plane, core):
    barrier = pltpu.get_barrier_semaphore()
    pl.semaphore_signal(
        barrier, inc=1, device_id={"ctx": plane * 2 + 1 - core}, device_id_type=MESH
    )
    for step in range(1, planes):
        there = (plane + step) % planes
        pl.semaphore_signal(
            barrier, inc=1, device_id={"ctx": there * 2 + core}, device_id_type=MESH
        )
    pl.semaphore_wait(barrier, planes)


def attend_kernel(
    planes, heads, q_ref, kv_ref, qpos_ref, kpos_ref, out_ref, low_ref, log_ref, all_ref,
    zs, zr, cs, cr,
):
    ctx = lax.axis_index("ctx")
    plane, core = ctx // 2, ctx % 2
    batch, tokens, pair = kv_ref.shape
    head_dim = pair // 2
    factor = 1.0 / math.sqrt(head_dim)
    greet_line(planes, plane, core)
    core_peer = {"ctx": plane * 2 + 1 - core}

    def block(at):
        return all_ref.at[:, pl.ds(pl.multiple_of(at * tokens, tokens), tokens)]

    def along(there, source):
        ref = block(source * 2 + core)
        return remote(ref, ref, zs.at[there], zr.at[source], {"ctx": there * 2 + core})

    def beside(source, which):
        ref = block(source * 2 + which)
        return remote(ref, ref, cs.at[source], cr.at[source], core_peer)

    all_ref[:, pl.ds(pl.multiple_of(ctx * tokens, tokens), tokens)] = kv_ref[...]
    for step in range(1, planes):
        along((plane + step) % planes, plane).start()
    beside(plane, core).start()
    for step in range(1, planes):
        source = (plane + step) % planes
        along(source, source).wait_recv()
        beside(source, core).start()
    for step in range(planes):
        beside((plane + step) % planes, 1 - core).wait_recv()

    def one(index, carry):
        rows = pl.ds(pl.multiple_of(index * tokens, tokens), tokens)
        keys = all_ref[index, :, :head_dim]
        values = all_ref[index, :, head_dim:]
        allowed = qpos_ref[index] >= kpos_ref[index]
        lane = lax.broadcasted_iota(jnp.int32, (tokens, head_dim), 1)
        logs = jnp.zeros((tokens, head_dim), F32)
        for head in range(heads):
            span = slice(head * head_dim, (head + 1) * head_dim)
            scores = dot(q_ref[rows, span], keys, LAST)
            scores = jnp.where(allowed, scores * factor, -1e30)
            top = jnp.max(scores, axis=1, keepdims=True)
            weights = jnp.exp(scores - top)
            total = jnp.sum(weights, axis=1, keepdims=True)
            logs = jnp.where(lane == head, top + jnp.log(total), logs)
            out = dot((weights * (1.0 / total)).astype(BF16), values)
            out_ref[rows, span] = out
            low_ref[rows, span] = out.astype(BF16)
        log_ref[rows] = logs
        return carry

    lax.fori_loop(0, batch, one, 0)
    for step in range(1, planes):
        along((plane + step) % planes, plane).wait_send()
        beside((plane + step) % planes, core).wait_send()
    beside(plane, core).wait_send()


def attend_back_kernel(
    planes, heads, q_ref, kv_ref, qpos_ref, kpos_ref, grad_ref, out_ref, log_ref, dq_ref, dkv_ref,
    whole, core_out, core_in, z_out, z_in, cs, cr, zs, zr,
):
    ctx = lax.axis_index("ctx")
    plane, core = ctx // 2, ctx % 2
    batch = qpos_ref.shape[0]
    tokens = q_ref.shape[0] // batch
    head_dim = kv_ref.shape[2] // 2
    factor = 1.0 / math.sqrt(head_dim)
    greet_line(planes, plane, core)
    core_peer = {"ctx": plane * 2 + 1 - core}

    def to_core(index):
        return remote(core_out.at[index], core_in.at[index], cs.at[index], cr.at[index], core_peer)

    def to_plane(index, there, source):
        return remote(
            z_out.at[index, there],
            z_in.at[index, source],
            zs.at[index, there],
            zr.at[index, source],
            {"ctx": there * 2 + core},
        )

    def one(index, carry):
        rows = pl.ds(pl.multiple_of(index * tokens, tokens), tokens)
        keys = kv_ref[index, :, :head_dim]
        values = kv_ref[index, :, head_dim:]
        allowed = qpos_ref[index] >= kpos_ref[index]
        logs = log_ref[rows]
        for head in range(heads):
            span = slice(head * head_dim, (head + 1) * head_dim)
            queries = q_ref[rows, span]
            grads = grad_ref[rows, span]
            delta = jnp.sum(grads.astype(F32) * out_ref[rows, span], axis=1, keepdims=True)
            scores = jnp.where(allowed, dot(queries, keys, LAST) * factor, -1e30)
            weights = jnp.exp(scores - logs[:, head : head + 1])
            grad_scores = (weights * (dot(grads, values, LAST) - delta) * factor).astype(BF16)
            dq_ref[rows, span] = dot(grad_scores, keys)
            grad_keys = dot(grad_scores, queries, ROWS)
            grad_values = dot(weights.astype(BF16), grads, ROWS)
            if head == 0:
                whole[index, :, :head_dim] = grad_keys
                whole[index, :, head_dim:] = grad_values
            else:
                whole[index, :, :head_dim] += grad_keys
                whole[index, :, head_dim:] += grad_values

        for at in range(planes):
            theirs = pl.multiple_of((at * 2 + 1 - core) * tokens, tokens)
            core_out[index, at] = whole[index, pl.ds(theirs, tokens)].astype(BF16)
        to_core(index).start()
        return carry

    lax.fori_loop(0, batch, one, 0)

    def mine(index, at):
        start = pl.multiple_of((at * 2 + core) * tokens, tokens)
        return whole[index, pl.ds(start, tokens)] + core_in[index, at].astype(F32)

    for index in range(batch):
        to_core(index).wait_recv()
        for step in range(1, planes):
            there = (plane + step) % planes
            z_out[index, there] = mine(index, there).astype(BF16)
            to_plane(index, there, plane).start()
        dkv_ref[index] = mine(index, plane)
    for index in range(batch):
        for step in range(1, planes):
            source = (plane + step) % planes
            to_plane(index, source, source).wait_recv()
            dkv_ref[index] += z_in[index, source].astype(F32)
    for index in range(batch):
        to_core(index).wait_send()
        for step in range(1, planes):
            to_plane(index, (plane + step) % planes, plane).wait_send()


def attend(queries, kv, query_pos, key_pos):
    batch, tokens, pair = kv.shape
    head_dim = pair // 2
    heads = queries.shape[1] // head_dim
    planes = lax.axis_size("ctx") // 2
    keys = key_pos.shape[1]
    if planes != 4:
        kv_all = gather_ctx(kv, 1)
        split = queries.reshape(batch, tokens, heads, head_dim)
        scores = jnp.einsum(
            "bqhd,bkd->bqhk", split, kv_all[..., :head_dim], preferred_element_type=F32
        )
        allowed = query_pos[:, :, None, None] >= key_pos[:, None, None, :]
        scores = jnp.where(allowed, scores / math.sqrt(head_dim), -1e30)
        logs = jax.nn.logsumexp(scores, axis=-1)
        probs = jnp.exp(scores - logs[..., None]).astype(BF16)
        out = jnp.einsum(
            "bqhk,bkd->bqhd", probs, kv_all[..., head_dim:], preferred_element_type=F32
        ).reshape(queries.shape)
        return out, out.astype(BF16), logs, kv_all
    shape = jax.ShapeDtypeStruct
    dma = pltpu.SemaphoreType.DMA
    rows = batch * tokens
    return pl.pallas_call(
        functools.partial(attend_kernel, planes, heads),
        out_shape=[
            shape(queries.shape, F32),
            shape(queries.shape, BF16),
            shape((rows, head_dim), F32),
            shape((batch, keys, pair), BF16),
        ],
        in_specs=[VMEM] * 4,
        out_specs=[VMEM] * 4,
        scratch_shapes=[dma((planes,)), dma((planes,)), dma((planes,)), dma((planes,))],
        compiler_params=pltpu.CompilerParams(
            collective_id=3, has_side_effects=True, vmem_limit_bytes=48 << 20
        ),
        cost_estimate=pl.CostEstimate(
            flops=rows * keys, bytes_accessed=rows, transcendentals=0
        ),
        name="attend",
    )(queries, kv, query_pos[:, :, None], key_pos[:, None, :])


def attend_backward(queries, kv_all, query_pos, key_pos, grads, out, logs):
    batch, keys, pair = kv_all.shape
    head_dim = pair // 2
    heads = queries.shape[1] // head_dim
    rows = queries.shape[0]
    tokens = rows // batch
    planes = lax.axis_size("ctx") // 2
    if planes != 4:
        factor = 1.0 / math.sqrt(head_dim)
        k_all, v_all = kv_all[..., :head_dim], kv_all[..., head_dim:]
        split = queries.reshape(batch, tokens, heads, head_dim)
        grad_split = grads.reshape(split.shape)
        delta = jnp.sum(grad_split.astype(F32) * out.reshape(split.shape), axis=-1)
        scores = jnp.einsum("bqhd,bkd->bqhk", split, k_all, preferred_element_type=F32)
        allowed = query_pos[:, :, None, None] >= key_pos[:, None, None, :]
        scores = jnp.where(allowed, scores * factor, -1e30)
        probs = jnp.exp(scores - logs[..., None])
        grad_probs = jnp.einsum("bqhd,bkd->bqhk", grad_split, v_all, preferred_element_type=F32)
        grad_scores = (probs * (grad_probs - delta[..., None]) * factor).astype(BF16)
        dq = jnp.einsum("bqhk,bkd->bqhd", grad_scores, k_all, preferred_element_type=F32)
        dk = jnp.einsum("bqhk,bqhd->bkd", grad_scores, split, preferred_element_type=F32)
        dv = jnp.einsum(
            "bqhk,bqhd->bkd", probs.astype(BF16), grad_split, preferred_element_type=F32
        )
        dkv = lax.psum_scatter(
            jnp.concatenate([dk, dv], axis=-1).astype(BF16), "ctx", scatter_dimension=1, tiled=True
        )
        return dq.reshape(queries.shape), dkv.astype(F32)
    shape = jax.ShapeDtypeStruct
    dma = pltpu.SemaphoreType.DMA
    return pl.pallas_call(
        functools.partial(attend_back_kernel, planes, heads),
        out_shape=[shape(queries.shape, F32), shape((batch, tokens, pair), F32)],
        in_specs=[VMEM] * 7,
        out_specs=[VMEM] * 2,
        scratch_shapes=[
            pltpu.VMEM((batch, keys, pair), F32),
            pltpu.VMEM((batch, planes, tokens, pair), BF16),
            pltpu.VMEM((batch, planes, tokens, pair), BF16),
            pltpu.VMEM((batch, planes, tokens, pair), BF16),
            pltpu.VMEM((batch, planes, tokens, pair), BF16),
            dma((batch,)), dma((batch,)), dma((batch, planes)), dma((batch, planes)),
        ],
        compiler_params=pltpu.CompilerParams(
            collective_id=4, has_side_effects=True, vmem_limit_bytes=48 << 20
        ),
        cost_estimate=pl.CostEstimate(
            flops=rows * keys, bytes_accessed=rows, transcendentals=0
        ),
        name="attend_backward",
    )(queries, kv_all, query_pos[:, :, None], key_pos[:, None, :], grads, out, logs)


def layer_forward(x_low, weights, tables):
    gain_attn, w_mixed, bias, w_project, gain_mlp, w_expand, w_reduce = weights
    cosine, sine, query_pos, key_pos, mine = tables
    count, width = x_low.shape
    query_width = w_project.shape[0]
    head_dim = (w_mixed.shape[1] - query_width) // 2
    heads = query_width // head_dim
    batch = query_pos.shape[0]
    tokens = count // batch
    x = x_low.astype(F32)
    root_attn = inverse_root(x)
    normed = (x * root_attn * gain_attn).astype(BF16)
    mixed = dot(normed, w_mixed) + bias
    queries = rotate(
        mixed[:, :query_width].reshape(count, heads, head_dim),
        cosine[:, None, :],
        sine[:, None, :],
    ).astype(BF16).reshape(count, query_width)
    keys = rotate(mixed[:, query_width : query_width + head_dim], cosine, sine)
    kv = jnp.concatenate([keys, mixed[:, query_width + head_dim :]], axis=1).astype(BF16)
    attended_full, attended, log_total, kv = attend(
        queries, kv.reshape(batch, tokens, 2 * head_dim), query_pos, key_pos
    )
    x_mine = lax.dynamic_slice_in_dim(x, mine * tokens, tokens, 0)
    middle = x_mine + tensor_scatter(dot(attended, w_project))
    root_mlp = inverse_root(middle)
    normed_mlp = (middle * root_mlp * gain_mlp).astype(BF16)
    all_normed, branch, gate_slope, up_slope, hidden = feed_forward(
        normed_mlp, w_expand, w_reduce
    )
    result = middle + branch
    kept = (
        x_mine,
        lax.dynamic_slice_in_dim(root_attn, mine * tokens, tokens, 0),
        normed,
        queries,
        kv,
        attended_full,
        log_total,
        attended,
        middle,
        root_mlp,
        all_normed,
        gate_slope,
        up_slope,
        hidden,
    )
    return result.astype(BF16), kept


def layer_backward(grad_out, kept, weights, tables, route, earlier):
    gain_attn, w_mixed, bias, w_project, gain_mlp, w_expand, w_reduce = weights
    cosine, sine, query_pos, key_pos, mine = tables
    (
        x_mine,
        root_attn,
        normed,
        queries,
        kv,
        attended_full,
        log_total,
        attended,
        middle,
        root_mlp,
        all_normed,
        gate_slope,
        up_slope,
        hidden,
    ) = kept
    count, query_width = queries.shape
    head_dim = (w_mixed.shape[1] - query_width) // 2
    heads = query_width // head_dim
    grad_normed_mlp, d_expand, d_reduce = feed_backward(
        grad_out.astype(BF16),
        w_expand,
        w_reduce,
        gate_slope,
        up_slope,
        all_normed,
        hidden,
    )
    moved_reduce = lax.ppermute(d_reduce, "section", route)
    grad_middle, d_gain_mlp = norm_backward(middle, root_mlp, gain_mlp, grad_normed_mlp)
    grad_middle = grad_middle + grad_out
    grad_low, earlier = lax.optimization_barrier((grad_middle.astype(BF16), earlier))
    grad_branch = tensor_gather(grad_low)
    d_project = dot(attended, grad_branch, ROWS)
    grad_attended = dot(grad_branch, w_project, LAST).astype(BF16)
    grad_q, grad_kv = attend_backward(
        queries, kv, query_pos, key_pos, grad_attended, attended_full, log_total
    )
    grad_q, grad_kv, moved_reduce = lax.optimization_barrier((grad_q, grad_kv, moved_reduce))
    grad_kv = grad_kv.reshape(count, 2 * head_dim)
    grad_q = unrotate(
        grad_q.reshape(count, heads, head_dim), cosine[:, None, :], sine[:, None, :]
    )
    grad_k = unrotate(grad_kv[:, :head_dim], cosine, sine)
    grad_mixed = jnp.concatenate(
        [grad_q.reshape(count, heads * head_dim), grad_k, grad_kv[:, head_dim:]], axis=1
    ).astype(BF16)
    d_mixed = dot(normed, grad_mixed, ROWS)
    d_bias = jnp.sum(grad_mixed.astype(F32), axis=0)
    grad_normed = tensor_scatter(dot(grad_mixed, w_mixed, LAST))
    grad_x, d_gain_attn = norm_backward(x_mine, root_attn, gain_attn, grad_normed)
    grad_x = (grad_x + grad_middle).astype(BF16)
    vectors = (d_gain_attn, d_mixed, d_bias, d_project, d_gain_mlp)
    return grad_x, vectors, d_expand, (d_reduce, moved_reduce), earlier


def shards(
    block_input, positions, cotangent, norm_attn, w_qkv, b_qkv, w_out, norm_mlp, w_gate_up, w_down
):
    section = lax.axis_index("section")
    tensor = lax.axis_index("tensor")
    ctx = lax.axis_index("ctx")
    ctx_size = lax.axis_size("ctx")
    first = section == 0
    micro, tokens, width = block_input.shape
    half = micro // 2
    head_dim = w_qkv.shape[3] - w_out.shape[2] * ctx_size
    head_dim = head_dim // 2
    slice_width = norm_attn.shape[1]
    slice_bias = b_qkv.shape[2]
    units = w_down.shape[1]

    def plane_part(value):
        return lax.dynamic_slice_in_dim(value, section * half, half, 0)

    def layers(own, other):
        return jnp.where(first, own, other), jnp.where(first, other, own)

    x = plane_part(block_input).reshape(half * tokens, width)
    pos_local = plane_part(positions)
    cosine, sine = angles(pos_local.reshape(-1), head_dim)

    small = jnp.concatenate([norm_attn[0], norm_mlp[0], b_qkv[0, 0]])
    qkv, out = w_qkv[0, :, 0, :], w_out[0, 0]
    vectors = jnp.concatenate(layers(small, swap(small)))
    places = jnp.concatenate([pos_local // 64, pos_local % 64]).reshape(-1).astype(BF16)
    packed = gather_ctx(jnp.concatenate([vectors, places])[None], 0)
    places = packed[:, vectors.shape[0] :].astype(jnp.int32).reshape(ctx_size, 2, half, tokens)
    pos_all = jnp.swapaxes(places[:, 0] * 64 + places[:, 1], 0, 1).reshape(half, -1)
    tables = (cosine, sine, pos_local, pos_all, tensor)
    small_size = 2 * slice_width + slice_bias
    small0, small1 = packed[:, :small_size], packed[:, small_size : 2 * small_size]
    qkv0, qkv1 = layers(qkv, swap(qkv))
    out0, out1 = layers(out, swap(out))
    down0, down1 = layers(w_down[0], swap(w_down[0]))
    expand = w_gate_up[0].reshape(slice_width, 2, ctx_size, units)
    expand = share(jnp.transpose(expand, (1, 2, 0, 3))).reshape(2, 2, width, units)
    x, expand = lax.optimization_barrier((x, expand))
    expand0, expand1 = (expand, 0), (expand, 1)

    def whole(small, qkv, out, expand, down):
        return (
            small[:, :slice_width].reshape(1, width),
            gather_ctx(qkv, 0),
            small[:, 2 * slice_width :].reshape(1, slice_bias * ctx_size),
            gather_ctx(out, 0),
            small[:, slice_width : 2 * slice_width].reshape(1, width),
            expand,
            down,
        )

    weights0 = whole(small0, qkv0, out0, expand0, down0)
    weights1 = whole(small1, qkv1, out1, expand1, down1)

    result0, kept0 = layer_forward(x, weights0, tables)
    x1 = tensor_gather(result0)
    result1, kept1 = layer_forward(x1, weights1, tables)
    out1_all = tensor_gather(result1)

    def exchange(layer0, layer1):
        kept_here = jnp.where(first, layer0, layer1)
        received = swap(jnp.where(first, layer1, layer0))
        low = jnp.where(first, kept_here, received)
        high = jnp.where(first, received, kept_here)
        both = jnp.concatenate([low, high], axis=0)
        return both.reshape(1, micro, tokens, width)

    section_output = exchange(x1, out1_all)

    seed = lax.dynamic_slice_in_dim(cotangent, section * half + tensor, 1, 0)[0].astype(F32)
    def ctx_scatter(value):
        return lax.psum_scatter(
            value.astype(BF16), "ctx", scatter_dimension=0, tiled=True
        )

    group = w_qkv.shape[3]
    split_at = group - head_dim

    def with_vectors(grads):
        gain_attn, mixed, bias, project, gain_mlp = grads[:5]
        rows = jnp.concatenate(
            [
                bias[:split_at].reshape(ctx_size, -1),
                bias[split_at:].reshape(ctx_size, -1),
                gain_attn.reshape(ctx_size, slice_width),
                gain_mlp.reshape(ctx_size, slice_width),
            ],
            axis=1,
        )
        rows = jnp.pad(rows[:, None, :], ((0, 0), (0, 15), (0, group - rows.shape[1])))
        mixed = mixed.reshape(ctx_size, slice_width, group)
        both = jnp.concatenate([mixed.astype(BF16), rows.astype(BF16)], axis=1)
        return both.reshape(ctx_size * (slice_width + 16), group)

    grad1, d1, d_expand1, d_reduce1, _ = layer_backward(
        seed, kept1, weights1, tables, [(0, 1)], ()
    )
    slices1 = (ctx_scatter(with_vectors(d1)), ctx_scatter(d1[3]))
    grad1_all = tensor_gather(grad1)
    grad1, grad1_all = lax.optimization_barrier((grad1, grad1_all))
    grad0, d0, d_expand0, d_reduce0, earlier = layer_backward(
        grad1.astype(F32), kept0, weights0, tables, [(1, 0)], slices1 + (section_output,)
    )
    slices1, section_output = earlier[:2], earlier[2]

    def to_owner(part0, part1):
        received0 = lax.ppermute(part0.astype(BF16), "section", [(1, 0)])
        received1 = lax.ppermute(part1.astype(BF16), "section", [(0, 1)])
        own = jnp.where(first, part0, part1).astype(F32)
        return own + jnp.where(first, received0, received1).astype(F32)

    def of_owner(pair0, pair1):
        own, received = (jnp.where(first, low, high).astype(F32) for low, high in zip(pair0, pair1))
        return own + received

    blocks = (2, ctx_size, slice_width, units)
    grad0_all = tensor_gather(grad0)
    grad0_all, d_expand0 = lax.optimization_barrier((grad0_all, d_expand0))
    input_grad = exchange(grad0_all, grad1_all)
    total = collect(d_expand0.reshape(blocks), d_expand1.reshape(blocks), first)
    d_expand = jnp.transpose(total, (2, 0, 1, 3)).reshape(1, slice_width, 2, ctx_size * units)
    d_expand = d_expand.astype(F32)
    d_reduce = of_owner(d_reduce0, d_reduce1)

    d_mixed = to_owner(ctx_scatter(with_vectors(d0)), slices1[0])
    d_project = to_owner(ctx_scatter(d0[3]), slices1[1])
    vectors = d_mixed[slice_width]
    d_mixed = d_mixed[:slice_width]
    count_qk, count_v = split_at // ctx_size, head_dim // ctx_size
    bias_qk = vectors[:count_qk][None]
    bias_v = vectors[count_qk : count_qk + count_v][None]
    start = count_qk + count_v
    gains = vectors[start : start + 2 * slice_width].reshape(1, 2 * slice_width)
    gains = gains + lax.ppermute(gains, "tensor", SWAP)
    return (
        section_output,
        input_grad,
        gains[:, :slice_width],
        d_mixed[None, :, None, :],
        bias_qk[None],
        bias_v[None],
        d_project[None, None],
        gains[:, slice_width:],
        d_expand,
        d_reduce[None],
    )


def solution(mesh):
    in_specs = (
        P(None, "ctx", None),
        P(None, "ctx"),
        P(None, "ctx", None),
        P("section", "ctx"),
        P("section", "ctx", "tensor", None),
        P("section", "tensor", "ctx"),
        P("section", "tensor", "ctx", None),
        P("section", "ctx"),
        P("section", "ctx", None, "tensor"),
        P("section", ("tensor", "ctx"), None),
    )
    out_specs = (
        P("section", None, "ctx", None),
        P("section", None, "ctx", None),
        P("section", "ctx"),
        P("section", "ctx", "tensor", None),
        P("section", "tensor", "ctx"),
        P("section", "tensor", "ctx"),
        P("section", "tensor", "ctx", None),
        P("section", "ctx"),
        P("section", "ctx", None, "tensor"),
        P("section", ("tensor", "ctx"), None),
    )
    return jax.shard_map(shards, mesh=mesh, in_specs=in_specs, out_specs=out_specs, check_vma=False)
```

```python
import functools
import functools
import math

import jax
import jax.numpy as jnp
from jax import lax
from jax.experimental import pallas as pl
from jax.experimental.pallas import tpu as pltpu
from jax.sharding import PartitionSpec as P

EPSILON = 1e-06
ROPE_BASE = 1000000.0
ROWS = (((0,), (0,)), ((), ()))
LAST = (((1,), (1,)), ((), ()))
F32 = jnp.float32
BF16 = jnp.bfloat16
SWAP = [(0, 1), (1, 0)]
MESH = pl.DeviceIdType.MESH
VMEM = pl.BlockSpec(memory_space=pltpu.VMEM)
HBM = pl.BlockSpec(memory_space=pl.ANY)


def dot(a, b, dims=(((1,), (0,)), ((), ()))):
    return lax.dot_general(a, b, dims, preferred_element_type=F32)


def angles(positions, head_dim):
    half_dim = head_dim // 2
    frequency = ROPE_BASE ** (-(jnp.arange(half_dim, dtype=F32) * 2.0) / head_dim)
    phases = positions.astype(F32)[:, None] * frequency[None, :]
    phases = jnp.concatenate([phases, phases], axis=-1)
    return jnp.cos(phases), jnp.sin(phases)


def rotate(values, cosine, sine):
    half = values.shape[-1] // 2
    turned = jnp.concatenate([-values[..., half:], values[..., :half]], axis=-1)
    return values * cosine + turned * sine


def unrotate(grads, cosine, sine):
    half = grads.shape[-1] // 2
    twisted = grads * sine
    turned = jnp.concatenate([twisted[..., half:], -twisted[..., :half]], axis=-1)
    return grads * cosine + turned


def inverse_root(values):
    return lax.rsqrt(jnp.mean(values * values, axis=-1, keepdims=True) + EPSILON)


def norm_backward(values, root, gain, grad_normed):
    normal = values * root
    gain_grad = jnp.sum(grad_normed * normal, axis=0)
    scaled = grad_normed * gain
    mean = jnp.mean(scaled * normal, axis=-1, keepdims=True)
    return root * (scaled - normal * mean), gain_grad


def swap(value):
    return lax.ppermute(value, "section", SWAP)


def gather_ctx(value, axis):
    return lax.all_gather(value, "ctx", axis=axis, tiled=True)


def gather_tokens(rows):
    return lax.all_gather(rows, ("ctx", "tensor"), axis=0, tiled=True)


def scatter_tokens(rows):
    return lax.psum_scatter(rows, ("ctx", "tensor"), scatter_dimension=0, tiled=True).astype(F32)


def tensor_gather(rows):
    return lax.all_gather(rows, "tensor", axis=0, tiled=True)


def tensor_pair(rows):
    received = lax.ppermute(rows, "tensor", SWAP)
    mine = lax.axis_index("tensor") == 0
    return jnp.concatenate([jnp.where(mine, rows, received), jnp.where(mine, received, rows)])


def tensor_scatter(rows):
    mine = lax.axis_index("tensor")
    tokens = rows.shape[0] // 2
    own = lax.dynamic_slice_in_dim(rows, mine * tokens, tokens, 0)
    other = lax.dynamic_slice_in_dim(rows, (1 - mine) * tokens, tokens, 0)
    return own + lax.ppermute(other.astype(BF16), "tensor", SWAP).astype(F32)


def greet_all(size, me):
    barrier = pltpu.get_barrier_semaphore()
    for step in range(1, size):
        pl.semaphore_signal(
            barrier, inc=1, device_id={"ctx": (me + step) % size}, device_id_type=MESH
        )
    there = 1 - lax.axis_index("section")
    pl.semaphore_signal(barrier, inc=1, device_id={"section": there}, device_id_type=MESH)
    pl.semaphore_wait(barrier, size)


def by_distance(size):
    return sorted(range(size), key=lambda step: min(step, size - step))


def share_job(size, from_ref, all_ref, send, recv, over_send, over_recv, local):
    me = lax.axis_index("ctx")
    section = lax.axis_index("section")
    order = by_distance(size)[1:]

    def copy(there, source):
        return remote(
            from_ref.at[:, there],
            all_ref.at[section, :, source],
            send.at[there],
            recv.at[source],
            {"ctx": there},
        )

    def over(block, source):
        return remote(
            block,
            all_ref.at[section, :, source],
            over_send.at[source],
            over_recv.at[source],
            {"section": 1 - section},
        )

    def own():
        return pltpu.make_async_copy(from_ref.at[:, me], all_ref.at[section, :, me], local)

    def start():
        own().start()
        over(from_ref.at[:, me], me).start()
        for step in order[:2]:
            copy((me + step) % size, me).start()

    def stage(index):
        step = order[index]
        source = (me + size - step) % size
        copy(source, source).wait_recv()
        over(all_ref.at[section, :, source], source).start()
        copy((me + step) % size, me).wait_send()
        if index + 2 < len(order):
            copy((me + order[index + 2]) % size, me).start()

    def finish():
        own().wait()
        for step in range(size):
            source = (me + step) % size
            over(all_ref.at[section, :, source], source).wait()

    return start, stage, finish


def share(blocks):
    moved = lax.all_to_all(blocks, "ctx", split_axis=1, concat_axis=1, tiled=True)
    return lax.all_gather(moved, "section")


def collect_kernel(
    size, first_ref, second_ref, to_ref, own, other, send, recv, over_send, over_recv, local, store
):
    me = lax.axis_index("ctx")
    section = lax.axis_index("section")
    greet_all(size, me)
    order = by_distance(size)[::-1]

    def over(source_ref, at):
        return remote(
            source_ref.at[:, at], other.at[at], over_send.at[at], over_recv.at[at],
            {"section": 1 - section},
        )

    def load(source_ref, at):
        return pltpu.make_async_copy(source_ref.at[:, at], own.at[at], local.at[at])

    def copy(there, source):
        return remote(
            own.at[there], to_ref.at[:, source], send.at[there], recv.at[source], {"ctx": there}
        )

    def start(at):
        @pl.when(section == 0)
        def _():
            over(second_ref, at).start()
            load(first_ref, at).start()

        @pl.when(section == 1)
        def _():
            over(first_ref, at).start()
            load(second_ref, at).start()

    for index, step in enumerate(order):
        at = (me + step) % size
        if index == 0:
            start(at)
        if index + 1 < size:
            start((me + order[index + 1]) % size)
        over(first_ref, at).wait()
        load(first_ref, at).wait()
        own[at] = (own[at].astype(F32) + other[at].astype(F32)).astype(own.dtype)
        if step > 0:
            copy(at, me).start()
        else:
            mine = pltpu.make_async_copy(own.at[at], to_ref.at[:, me], store)
            mine.start()
            mine.wait()
    for step in order:
        at = (me + step) % size
        if step > 0:
            copy(at, at).wait_recv()
            copy(at, me).wait_send()


def collect(first, second, is_first):
    parts, size, rows, columns = first.shape
    if size != 8:
        received = lax.ppermute(jnp.where(is_first, second, first), "section", SWAP)
        total = jnp.where(is_first, first, second).astype(F32) + received.astype(F32)
        return lax.all_to_all(
            total.astype(BF16), "ctx", split_axis=1, concat_axis=1, tiled=True
        )
    dma = pltpu.SemaphoreType.DMA
    block = pltpu.VMEM((size, parts, rows, columns), first.dtype)
    return pl.pallas_call(
        functools.partial(collect_kernel, size),
        out_shape=jax.ShapeDtypeStruct(first.shape, first.dtype),
        in_specs=[HBM, HBM],
        out_specs=HBM,
        scratch_shapes=[block, block]
        + [dma((size,)), dma((size,)), dma((size,)), dma((size,)), dma((size,)), dma],
        compiler_params=pltpu.CompilerParams(
            collective_id=6, has_side_effects=True, vmem_limit_bytes=24 << 20
        ),
        cost_estimate=pl.CostEstimate(flops=first.size, bytes_accessed=1024, transcendentals=0),
        name="collect",
    )(first, second)


def remote(src, dst, send, recv, device):
    return pltpu.make_async_remote_copy(
        src_ref=src, dst_ref=dst, send_sem=send, recv_sem=recv, device_id=device, device_id_type=MESH
    )


def spread_kernel(chunk, piece, layer, planes, gathered, ins, outs, extra, own_ref, *refs):
    in_refs, refs = refs[:ins], refs[ins:]
    all_ref, sum_ref = refs[:2]
    out_refs, refs = refs[2 : 2 + outs], refs[2 + outs :]
    work_refs, refs = refs[:extra], refs[extra:]
    (expand_w, load_sem), refs = refs[:2], refs[2:]
    load = pltpu.make_async_copy(in_refs[0].at[layer], expand_w, load_sem)
    load.start()
    in_refs = (expand_w,) + in_refs[1:]
    (land, core_out, core_in, y_out, y_in, z_out, z_in, both, kept,
     zs, zr, ys, yr, cs, cr, rcs, rcr, rys, ryr, rzs, rzr, local) = refs
    tensor = lax.axis_index("tensor")
    ctx = lax.axis_index("ctx")
    plane, core = ctx // 2, ctx % 2
    rows = own_ref.shape[0] // (4 * planes if gathered else 1)
    y_peer = {"tensor": 1 - tensor}
    core_peer = {"ctx": plane * 2 + 1 - core}

    barrier = pltpu.get_barrier_semaphore()
    pl.semaphore_signal(barrier, inc=1, device_id=y_peer, device_id_type=MESH)
    pl.semaphore_signal(barrier, inc=1, device_id=core_peer, device_id_type=MESH)
    for step in range(1, planes):
        there = (plane + step) % planes
        pl.semaphore_signal(barrier, inc=1, device_id={"ctx": there * 2 + core}, device_id_type=MESH)
    pl.semaphore_wait(barrier, planes + 1)

    def block(at, which_core, which_tensor):
        start = pl.multiple_of(((at * 2 + which_core) * 2 + which_tensor) * rows, rows)
        return land.at[pl.ds(start, rows)]

    def along(at, target, direction):
        ref = block(at, core, tensor)
        return remote(ref, ref, zs.at[at, direction], zr.at[at], {"ctx": target * 2 + core})

    def across(at, which_tensor):
        ref = block(at, core, which_tensor)
        return remote(ref, ref, ys.at[at], yr.at[at], y_peer)

    def beside(at, which_core, which_tensor, slot):
        ref = block(at, which_core, which_tensor)
        return remote(ref, ref, cs.at[at, slot], cr.at[at, slot], core_peer)

    if not gathered:
        start = pl.multiple_of(((plane * 2 + core) * 2 + tensor) * rows, rows)
        land[pl.ds(start, rows)] = own_ref[...]

        @pl.when(plane < planes - 1)
        def _():
            along(plane, plane + 1, 0).start()

        @pl.when(plane > 0)
        def _():
            along(plane, plane - 1, 1).start()

        across(plane, tensor).start()
        beside(plane, core, tensor, 0).start()

    def reduce_core(at):
        return remote(core_out.at[at], core_in.at[at], rcs.at[at], rcr.at[at], core_peer)

    def reduce_y(at):
        return remote(y_out.at[at], y_in.at[at], rys.at[at], ryr.at[at], y_peer)

    def reduce_z(at):
        return remote(z_out.at[at], z_in.at[plane], rzs.at[at], rzr.at[plane], {"ctx": at * 2 + core})

    def reduced_z(at):
        return remote(z_out.at[at], z_in.at[at], rzs.at[at], rzr.at[at], {"ctx": at * 2 + core})

    def save(at):
        span = pl.ds(pl.multiple_of(at * 4 * rows, 4 * rows), 4 * rows)
        return pltpu.make_async_copy(land.at[span], all_ref.at[span], local.at[at])

    def side_plane(distance, side):
        return plane + distance * (2 * side - 1)

    def inside(at):
        return jnp.logical_and(at >= 0, at < planes)

    def pass_on(distance, side):
        at = side_plane(distance, side)
        target = plane + 1 - 2 * side

        @pl.when(inside(at))
        def _():
            along(at, plane, 0).wait_recv()

            @pl.when(inside(target))
            def _():
                along(at, target, side).start()

            across(at, tensor).start()
            beside(at, core, tensor, 0).start()

    def pass_beside(distance, side):
        at = side_plane(distance, side)

        @pl.when(inside(at))
        def _():
            across(at, 1 - tensor).wait_recv()
            beside(at, core, 1 - tensor, 1).start()

    def fetch(at):
        span = pl.ds(pl.multiple_of(at * 4 * rows, 4 * rows), 4 * rows)
        return pltpu.make_async_copy(own_ref.at[span], land.at[span], local.at[at])

    if gathered:
        for at in range(planes):
            fetch(at).start()

    def step(index, carry):
        if gathered:
            index = 2 * planes - 2 - index
        distance = (index + 1) // 2
        at = side_plane(distance, 1 - index % 2)

        if not gathered:

            @pl.when(jnp.logical_or(index == 0, index % 2 == 1))
            def _():
                pass_on(distance + 1, 0)
                pass_on(distance + 1, 1)

                @pl.when(distance > 0)
                def _():
                    pass_beside(distance, 0)

                pass_beside(distance, 1)

        @pl.when(inside(at))
        def _():
            if gathered:
                fetch(at).wait()
            else:
                beside(at, 1 - core, tensor, 0).wait_recv()
                beside(at, 1 - core, 1 - tensor, 1).wait_recv()
            if piece is None:
                save(at).start()
            theirs = pl.multiple_of((at * 2 + 1 - core) * 2 * rows, 2 * rows)
            core_out[at] = chunk(land, theirs, 2 * rows, in_refs, out_refs, work_refs).astype(BF16)
            reduce_core(at).start()
            mine = pl.multiple_of((at * 2 + core) * 2 * rows, 2 * rows)
            both[...] = chunk(land, mine, 2 * rows, in_refs, out_refs, work_refs)
            reduce_core(at).wait_recv()
            both[...] += core_in[at].astype(F32)
            other = pl.multiple_of((1 - tensor) * rows, rows)
            own = pl.multiple_of(tensor * rows, rows)
            y_out[at] = both[pl.ds(other, rows)].astype(BF16)

            @pl.when(index > 0)
            def _():
                reduce_y(at).start()

            kept[at] = both[pl.ds(own, rows)]

        return carry

    load.wait()
    lax.fori_loop(0, 2 * planes - 1, step, 0)

    reduce_y(plane).start()

    def collect(index, count):
        if gathered:
            index = 2 * planes - 3 - index
        at = side_plane((index + 2) // 2, index % 2)

        @pl.when(inside(at))
        def _():
            if piece is not None:
                piece(land, count, planes, in_refs, out_refs, work_refs)
            reduce_y(at).wait_recv()
            z_out[at] = (kept[at] + y_in[at].astype(F32)).astype(BF16)
            reduce_z(at).start()

        return count + inside(at).astype(jnp.int32)

    count = lax.fori_loop(0, 2 * planes - 2, collect, 0)
    if piece is not None:
        piece(land, count, planes, in_refs, out_refs, work_refs)
    reduce_y(plane).wait_recv()
    sum_ref[...] = kept[plane] + y_in[plane].astype(F32)

    def finish(index, carry):
        at = (plane + 1 + index) % planes
        reduced_z(at).wait_recv()
        sum_ref[...] += z_in[at].astype(F32)
        return carry

    lax.fori_loop(0, planes - 1, finish, 0)

    if not gathered:
        @pl.when(plane < planes - 1)
        def _():
            along(plane, plane + 1, 0).wait_send()

        @pl.when(plane > 0)
        def _():
            along(plane, plane - 1, 1).wait_send()

    def drain(index, carry):
        distance = (index + 1) // 2
        side = 1 - index % 2
        at = side_plane(distance, side)
        target = plane + 1 - 2 * side

        @pl.when(inside(at))
        def _():
            if not gathered:

                @pl.when(jnp.logical_and(index > 0, inside(target)))
                def _():
                    along(at, target, side).wait_send()

                across(at, tensor).wait_send()
                beside(at, core, tensor, 0).wait_send()
                beside(at, core, 1 - tensor, 1).wait_send()
            if piece is None:
                save(at).wait()
            reduce_core(at).wait_send()
            reduce_y(at).wait_send()

            @pl.when(index > 0)
            def _():
                reduce_z(at).wait_send()

        return carry

    lax.fori_loop(0, 2 * planes - 1, drain, 0)


def spread(chunk, piece, own, inputs, layer, outputs, work, planes, ident, name):
    rows, width = own.shape
    gathered = rows == inputs[2].shape[0] if len(inputs) > 2 else False
    if gathered:
        rows //= 4 * planes
    count = planes * 4 * rows
    dma = pltpu.SemaphoreType.DMA
    shape = jax.ShapeDtypeStruct
    saved = (count, width) if piece is None else (16, width)
    outs = [shape(saved, BF16), shape((rows, width), F32)] + list(outputs)
    return pl.pallas_call(
        functools.partial(
            spread_kernel, chunk, piece, layer, planes, gathered, len(inputs), len(outputs), len(work)
        ),
        out_shape=outs,
        in_specs=[HBM if gathered else VMEM, HBM] + [VMEM] * (len(inputs) - 1),
        out_specs=[HBM, VMEM] + [VMEM] * len(outputs),
        scratch_shapes=list(work)
        + [
            pltpu.VMEM(inputs[0].shape[1:], BF16),
            pltpu.SemaphoreType.DMA,
            pltpu.VMEM((count, width), BF16),
            pltpu.VMEM((planes, 2 * rows, width), BF16),
            pltpu.VMEM((planes, 2 * rows, width), BF16),
            pltpu.VMEM((planes, rows, width), BF16),
            pltpu.VMEM((planes, rows, width), BF16),
            pltpu.VMEM((planes, rows, width), BF16),
            pltpu.VMEM((planes, rows, width), BF16),
            pltpu.VMEM((2 * rows, width), F32),
            pltpu.VMEM((planes, rows, width), F32),
            dma((planes, 2)), dma((planes,)), dma((planes,)), dma((planes,)), dma((planes, 2)), dma((planes, 2)),
            dma((planes,)), dma((planes,)), dma((planes,)), dma((planes,)), dma((planes,)), dma((planes,)), dma((planes,)),
        ],
        compiler_params=pltpu.CompilerParams(collective_id=ident + 10 * layer, has_side_effects=True, vmem_limit_bytes=62 << 20),
        cost_estimate=pl.CostEstimate(
            flops=count * width, bytes_accessed=count, transcendentals=0
        ),
        name=name,
    )(own, *inputs)


def mlp_chunk(land, start, rows, in_refs, out_refs, work_refs):
    expand_w, down_w = in_refs
    gate_slope, up_slope, hidden_ref = out_refs
    span = pl.ds(start, rows)
    x = land[span]
    gate = dot(x, expand_w[0])
    up = dot(x, expand_w[1])
    sig = jax.nn.sigmoid(gate)
    silu = gate * sig
    hidden = (silu * up).astype(BF16)
    gate_slope[span] = (up * sig * (1.0 + gate * (1.0 - sig))).astype(BF16)
    up_slope[span] = silu.astype(BF16)
    hidden_ref[span] = hidden
    return dot(hidden, down_w[...])


def mlp_back_chunk(land, start, rows, in_refs, out_refs, work_refs):
    expand_w, down_w, gate_slope, up_slope = in_refs[:4]
    gate_ref, up_ref = work_refs
    span = pl.ds(start, rows)
    grad_hidden = dot(land[span], down_w[...], LAST)
    grad_gate = (grad_hidden * gate_slope[span].astype(F32)).astype(BF16)
    grad_up = (grad_hidden * up_slope[span].astype(F32)).astype(BF16)
    gate_ref[span] = grad_gate
    up_ref[span] = grad_up
    return dot(grad_gate, expand_w[0], LAST) + dot(grad_up, expand_w[1], LAST)


def mlp_back_piece(land, index, pieces, in_refs, out_refs, work_refs):
    normed, hidden = in_refs[4:]
    gate_ref, up_ref = work_refs
    d_expand, d_down = out_refs
    size = d_expand.shape[1] // pieces
    span = pl.ds(pl.multiple_of(index * size, size), size)
    rows = normed[:, span]
    d_expand[0, span] = dot(rows, gate_ref[...], ROWS).astype(BF16)
    d_expand[1, span] = dot(rows, up_ref[...], ROWS).astype(BF16)
    d_down[:, span] = dot(hidden[...], land[:, span], ROWS).astype(BF16)


def mlp_forward(own, expand, layer, down_w, planes):
    count = planes * 4 * own.shape[0]
    shape = jax.ShapeDtypeStruct((count, down_w.shape[0]), BF16)
    return spread(
        mlp_chunk,
        None,
        own,
        (expand, down_w),
        layer,
        (shape,) * 3,
        (),
        planes,
        1,
        "mlp_forward",
    )


def mlp_backward(own, expand, layer, down_w, gate_slope, up_slope, normed, hidden, planes):
    d_expand = jax.ShapeDtypeStruct(expand.shape[1:], BF16)
    reduce = jax.ShapeDtypeStruct(down_w.shape, BF16)
    work = pltpu.VMEM(gate_slope.shape, BF16)
    return spread(
        mlp_back_chunk,
        mlp_back_piece,
        own,
        (expand, down_w, gate_slope, up_slope, normed, hidden),
        layer,
        (d_expand, reduce),
        (work, work),
        planes,
        2,
        "mlp_backward",
    )[1:]


def feed_forward(own, expand_layer, down_w):
    planes = lax.axis_size("ctx") // 2
    if planes == 4:
        return mlp_forward(own, *expand_layer, down_w, planes)
    expand = expand_layer[0][expand_layer[1]]
    rows = gather_tokens(own)
    gate, up = dot(rows, expand[0]), dot(rows, expand[1])
    sig = jax.nn.sigmoid(gate)
    silu = gate * sig
    hidden = (silu * up).astype(BF16)
    gate_slope = (up * sig * (1.0 + gate * (1.0 - sig))).astype(BF16)
    total = scatter_tokens(dot(hidden, down_w).astype(BF16))
    return rows, total, gate_slope, silu.astype(BF16), hidden


def feed_backward(own, expand_layer, down_w, gate_slope, up_slope, normed, hidden):
    planes = lax.axis_size("ctx") // 2
    if planes == 4:
        return mlp_backward(
            own, *expand_layer, down_w, gate_slope, up_slope, normed, hidden, planes
        )
    expand = expand_layer[0][expand_layer[1]]
    rows = own if own.shape[0] == normed.shape[0] else gather_tokens(own)
    grad_hidden = dot(rows, down_w, LAST)
    grad_gate = (grad_hidden * gate_slope.astype(F32)).astype(BF16)
    grad_up = (grad_hidden * up_slope.astype(F32)).astype(BF16)
    part = dot(grad_gate, expand[0], LAST) + dot(grad_up, expand[1], LAST)
    return (
        scatter_tokens(part.astype(BF16)),
        jnp.stack([dot(normed, grad_gate, ROWS), dot(normed, grad_up, ROWS)]).astype(BF16),
        dot(hidden, rows, ROWS).astype(BF16),
    )


def greet_line(planes, plane, core):
    barrier = pltpu.get_barrier_semaphore()
    pl.semaphore_signal(
        barrier, inc=1, device_id={"ctx": plane * 2 + 1 - core}, device_id_type=MESH
    )
    for step in range(1, planes):
        there = (plane + step) % planes
        pl.semaphore_signal(
            barrier, inc=1, device_id={"ctx": there * 2 + core}, device_id_type=MESH
        )
    pl.semaphore_wait(barrier, planes)


def attend_kernel(planes, heads, with_job, *refs):
    q_ref, kv_ref, qpos_ref, kpos_ref = refs[:4]
    if with_job:
        out_ref, low_ref, log_ref, all_ref = refs[5:9]
        zs, zr, cs, cr = refs[10:14]
        start, stage, finish = share_job(2 * planes, refs[4], refs[9], *refs[14:])
    else:
        out_ref, low_ref, log_ref, all_ref, zs, zr, cs, cr = refs[4:]
    ctx = lax.axis_index("ctx")
    plane, core = ctx // 2, ctx % 2
    batch, tokens, pair = kv_ref.shape
    head_dim = pair // 2
    factor = 1.0 / math.sqrt(head_dim)
    if with_job:
        greet_all(2 * planes, ctx)
    else:
        greet_line(planes, plane, core)
    core_peer = {"ctx": plane * 2 + 1 - core}

    def block(at):
        return all_ref.at[:, pl.ds(pl.multiple_of(at * tokens, tokens), tokens)]

    def along(there, source):
        ref = block(source * 2 + core)
        return remote(ref, ref, zs.at[there], zr.at[source], {"ctx": there * 2 + core})

    def beside(source, which):
        ref = block(source * 2 + which)
        return remote(ref, ref, cs.at[source], cr.at[source], core_peer)

    all_ref[:, pl.ds(pl.multiple_of(ctx * tokens, tokens), tokens)] = kv_ref[...]
    for step in range(1, planes):
        along((plane + step) % planes, plane).start()
    beside(plane, core).start()
    if with_job:
        start()
    for step in range(1, planes):
        source = (plane + step) % planes
        along(source, source).wait_recv()
        beside(source, core).start()
    for step in range(planes):
        beside((plane + step) % planes, 1 - core).wait_recv()

    def one(index, carry):
        rows = pl.ds(pl.multiple_of(index * tokens, tokens), tokens)
        keys = all_ref[index, :, :head_dim]
        values = all_ref[index, :, head_dim:]
        allowed = qpos_ref[index] >= kpos_ref[index]
        lane = lax.broadcasted_iota(jnp.int32, (tokens, head_dim), 1)
        logs = jnp.zeros((tokens, head_dim), F32)
        for head in range(heads):
            span = slice(head * head_dim, (head + 1) * head_dim)
            scores = dot(q_ref[rows, span], keys, LAST)
            scores = jnp.where(allowed, scores * factor, -1e30)
            top = jnp.max(scores, axis=1, keepdims=True)
            weights = jnp.exp(scores - top)
            total = jnp.sum(weights, axis=1, keepdims=True)
            logs = jnp.where(lane == head, top + jnp.log(total), logs)
            out = dot((weights * (1.0 / total)).astype(BF16), values)
            out_ref[rows, span] = out
            low_ref[rows, span] = out.astype(BF16)
        log_ref[rows] = logs
        return carry

    if with_job:
        stages = 2 * planes - 1
        for index in range(batch):
            stage(index)
            one(index, 0)
        for index in range(batch, stages):
            stage(index)
        finish()
    else:
        lax.fori_loop(0, batch, one, 0)
    for step in range(1, planes):
        along((plane + step) % planes, plane).wait_send()
        beside((plane + step) % planes, core).wait_send()
    beside(plane, core).wait_send()


def attend_back_kernel(
    planes, heads, q_ref, kv_ref, qpos_ref, kpos_ref, grad_ref, out_ref, log_ref, dq_ref, dkv_ref,
    whole, core_out, core_in, z_out, z_in, cs, cr, zs, zr,
):
    ctx = lax.axis_index("ctx")
    plane, core = ctx // 2, ctx % 2
    batch = qpos_ref.shape[0]
    tokens = q_ref.shape[0] // batch
    head_dim = kv_ref.shape[2] // 2
    factor = 1.0 / math.sqrt(head_dim)
    greet_line(planes, plane, core)
    core_peer = {"ctx": plane * 2 + 1 - core}

    def to_core(index):
        return remote(core_out.at[index], core_in.at[index], cs.at[index], cr.at[index], core_peer)

    def to_plane(index, there, source):
        return remote(
            z_out.at[index, there],
            z_in.at[index, source],
            zs.at[index, there],
            zr.at[index, source],
            {"ctx": there * 2 + core},
        )

    def one(index, carry):
        rows = pl.ds(pl.multiple_of(index * tokens, tokens), tokens)
        keys = kv_ref[index, :, :head_dim]
        values = kv_ref[index, :, head_dim:]
        allowed = qpos_ref[index] >= kpos_ref[index]
        logs = log_ref[rows]
        for head in range(heads):
            span = slice(head * head_dim, (head + 1) * head_dim)
            queries = q_ref[rows, span]
            grads = grad_ref[rows, span]
            delta = jnp.sum(grads.astype(F32) * out_ref[rows, span], axis=1, keepdims=True)
            scores = jnp.where(allowed, dot(queries, keys, LAST) * factor, -1e30)
            weights = jnp.exp(scores - logs[:, head : head + 1])
            grad_scores = (weights * (dot(grads, values, LAST) - delta) * factor).astype(BF16)
            dq_ref[rows, span] = dot(grad_scores, keys)
            grad_keys = dot(grad_scores, queries, ROWS)
            grad_values = dot(weights.astype(BF16), grads, ROWS)
            if head == 0:
                whole[index, :, :head_dim] = grad_keys
                whole[index, :, head_dim:] = grad_values
            else:
                whole[index, :, :head_dim] += grad_keys
                whole[index, :, head_dim:] += grad_values

        for at in range(planes):
            theirs = pl.multiple_of((at * 2 + 1 - core) * tokens, tokens)
            core_out[index, at] = whole[index, pl.ds(theirs, tokens)].astype(BF16)
        to_core(index).start()
        return carry

    lax.fori_loop(0, batch, one, 0)

    def mine(index, at):
        start = pl.multiple_of((at * 2 + core) * tokens, tokens)
        return whole[index, pl.ds(start, tokens)] + core_in[index, at].astype(F32)

    for index in range(batch):
        to_core(index).wait_recv()
        for step in range(1, planes):
            there = (plane + step) % planes
            z_out[index, there] = mine(index, there).astype(BF16)
            to_plane(index, there, plane).start()
        dkv_ref[index] = mine(index, plane)
    for index in range(batch):
        for step in range(1, planes):
            source = (plane + step) % planes
            to_plane(index, source, source).wait_recv()
            dkv_ref[index] += z_in[index, source].astype(F32)
    for index in range(batch):
        to_core(index).wait_send()
        for step in range(1, planes):
            to_plane(index, (plane + step) % planes, plane).wait_send()


def attend(queries, kv, query_pos, key_pos, blocks):
    batch, tokens, pair = kv.shape
    head_dim = pair // 2
    heads = queries.shape[1] // head_dim
    planes = lax.axis_size("ctx") // 2
    keys = key_pos.shape[1]
    if planes != 4:
        kv_all = gather_ctx(kv, 1)
        split = queries.reshape(batch, tokens, heads, head_dim)
        scores = jnp.einsum(
            "bqhd,bkd->bqhk", split, kv_all[..., :head_dim], preferred_element_type=F32
        )
        allowed = query_pos[:, :, None, None] >= key_pos[:, None, None, :]
        scores = jnp.where(allowed, scores / math.sqrt(head_dim), -1e30)
        logs = jax.nn.logsumexp(scores, axis=-1)
        probs = jnp.exp(scores - logs[..., None]).astype(BF16)
        out = jnp.einsum(
            "bqhk,bkd->bqhd", probs, kv_all[..., head_dim:], preferred_element_type=F32
        ).reshape(queries.shape)
        shared = [share(part) for part in blocks]
        return out, out.astype(BF16), logs, kv_all, *shared
    size = 2 * planes
    shape = jax.ShapeDtypeStruct
    dma = pltpu.SemaphoreType.DMA
    rows = batch * tokens
    return pl.pallas_call(
        functools.partial(attend_kernel, planes, heads, len(blocks) > 0),
        out_shape=[
            shape(queries.shape, F32),
            shape(queries.shape, BF16),
            shape((rows, head_dim), F32),
            shape((batch, keys, pair), BF16),
        ]
        + [shape((2,) + part.shape, part.dtype) for part in blocks],
        in_specs=[VMEM] * 4 + [HBM] * len(blocks),
        out_specs=[VMEM] * 4 + [HBM] * len(blocks),
        scratch_shapes=[dma((planes,)), dma((planes,)), dma((planes,)), dma((planes,))]
        + ([dma((size,))] * 4 + [dma]) * len(blocks),
        compiler_params=pltpu.CompilerParams(
            collective_id=3 + 2 * len(blocks), has_side_effects=True, vmem_limit_bytes=48 << 20
        ),
        cost_estimate=pl.CostEstimate(
            flops=rows * keys, bytes_accessed=rows, transcendentals=0
        ),
        name="attend",
    )(queries, kv, query_pos[:, :, None], key_pos[:, None, :], *blocks)


def attend_backward(queries, kv_all, query_pos, key_pos, grads, out, logs):
    batch, keys, pair = kv_all.shape
    head_dim = pair // 2
    heads = queries.shape[1] // head_dim
    rows = queries.shape[0]
    tokens = rows // batch
    planes = lax.axis_size("ctx") // 2
    if planes != 4:
        factor = 1.0 / math.sqrt(head_dim)
        k_all, v_all = kv_all[..., :head_dim], kv_all[..., head_dim:]
        split = queries.reshape(batch, tokens, heads, head_dim)
        grad_split = grads.reshape(split.shape)
        delta = jnp.sum(grad_split.astype(F32) * out.reshape(split.shape), axis=-1)
        scores = jnp.einsum("bqhd,bkd->bqhk", split, k_all, preferred_element_type=F32)
        allowed = query_pos[:, :, None, None] >= key_pos[:, None, None, :]
        scores = jnp.where(allowed, scores * factor, -1e30)
        probs = jnp.exp(scores - logs[..., None])
        grad_probs = jnp.einsum("bqhd,bkd->bqhk", grad_split, v_all, preferred_element_type=F32)
        grad_scores = (probs * (grad_probs - delta[..., None]) * factor).astype(BF16)
        dq = jnp.einsum("bqhk,bkd->bqhd", grad_scores, k_all, preferred_element_type=F32)
        dk = jnp.einsum("bqhk,bqhd->bkd", grad_scores, split, preferred_element_type=F32)
        dv = jnp.einsum(
            "bqhk,bqhd->bkd", probs.astype(BF16), grad_split, preferred_element_type=F32
        )
        dkv = lax.psum_scatter(
            jnp.concatenate([dk, dv], axis=-1).astype(BF16), "ctx", scatter_dimension=1, tiled=True
        )
        return dq.reshape(queries.shape), dkv.astype(F32)
    shape = jax.ShapeDtypeStruct
    dma = pltpu.SemaphoreType.DMA
    return pl.pallas_call(
        functools.partial(attend_back_kernel, planes, heads),
        out_shape=[shape(queries.shape, F32), shape((batch, tokens, pair), F32)],
        in_specs=[VMEM] * 7,
        out_specs=[VMEM] * 2,
        scratch_shapes=[
            pltpu.VMEM((batch, keys, pair), F32),
            pltpu.VMEM((batch, planes, tokens, pair), BF16),
            pltpu.VMEM((batch, planes, tokens, pair), BF16),
            pltpu.VMEM((batch, planes, tokens, pair), BF16),
            pltpu.VMEM((batch, planes, tokens, pair), BF16),
            dma((batch,)), dma((batch,)), dma((batch, planes)), dma((batch, planes)),
        ],
        compiler_params=pltpu.CompilerParams(
            collective_id=4, has_side_effects=True, vmem_limit_bytes=48 << 20
        ),
        cost_estimate=pl.CostEstimate(
            flops=rows * keys, bytes_accessed=rows, transcendentals=0
        ),
        name="attend_backward",
    )(queries, kv_all, query_pos[:, :, None], key_pos[:, None, :], grads, out, logs)


def layer_forward(x_low, weights, tables, blocks, sooner, later):
    gain_attn, w_mixed, bias, w_project, gain_mlp, w_expand, w_reduce = weights
    cosine, sine, query_pos, key_pos, mine = tables
    count, width = x_low.shape
    query_width = w_project.shape[0]
    head_dim = (w_mixed.shape[1] - query_width) // 2
    heads = query_width // head_dim
    batch = query_pos.shape[0]
    tokens = count // batch
    x = x_low.astype(F32)
    root_attn = inverse_root(x)
    normed = (x * root_attn * gain_attn).astype(BF16)
    mixed = dot(normed, w_mixed) + bias
    queries = rotate(
        mixed[:, :query_width].reshape(count, heads, head_dim),
        cosine[:, None, :],
        sine[:, None, :],
    ).astype(BF16).reshape(count, query_width)
    keys = rotate(mixed[:, query_width : query_width + head_dim], cosine, sine)
    kv = jnp.concatenate([keys, mixed[:, query_width + head_dim :]], axis=1).astype(BF16)
    kv, sooner = lax.optimization_barrier((kv, sooner))
    attended_full, attended, log_total, kv, *shared = attend(
        queries, kv.reshape(batch, tokens, 2 * head_dim), query_pos, key_pos, blocks
    )
    if shared:
        w_expand = (shared[0].reshape((2, 2, width, -1)), 0)
    x_mine = lax.dynamic_slice_in_dim(x, mine * tokens, tokens, 0)
    middle = x_mine + tensor_scatter(dot(attended, w_project))
    root_mlp = inverse_root(middle)
    normed_mlp = (middle * root_mlp * gain_mlp).astype(BF16)
    normed_mlp, later = lax.optimization_barrier((normed_mlp, later))
    all_normed, branch, gate_slope, up_slope, hidden = feed_forward(
        normed_mlp, w_expand, w_reduce
    )
    result = middle + branch
    kept = (
        x_mine,
        lax.dynamic_slice_in_dim(root_attn, mine * tokens, tokens, 0),
        normed,
        queries,
        kv,
        attended_full,
        log_total,
        attended,
        middle,
        root_mlp,
        all_normed,
        gate_slope,
        up_slope,
        hidden,
    )
    return result.astype(BF16), kept, w_expand, sooner, later


def layer_backward(grad_out, grad_rows, kept, weights, tables, route, earlier, pinned):
    gain_attn, w_mixed, bias, w_project, gain_mlp, w_expand, w_reduce = weights
    cosine, sine, query_pos, key_pos, mine = tables
    (
        x_mine,
        root_attn,
        normed,
        queries,
        kv,
        attended_full,
        log_total,
        attended,
        middle,
        root_mlp,
        all_normed,
        gate_slope,
        up_slope,
        hidden,
    ) = kept
    count, query_width = queries.shape
    head_dim = (w_mixed.shape[1] - query_width) // 2
    heads = query_width // head_dim
    grad_normed_mlp, d_expand, d_reduce = feed_backward(
        grad_rows,
        w_expand,
        w_reduce,
        gate_slope,
        up_slope,
        all_normed,
        hidden,
    )
    grad_normed_mlp, earlier = lax.optimization_barrier((grad_normed_mlp, earlier))
    moved_reduce = lax.ppermute(d_reduce, "section", route)
    grad_middle, d_gain_mlp = norm_backward(middle, root_mlp, gain_mlp, grad_normed_mlp)
    grad_middle = grad_middle + grad_out
    grad_branch = tensor_gather(grad_middle.astype(BF16))
    d_project = dot(attended, grad_branch, ROWS)
    grad_attended = dot(grad_branch, w_project, LAST).astype(BF16)
    grad_q, grad_kv = attend_backward(
        queries, kv, query_pos, key_pos, grad_attended, attended_full, log_total
    )
    grad_q, grad_kv, moved_reduce, pinned = lax.optimization_barrier(
        (grad_q, grad_kv, moved_reduce, pinned)
    )
    grad_kv = grad_kv.reshape(count, 2 * head_dim)
    grad_q = unrotate(
        grad_q.reshape(count, heads, head_dim), cosine[:, None, :], sine[:, None, :]
    )
    grad_k = unrotate(grad_kv[:, :head_dim], cosine, sine)
    grad_mixed = jnp.concatenate(
        [grad_q.reshape(count, heads * head_dim), grad_k, grad_kv[:, head_dim:]], axis=1
    ).astype(BF16)
    d_mixed = dot(normed, grad_mixed, ROWS)
    d_bias = jnp.sum(grad_mixed.astype(F32), axis=0)
    grad_normed = tensor_scatter(dot(grad_mixed, w_mixed, LAST))
    grad_x, d_gain_attn = norm_backward(x_mine, root_attn, gain_attn, grad_normed)
    grad_x = (grad_x + grad_middle).astype(BF16)
    vectors = (d_gain_attn, d_mixed, d_bias, d_project, d_gain_mlp)
    return grad_x, vectors, d_expand, (d_reduce, moved_reduce), earlier, pinned


def shards(
    block_input, positions, cotangent, norm_attn, w_qkv, b_qkv, w_out, norm_mlp, w_gate_up, w_down
):
    section = lax.axis_index("section")
    tensor = lax.axis_index("tensor")
    ctx = lax.axis_index("ctx")
    ctx_size = lax.axis_size("ctx")
    first = section == 0
    micro, tokens, width = block_input.shape
    half = micro // 2
    head_dim = w_qkv.shape[3] - w_out.shape[2] * ctx_size
    head_dim = head_dim // 2
    slice_width = norm_attn.shape[1]
    slice_bias = b_qkv.shape[2]
    units = w_down.shape[1]

    def plane_part(value):
        return lax.dynamic_slice_in_dim(value, section * half, half, 0)

    def layers(own, other):
        return jnp.where(first, own, other), jnp.where(first, other, own)

    x = plane_part(block_input).reshape(half * tokens, width)
    pos_local = plane_part(positions)
    cosine, sine = angles(pos_local.reshape(-1), head_dim)

    small = jnp.concatenate([norm_attn[0], norm_mlp[0], b_qkv[0, 0]])
    qkv, out = w_qkv[0, :, 0, :], w_out[0, 0]
    vectors = jnp.concatenate(layers(small, swap(small)))
    places = jnp.concatenate([pos_local // 64, pos_local % 64]).reshape(-1).astype(BF16)
    packed = gather_ctx(jnp.concatenate([vectors, places])[None], 0)
    places = packed[:, vectors.shape[0] :].astype(jnp.int32).reshape(ctx_size, 2, half, tokens)
    pos_all = jnp.swapaxes(places[:, 0] * 64 + places[:, 1], 0, 1).reshape(half, -1)
    tables = (cosine, sine, pos_local, pos_all, tensor)
    small_size = 2 * slice_width + slice_bias
    small0, small1 = packed[:, :small_size], packed[:, small_size : 2 * small_size]
    qkv0, qkv1 = layers(qkv, swap(qkv))
    out0, out1 = layers(out, swap(out))
    down_moved = swap(w_down[0])
    down0, down1 = layers(w_down[0], down_moved)
    expand = w_gate_up[0].reshape(slice_width, 2, ctx_size, units)
    blocks = jnp.transpose(expand, (1, 2, 0, 3))

    def whole(small, qkv, out, expand, down):
        return (
            small[:, :slice_width].reshape(1, width),
            gather_ctx(qkv, 0),
            small[:, 2 * slice_width :].reshape(1, slice_bias * ctx_size),
            gather_ctx(out, 0),
            small[:, slice_width : 2 * slice_width].reshape(1, width),
            expand,
            down,
        )

    weights0 = whole(small0, qkv0, out0, None, down0)

    result0, kept0, expand0, down_moved, (qkv1, out1) = layer_forward(
        x, weights0, tables, (blocks,), down_moved, (qkv1, out1)
    )
    weights0 = weights0[:5] + (expand0, down0)
    weights1 = whole(small1, qkv1, out1, (expand0[0], 1), down1)
    x1 = tensor_gather(result0)
    seeds, x1 = lax.optimization_barrier((plane_part(cotangent), x1))
    seed_rows = gather_ctx(seeds.reshape(half * tokens, width), 0)
    result1, kept1, *_ = layer_forward(x1, weights1, tables, (), (), ())
    out1_all = tensor_pair(result1)

    def exchange(layer0, layer1):
        kept_here = jnp.where(first, layer0, layer1)
        received = swap(jnp.where(first, layer1, layer0))
        low = jnp.where(first, kept_here, received)
        high = jnp.where(first, received, kept_here)
        both = jnp.concatenate([low, high], axis=0)
        return both.reshape(1, micro, tokens, width)

    seed = lax.dynamic_slice_in_dim(seeds, tensor, 1, 0)[0].astype(F32)
    def ctx_scatter(value):
        return lax.psum_scatter(
            value.astype(BF16), "ctx", scatter_dimension=0, tiled=True
        )

    group = w_qkv.shape[3]
    split_at = group - head_dim

    def with_vectors(grads):
        gain_attn, mixed, bias, project, gain_mlp = grads[:5]
        rows = jnp.concatenate(
            [
                bias[:split_at].reshape(ctx_size, -1),
                bias[split_at:].reshape(ctx_size, -1),
                gain_attn.reshape(ctx_size, slice_width),
                gain_mlp.reshape(ctx_size, slice_width),
            ],
            axis=1,
        )
        rows = jnp.pad(rows[:, None, :], ((0, 0), (0, 15), (0, group - rows.shape[1])))
        mixed = mixed.reshape(ctx_size, slice_width, group)
        both = jnp.concatenate([mixed.astype(BF16), rows.astype(BF16)], axis=1)
        return both.reshape(ctx_size * (slice_width + 16), group)

    grad1, d1, d_expand1, d_reduce1, _, out1_all = layer_backward(
        seed, seed_rows, kept1, weights1, tables, [(0, 1)], (), out1_all
    )
    section_output = exchange(x1, out1_all)
    slices1 = (ctx_scatter(with_vectors(d1)), ctx_scatter(d1[3]))
    grad1_all = tensor_pair(grad1)
    grad0, d0, d_expand0, d_reduce0, earlier, _ = layer_backward(
        grad1.astype(F32), grad1, kept0, weights0, tables, [(1, 0)], slices1 + (section_output, grad1_all), ()
    )
    slices1, (section_output, grad1_all) = earlier[:2], earlier[2:]

    def to_owner(part0, part1):
        received0 = lax.ppermute(part0.astype(BF16), "section", [(1, 0)])
        received1 = lax.ppermute(part1.astype(BF16), "section", [(0, 1)])
        own = jnp.where(first, part0, part1).astype(F32)
        return own + jnp.where(first, received0, received1).astype(F32)

    def of_owner(pair0, pair1):
        own, received = (jnp.where(first, low, high).astype(F32) for low, high in zip(pair0, pair1))
        return own + received

    blocks = (2, ctx_size, slice_width, units)
    grad0_all = tensor_pair(grad0)
    grad0_all, d_expand0 = lax.optimization_barrier((grad0_all, d_expand0))
    input_grad = exchange(grad0_all, grad1_all)
    total = collect(d_expand0.reshape(blocks), d_expand1.reshape(blocks), first)
    d_expand = lax.optimization_barrier(jnp.transpose(total, (2, 0, 1, 3)))
    d_expand = lax.optimization_barrier(d_expand.reshape(1, slice_width, 2, ctx_size * units))
    d_expand = d_expand.astype(F32)
    d_reduce = of_owner(d_reduce0, d_reduce1)

    d_mixed = to_owner(ctx_scatter(with_vectors(d0)), slices1[0])
    d_project = to_owner(ctx_scatter(d0[3]), slices1[1])
    vectors = d_mixed[slice_width]
    d_mixed = d_mixed[:slice_width]
    count_qk, count_v = split_at // ctx_size, head_dim // ctx_size
    bias_qk = vectors[:count_qk][None]
    bias_v = vectors[count_qk : count_qk + count_v][None]
    start = count_qk + count_v
    gains = vectors[start : start + 2 * slice_width].reshape(1, 2 * slice_width)
    gains = gains + lax.ppermute(gains, "tensor", SWAP)
    return (
        section_output,
        input_grad,
        gains[:, :slice_width],
        d_mixed[None, :, None, :],
        bias_qk[None],
        bias_v[None],
        d_project[None, None],
        gains[:, slice_width:],
        d_expand,
        d_reduce[None],
    )


def solution(mesh):
    in_specs = (
        P(None, "ctx", None),
        P(None, "ctx"),
        P(None, "ctx", None),
        P("section", "ctx"),
        P("section", "ctx", "tensor", None),
        P("section", "tensor", "ctx"),
        P("section", "tensor", "ctx", None),
        P("section", "ctx"),
        P("section", "ctx", None, "tensor"),
        P("section", ("tensor", "ctx"), None),
    )
    out_specs = (
        P("section", None, "ctx", None),
        P("section", None, "ctx", None),
        P("section", "ctx"),
        P("section", "ctx", "tensor", None),
        P("section", "tensor", "ctx"),
        P("section", "tensor", "ctx"),
        P("section", "tensor", "ctx", None),
        P("section", "ctx"),
        P("section", "ctx", None, "tensor"),
        P("section", ("tensor", "ctx"), None),
    )
    return jax.shard_map(shards, mesh=mesh, in_specs=in_specs, out_specs=out_specs, check_vma=False)
```

```python
import functools
import functools
import math

import jax
import jax.numpy as jnp
from jax import lax
from jax.experimental import pallas as pl
from jax.experimental.pallas import tpu as pltpu
from jax.sharding import PartitionSpec as P

EPSILON = 1e-06
ROPE_BASE = 1000000.0
ROWS = (((0,), (0,)), ((), ()))
LAST = (((1,), (1,)), ((), ()))
F32 = jnp.float32
BF16 = jnp.bfloat16
SWAP = [(0, 1), (1, 0)]
MESH = pl.DeviceIdType.MESH
VMEM = pl.BlockSpec(memory_space=pltpu.VMEM)
HBM = pl.BlockSpec(memory_space=pl.ANY)


def dot(a, b, dims=(((1,), (0,)), ((), ()))):
    return lax.dot_general(a, b, dims, preferred_element_type=F32)


def angles(positions, head_dim):
    half_dim = head_dim // 2
    frequency = ROPE_BASE ** (-(jnp.arange(half_dim, dtype=F32) * 2.0) / head_dim)
    phases = positions.astype(F32)[:, None] * frequency[None, :]
    phases = jnp.concatenate([phases, phases], axis=-1)
    return jnp.cos(phases), jnp.sin(phases)


def rotate(values, cosine, sine):
    half = values.shape[-1] // 2
    turned = jnp.concatenate([-values[..., half:], values[..., :half]], axis=-1)
    return values * cosine + turned * sine


def unrotate(grads, cosine, sine):
    half = grads.shape[-1] // 2
    twisted = grads * sine
    turned = jnp.concatenate([twisted[..., half:], -twisted[..., :half]], axis=-1)
    return grads * cosine + turned


def inverse_root(values):
    return lax.rsqrt(jnp.mean(values * values, axis=-1, keepdims=True) + EPSILON)


def norm_backward(values, root, gain, grad_normed):
    normal = values * root
    gain_grad = jnp.sum(grad_normed * normal, axis=0)
    scaled = grad_normed * gain
    mean = jnp.mean(scaled * normal, axis=-1, keepdims=True)
    return root * (scaled - normal * mean), gain_grad


def swap(value):
    return lax.ppermute(value, "section", SWAP)


def gather_ctx(value, axis):
    return lax.all_gather(value, "ctx", axis=axis, tiled=True)


def gather_tokens(rows):
    return lax.all_gather(rows, ("ctx", "tensor"), axis=0, tiled=True)


def scatter_tokens(rows):
    return lax.psum_scatter(rows, ("ctx", "tensor"), scatter_dimension=0, tiled=True).astype(F32)


def tensor_gather(rows):
    return lax.all_gather(rows, "tensor", axis=0, tiled=True)


def tensor_pair(rows):
    received = lax.ppermute(rows, "tensor", SWAP)
    mine = lax.axis_index("tensor") == 0
    return jnp.concatenate([jnp.where(mine, rows, received), jnp.where(mine, received, rows)])


def tensor_scatter(rows):
    mine = lax.axis_index("tensor")
    tokens = rows.shape[0] // 2
    own = lax.dynamic_slice_in_dim(rows, mine * tokens, tokens, 0)
    other = lax.dynamic_slice_in_dim(rows, (1 - mine) * tokens, tokens, 0)
    return own + lax.ppermute(other.astype(BF16), "tensor", SWAP).astype(F32)


def greet_all(size, me):
    barrier = pltpu.get_barrier_semaphore()
    for step in range(1, size):
        pl.semaphore_signal(
            barrier, inc=1, device_id={"ctx": (me + step) % size}, device_id_type=MESH
        )
    there = 1 - lax.axis_index("section")
    pl.semaphore_signal(barrier, inc=1, device_id={"section": there}, device_id_type=MESH)
    pl.semaphore_wait(barrier, size)


def by_distance(size):
    return sorted(range(size), key=lambda step: min(step, size - step))


def share_job(size, from_ref, all_ref, send, recv, over_send, over_recv, local):
    me = lax.axis_index("ctx")
    section = lax.axis_index("section")
    order = by_distance(size)[1:]

    def copy(there, source):
        return remote(
            from_ref.at[:, there],
            all_ref.at[section, :, source],
            send.at[there],
            recv.at[source],
            {"ctx": there},
        )

    def over(block, source):
        return remote(
            block,
            all_ref.at[section, :, source],
            over_send.at[source],
            over_recv.at[source],
            {"section": 1 - section},
        )

    def own():
        return pltpu.make_async_copy(from_ref.at[:, me], all_ref.at[section, :, me], local)

    def start():
        own().start()
        over(from_ref.at[:, me], me).start()
        for step in order[:2]:
            copy((me + step) % size, me).start()

    def stage(index):
        step = order[index]
        source = (me + size - step) % size
        copy(source, source).wait_recv()
        over(all_ref.at[section, :, source], source).start()
        copy((me + step) % size, me).wait_send()
        if index + 2 < len(order):
            copy((me + order[index + 2]) % size, me).start()

    def finish():
        own().wait()
        for step in range(size):
            source = (me + step) % size
            over(all_ref.at[section, :, source], source).wait()

    return start, stage, finish


def share(blocks):
    moved = lax.all_to_all(blocks, "ctx", split_axis=1, concat_axis=1, tiled=True)
    return lax.all_gather(moved, "section")


def collect_kernel(
    size, first_ref, second_ref, to_ref, own, other, send, recv, over_send, over_recv, local, store
):
    me = lax.axis_index("ctx")
    section = lax.axis_index("section")
    greet_all(size, me)
    order = by_distance(size)[::-1]

    def over(source_ref, at):
        return remote(
            source_ref.at[:, at], other.at[at], over_send.at[at], over_recv.at[at],
            {"section": 1 - section},
        )

    def load(source_ref, at):
        return pltpu.make_async_copy(source_ref.at[:, at], own.at[at], local.at[at])

    def copy(there, source):
        return remote(
            own.at[there], to_ref.at[:, source], send.at[there], recv.at[source], {"ctx": there}
        )

    def start(at):
        @pl.when(section == 0)
        def _():
            over(second_ref, at).start()
            load(first_ref, at).start()

        @pl.when(section == 1)
        def _():
            over(first_ref, at).start()
            load(second_ref, at).start()

    for index, step in enumerate(order):
        at = (me + step) % size
        if index == 0:
            start(at)
        if index + 1 < size:
            start((me + order[index + 1]) % size)
        over(first_ref, at).wait()
        load(first_ref, at).wait()
        own[at] = (own[at].astype(F32) + other[at].astype(F32)).astype(own.dtype)
        if step > 0:
            copy(at, me).start()
        else:
            mine = pltpu.make_async_copy(own.at[at], to_ref.at[:, me], store)
            mine.start()
            mine.wait()
    for step in order:
        at = (me + step) % size
        if step > 0:
            copy(at, at).wait_recv()
            copy(at, me).wait_send()


def collect(first, second, is_first):
    parts, size, rows, columns = first.shape
    if size != 8:
        received = lax.ppermute(jnp.where(is_first, second, first), "section", SWAP)
        total = jnp.where(is_first, first, second).astype(F32) + received.astype(F32)
        return lax.all_to_all(
            total.astype(BF16), "ctx", split_axis=1, concat_axis=1, tiled=True
        )
    dma = pltpu.SemaphoreType.DMA
    block = pltpu.VMEM((size, parts, rows, columns), first.dtype)
    return pl.pallas_call(
        functools.partial(collect_kernel, size),
        out_shape=jax.ShapeDtypeStruct(first.shape, first.dtype),
        in_specs=[HBM, HBM],
        out_specs=HBM,
        scratch_shapes=[block, block]
        + [dma((size,)), dma((size,)), dma((size,)), dma((size,)), dma((size,)), dma],
        compiler_params=pltpu.CompilerParams(
            collective_id=6, has_side_effects=True, vmem_limit_bytes=24 << 20
        ),
        cost_estimate=pl.CostEstimate(flops=first.size, bytes_accessed=1024, transcendentals=0),
        name="collect",
    )(first, second)


def remote(src, dst, send, recv, device):
    return pltpu.make_async_remote_copy(
        src_ref=src, dst_ref=dst, send_sem=send, recv_sem=recv, device_id=device, device_id_type=MESH
    )


def spread_kernel(
    chunk, piece, layer, planes, gathered, reduced, ins, outs, extra, own_ref, *refs
):
    in_refs, refs = refs[:ins], refs[ins:]
    all_ref, sum_ref = refs[:2]
    out_refs, refs = refs[2 : 2 + outs], refs[2 + outs :]
    work_refs, refs = refs[:extra], refs[extra:]
    (expand_w, load_sem), refs = refs[:2], refs[2:]
    load = pltpu.make_async_copy(in_refs[0].at[layer], expand_w, load_sem)
    load.start()
    in_refs = (expand_w,) + in_refs[1:]
    (land, core_out, core_in, y_out, y_in, z_out, z_in, both, kept,
     zs, zr, ys, yr, cs, cr, rcs, rcr, rys, ryr, rzs, rzr, local) = refs
    tensor = lax.axis_index("tensor")
    ctx = lax.axis_index("ctx")
    plane, core = ctx // 2, ctx % 2
    rows = own_ref.shape[0] // (4 * planes if gathered else 1)
    y_peer = {"tensor": 1 - tensor}
    core_peer = {"ctx": plane * 2 + 1 - core}

    barrier = pltpu.get_barrier_semaphore()
    pl.semaphore_signal(barrier, inc=1, device_id=y_peer, device_id_type=MESH)
    pl.semaphore_signal(barrier, inc=1, device_id=core_peer, device_id_type=MESH)
    for step in range(1, planes):
        there = (plane + step) % planes
        pl.semaphore_signal(barrier, inc=1, device_id={"ctx": there * 2 + core}, device_id_type=MESH)
    pl.semaphore_wait(barrier, planes + 1)

    def block(at, which_core, which_tensor):
        start = pl.multiple_of(((at * 2 + which_core) * 2 + which_tensor) * rows, rows)
        return land.at[pl.ds(start, rows)]

    def along(at, target, direction):
        ref = block(at, core, tensor)
        return remote(ref, ref, zs.at[at, direction], zr.at[at], {"ctx": target * 2 + core})

    def across(at, which_tensor):
        ref = block(at, core, which_tensor)
        return remote(ref, ref, ys.at[at], yr.at[at], y_peer)

    def beside(at, which_core, which_tensor, slot):
        ref = block(at, which_core, which_tensor)
        return remote(ref, ref, cs.at[at, slot], cr.at[at, slot], core_peer)

    if not gathered:
        start = pl.multiple_of(((plane * 2 + core) * 2 + tensor) * rows, rows)
        land[pl.ds(start, rows)] = own_ref[...]

        @pl.when(plane < planes - 1)
        def _():
            along(plane, plane + 1, 0).start()

        @pl.when(plane > 0)
        def _():
            along(plane, plane - 1, 1).start()

        across(plane, tensor).start()
        beside(plane, core, tensor, 0).start()

    def reduce_core(at):
        return remote(core_out.at[at], core_in.at[at], rcs.at[at], rcr.at[at], core_peer)

    def reduce_y(at):
        return remote(y_out.at[at], y_in.at[at], rys.at[at], ryr.at[at], y_peer)

    def reduce_z(at):
        return remote(z_out.at[at], z_in.at[plane], rzs.at[at], rzr.at[plane], {"ctx": at * 2 + core})

    def reduced_z(at):
        return remote(z_out.at[at], z_in.at[at], rzs.at[at], rzr.at[at], {"ctx": at * 2 + core})

    def save(at):
        span = pl.ds(pl.multiple_of(at * 4 * rows, 4 * rows), 4 * rows)
        return pltpu.make_async_copy(land.at[span], all_ref.at[span], local.at[at])

    def side_plane(distance, side):
        return plane + distance * (2 * side - 1)

    def inside(at):
        return jnp.logical_and(at >= 0, at < planes)

    def pass_on(distance, side):
        at = side_plane(distance, side)
        target = plane + 1 - 2 * side

        @pl.when(inside(at))
        def _():
            along(at, plane, 0).wait_recv()

            @pl.when(inside(target))
            def _():
                along(at, target, side).start()

            across(at, tensor).start()
            beside(at, core, tensor, 0).start()

    def pass_beside(distance, side):
        at = side_plane(distance, side)

        @pl.when(inside(at))
        def _():
            across(at, 1 - tensor).wait_recv()
            beside(at, core, 1 - tensor, 1).start()

    def fetch(at):
        span = pl.ds(pl.multiple_of(at * 4 * rows, 4 * rows), 4 * rows)
        return pltpu.make_async_copy(own_ref.at[span], land.at[span], local.at[at])

    if gathered:
        for at in range(planes):
            fetch(at).start()

    def step(index, carry):
        if gathered:
            index = 2 * planes - 2 - index
        distance = (index + 1) // 2
        at = side_plane(distance, 1 - index % 2)

        if not gathered:

            @pl.when(jnp.logical_or(index == 0, index % 2 == 1))
            def _():
                pass_on(distance + 1, 0)
                pass_on(distance + 1, 1)

                @pl.when(distance > 0)
                def _():
                    pass_beside(distance, 0)

                pass_beside(distance, 1)

        @pl.when(inside(at))
        def _():
            if gathered:
                fetch(at).wait()
            else:
                beside(at, 1 - core, tensor, 0).wait_recv()
                beside(at, 1 - core, 1 - tensor, 1).wait_recv()
            if piece is None:
                save(at).start()
            theirs = pl.multiple_of((at * 2 + 1 - core) * 2 * rows, 2 * rows)
            mine = pl.multiple_of((at * 2 + core) * 2 * rows, 2 * rows)
            if not reduced:
                for start in (theirs, mine):
                    part = chunk(land, start, 2 * rows, in_refs, out_refs, work_refs)
                    sum_ref[pl.ds(start, 2 * rows)] = part.astype(BF16)
                return
            core_out[at] = chunk(land, theirs, 2 * rows, in_refs, out_refs, work_refs).astype(BF16)
            reduce_core(at).start()
            both[...] = chunk(land, mine, 2 * rows, in_refs, out_refs, work_refs)
            reduce_core(at).wait_recv()
            both[...] += core_in[at].astype(F32)
            other = pl.multiple_of((1 - tensor) * rows, rows)
            own = pl.multiple_of(tensor * rows, rows)
            y_out[at] = both[pl.ds(other, rows)].astype(BF16)

            @pl.when(index > 0)
            def _():
                reduce_y(at).start()

            kept[at] = both[pl.ds(own, rows)]

        return carry

    load.wait()
    lax.fori_loop(0, 2 * planes - 1, step, 0)

    if reduced:
        reduce_y(plane).start()

        def collect(index, count):
            if gathered:
                index = 2 * planes - 3 - index
            at = side_plane((index + 2) // 2, index % 2)

            @pl.when(inside(at))
            def _():
                if piece is not None:
                    piece(land, count, planes, in_refs, out_refs, work_refs)
                reduce_y(at).wait_recv()
                z_out[at] = (kept[at] + y_in[at].astype(F32)).astype(BF16)
                reduce_z(at).start()

            return count + inside(at).astype(jnp.int32)

        count = lax.fori_loop(0, 2 * planes - 2, collect, 0)
        if piece is not None:
            piece(land, count, planes, in_refs, out_refs, work_refs)
        reduce_y(plane).wait_recv()
        sum_ref[...] = kept[plane] + y_in[plane].astype(F32)

        def finish(index, carry):
            at = (plane + 1 + index) % planes
            reduced_z(at).wait_recv()
            sum_ref[...] += z_in[at].astype(F32)
            return carry

        lax.fori_loop(0, planes - 1, finish, 0)

    if not gathered:
        @pl.when(plane < planes - 1)
        def _():
            along(plane, plane + 1, 0).wait_send()

        @pl.when(plane > 0)
        def _():
            along(plane, plane - 1, 1).wait_send()

    def drain(index, carry):
        distance = (index + 1) // 2
        side = 1 - index % 2
        at = side_plane(distance, side)
        target = plane + 1 - 2 * side

        @pl.when(inside(at))
        def _():
            if not gathered:

                @pl.when(jnp.logical_and(index > 0, inside(target)))
                def _():
                    along(at, target, side).wait_send()

                across(at, tensor).wait_send()
                beside(at, core, tensor, 0).wait_send()
                beside(at, core, 1 - tensor, 1).wait_send()
            if piece is None:
                save(at).wait()
            if reduced:
                reduce_core(at).wait_send()
                reduce_y(at).wait_send()

                @pl.when(index > 0)
                def _():
                    reduce_z(at).wait_send()

        return carry

    lax.fori_loop(0, 2 * planes - 1, drain, 0)


def spread(chunk, piece, own, inputs, layer, outputs, work, planes, ident, name, reduced=True):
    rows, width = own.shape
    gathered = rows == inputs[2].shape[0] if len(inputs) > 2 else False
    if gathered:
        rows //= 4 * planes
    count = planes * 4 * rows
    dma = pltpu.SemaphoreType.DMA
    shape = jax.ShapeDtypeStruct
    saved = (count, width) if piece is None else (16, width)
    total = shape((rows, width), F32) if reduced else shape((count, width), BF16)
    outs = [shape(saved, BF16), total] + list(outputs)
    held = planes if reduced else 1
    return pl.pallas_call(
        functools.partial(
            spread_kernel, chunk, piece, layer, planes, gathered, reduced, len(inputs), len(outputs), len(work)
        ),
        out_shape=outs,
        in_specs=[HBM if gathered else VMEM, HBM] + [VMEM] * (len(inputs) - 1),
        out_specs=[HBM, VMEM] + [VMEM] * len(outputs),
        scratch_shapes=list(work)
        + [
            pltpu.VMEM(inputs[0].shape[1:], BF16),
            pltpu.SemaphoreType.DMA,
            pltpu.VMEM((count, width), BF16),
            pltpu.VMEM((held, 2 * rows, width), BF16),
            pltpu.VMEM((held, 2 * rows, width), BF16),
            pltpu.VMEM((held, rows, width), BF16),
            pltpu.VMEM((held, rows, width), BF16),
            pltpu.VMEM((held, rows, width), BF16),
            pltpu.VMEM((held, rows, width), BF16),
            pltpu.VMEM((2 * rows, width), F32),
            pltpu.VMEM((held, rows, width), F32),
            dma((planes, 2)), dma((planes,)), dma((planes,)), dma((planes,)), dma((planes, 2)), dma((planes, 2)),
            dma((planes,)), dma((planes,)), dma((planes,)), dma((planes,)), dma((planes,)), dma((planes,)), dma((planes,)),
        ],
        compiler_params=pltpu.CompilerParams(collective_id=ident + 10 * layer, has_side_effects=True, vmem_limit_bytes=62 << 20),
        cost_estimate=pl.CostEstimate(
            flops=count * width, bytes_accessed=count, transcendentals=0
        ),
        name=name,
    )(own, *inputs)


def mlp_chunk(land, start, rows, in_refs, out_refs, work_refs):
    expand_w, down_w = in_refs
    gate_slope, up_slope, hidden_ref = out_refs
    span = pl.ds(start, rows)
    x = land[span]
    gate = dot(x, expand_w[0])
    up = dot(x, expand_w[1])
    sig = jax.nn.sigmoid(gate)
    silu = gate * sig
    hidden = (silu * up).astype(BF16)
    gate_slope[span] = (up * sig * (1.0 + gate * (1.0 - sig))).astype(BF16)
    up_slope[span] = silu.astype(BF16)
    hidden_ref[span] = hidden
    return dot(hidden, down_w[...])


def mlp_back_chunk(land, start, rows, in_refs, out_refs, work_refs):
    expand_w, down_w, gate_slope, up_slope = in_refs[:4]
    gate_ref, up_ref = work_refs
    span = pl.ds(start, rows)
    grad_hidden = dot(land[span], down_w[...], LAST)
    grad_gate = (grad_hidden * gate_slope[span].astype(F32)).astype(BF16)
    grad_up = (grad_hidden * up_slope[span].astype(F32)).astype(BF16)
    gate_ref[span] = grad_gate
    up_ref[span] = grad_up
    return dot(grad_gate, expand_w[0], LAST) + dot(grad_up, expand_w[1], LAST)


def mlp_back_piece(land, index, pieces, in_refs, out_refs, work_refs):
    normed, hidden = in_refs[4:]
    gate_ref, up_ref = work_refs
    d_expand, d_down = out_refs
    size = d_expand.shape[1] // pieces
    span = pl.ds(pl.multiple_of(index * size, size), size)
    rows = normed[:, span]
    d_expand[0, span] = dot(rows, gate_ref[...], ROWS).astype(BF16)
    d_expand[1, span] = dot(rows, up_ref[...], ROWS).astype(BF16)
    d_down[:, span] = dot(hidden[...], land[:, span], ROWS).astype(BF16)


def mlp_forward(own, expand, layer, down_w, planes):
    count = planes * 4 * own.shape[0]
    shape = jax.ShapeDtypeStruct((count, down_w.shape[0]), BF16)
    return spread(
        mlp_chunk,
        None,
        own,
        (expand, down_w),
        layer,
        (shape,) * 3,
        (),
        planes,
        1,
        "mlp_forward",
        layer == 0,
    )


def mlp_backward(own, expand, layer, down_w, gate_slope, up_slope, normed, hidden, planes):
    d_expand = jax.ShapeDtypeStruct(expand.shape[1:], BF16)
    reduce = jax.ShapeDtypeStruct(down_w.shape, BF16)
    work = pltpu.VMEM(gate_slope.shape, BF16)
    return spread(
        mlp_back_chunk,
        mlp_back_piece,
        own,
        (expand, down_w, gate_slope, up_slope, normed, hidden),
        layer,
        (d_expand, reduce),
        (work, work),
        planes,
        2,
        "mlp_backward",
    )[1:]


def feed_forward(own, expand_layer, down_w):
    planes = lax.axis_size("ctx") // 2
    if planes == 4:
        rows, total, *kept = mlp_forward(own, *expand_layer, down_w, planes)
        return rows, total if expand_layer[1] == 0 else scatter_tokens(total), *kept
    expand = expand_layer[0][expand_layer[1]]
    rows = gather_tokens(own)
    gate, up = dot(rows, expand[0]), dot(rows, expand[1])
    sig = jax.nn.sigmoid(gate)
    silu = gate * sig
    hidden = (silu * up).astype(BF16)
    gate_slope = (up * sig * (1.0 + gate * (1.0 - sig))).astype(BF16)
    total = scatter_tokens(dot(hidden, down_w).astype(BF16))
    return rows, total, gate_slope, silu.astype(BF16), hidden


def feed_backward(own, expand_layer, down_w, gate_slope, up_slope, normed, hidden):
    planes = lax.axis_size("ctx") // 2
    if planes == 4:
        return mlp_backward(
            own, *expand_layer, down_w, gate_slope, up_slope, normed, hidden, planes
        )
    expand = expand_layer[0][expand_layer[1]]
    rows = own if own.shape[0] == normed.shape[0] else gather_tokens(own)
    grad_hidden = dot(rows, down_w, LAST)
    grad_gate = (grad_hidden * gate_slope.astype(F32)).astype(BF16)
    grad_up = (grad_hidden * up_slope.astype(F32)).astype(BF16)
    part = dot(grad_gate, expand[0], LAST) + dot(grad_up, expand[1], LAST)
    return (
        scatter_tokens(part.astype(BF16)),
        jnp.stack([dot(normed, grad_gate, ROWS), dot(normed, grad_up, ROWS)]).astype(BF16),
        dot(hidden, rows, ROWS).astype(BF16),
    )


def greet_line(planes, plane, core):
    barrier = pltpu.get_barrier_semaphore()
    pl.semaphore_signal(
        barrier, inc=1, device_id={"ctx": plane * 2 + 1 - core}, device_id_type=MESH
    )
    for step in range(1, planes):
        there = (plane + step) % planes
        pl.semaphore_signal(
            barrier, inc=1, device_id={"ctx": there * 2 + core}, device_id_type=MESH
        )
    pl.semaphore_wait(barrier, planes)


def attend_kernel(planes, heads, with_job, *refs):
    mixed_ref, cosine_ref, sine_ref, qpos_ref, kpos_ref = refs[:5]
    if with_job:
        out_ref, low_ref, log_ref, all_ref, q_ref = refs[6:11]
        zs, zr, cs, cr = refs[12:16]
        start, stage, finish = share_job(2 * planes, refs[5], refs[11], *refs[16:])
    else:
        out_ref, low_ref, log_ref, all_ref, q_ref, zs, zr, cs, cr = refs[5:]
    ctx = lax.axis_index("ctx")
    plane, core = ctx // 2, ctx % 2
    batch, tokens = qpos_ref.shape[:2]
    head_dim = cosine_ref.shape[1]
    query_width = heads * head_dim
    factor = 1.0 / math.sqrt(head_dim)
    if with_job:
        greet_all(2 * planes, ctx)
    else:
        greet_line(planes, plane, core)
    core_peer = {"ctx": plane * 2 + 1 - core}

    def block(at):
        return all_ref.at[:, pl.ds(pl.multiple_of(at * tokens, tokens), tokens)]

    def along(there, source):
        ref = block(source * 2 + core)
        return remote(ref, ref, zs.at[there], zr.at[source], {"ctx": there * 2 + core})

    def beside(source, which):
        ref = block(source * 2 + which)
        return remote(ref, ref, cs.at[source], cr.at[source], core_peer)

    def turned(rows, span):
        values = mixed_ref[rows, span]
        return values * cosine_ref[rows] + pltpu.roll(values, head_dim // 2, 1) * sine_ref[rows]

    own = pl.ds(pl.multiple_of(ctx * tokens, tokens), tokens)
    for index in range(batch):
        rows = slice(index * tokens, (index + 1) * tokens)
        keys = turned(rows, slice(query_width, query_width + head_dim))
        all_ref[index, own, :head_dim] = keys.astype(BF16)
        all_ref[index, own, head_dim:] = mixed_ref[rows, query_width + head_dim :].astype(BF16)
    for step in range(1, planes):
        along((plane + step) % planes, plane).start()
    beside(plane, core).start()
    if with_job:
        start()
    for step in range(1, planes):
        source = (plane + step) % planes
        along(source, source).wait_recv()
        beside(source, core).start()
    for step in range(planes):
        beside((plane + step) % planes, 1 - core).wait_recv()

    def one(index, carry):
        rows = pl.ds(pl.multiple_of(index * tokens, tokens), tokens)
        keys = all_ref[index, :, :head_dim]
        values = all_ref[index, :, head_dim:]
        allowed = qpos_ref[index] >= kpos_ref[index]
        lane = lax.broadcasted_iota(jnp.int32, (tokens, head_dim), 1)
        logs = jnp.zeros((tokens, head_dim), F32)
        for head in range(heads):
            span = slice(head * head_dim, (head + 1) * head_dim)
            queries = turned(rows, span).astype(BF16)
            q_ref[rows, span] = queries
            scores = dot(queries, keys, LAST)
            scores = jnp.where(allowed, scores * factor, -1e30)
            top = jnp.max(scores, axis=1, keepdims=True)
            weights = jnp.exp(scores - top)
            total = jnp.sum(weights, axis=1, keepdims=True)
            logs = jnp.where(lane == head, top + jnp.log(total), logs)
            out = dot((weights * (1.0 / total)).astype(BF16), values)
            out_ref[rows, span] = out
            low_ref[rows, span] = out.astype(BF16)
        log_ref[rows] = logs
        return carry

    if with_job:
        stages = 2 * planes - 1
        for index in range(batch):
            stage(index)
            one(index, 0)
        for index in range(batch, stages):
            stage(index)
        finish()
    else:
        lax.fori_loop(0, batch, one, 0)
    for step in range(1, planes):
        along((plane + step) % planes, plane).wait_send()
        beside((plane + step) % planes, core).wait_send()
    beside(plane, core).wait_send()


def attend_back_kernel(
    planes, heads, q_ref, kv_ref, qpos_ref, kpos_ref, grad_ref, out_ref, log_ref, cosine_ref,
    sine_ref, mixed_ref, dkv_ref, whole, core_out, core_in, z_out, z_in, cs, cr, zs, zr,
):
    ctx = lax.axis_index("ctx")
    plane, core = ctx // 2, ctx % 2
    batch = qpos_ref.shape[0]
    tokens = q_ref.shape[0] // batch
    head_dim = kv_ref.shape[2] // 2
    factor = 1.0 / math.sqrt(head_dim)
    greet_line(planes, plane, core)
    core_peer = {"ctx": plane * 2 + 1 - core}

    def turned_back(grads, rows):
        rolled = pltpu.roll(grads, head_dim // 2, 1)
        return (grads * cosine_ref[rows] - rolled * sine_ref[rows]).astype(BF16)

    def to_core(index):
        return remote(core_out.at[index], core_in.at[index], cs.at[index], cr.at[index], core_peer)

    def to_plane(index, there, source):
        return remote(
            z_out.at[index, there],
            z_in.at[index, source],
            zs.at[index, there],
            zr.at[index, source],
            {"ctx": there * 2 + core},
        )

    def one(index, carry):
        rows = pl.ds(pl.multiple_of(index * tokens, tokens), tokens)
        keys = kv_ref[index, :, :head_dim]
        values = kv_ref[index, :, head_dim:]
        allowed = qpos_ref[index] >= kpos_ref[index]
        logs = log_ref[rows]
        for head in range(heads):
            span = slice(head * head_dim, (head + 1) * head_dim)
            queries = q_ref[rows, span]
            grads = grad_ref[rows, span]
            delta = jnp.sum(grads.astype(F32) * out_ref[rows, span], axis=1, keepdims=True)
            scores = jnp.where(allowed, dot(queries, keys, LAST) * factor, -1e30)
            weights = jnp.exp(scores - logs[:, head : head + 1])
            grad_scores = (weights * (dot(grads, values, LAST) - delta) * factor).astype(BF16)
            mixed_ref[rows, span] = turned_back(dot(grad_scores, keys), rows)
            grad_keys = dot(grad_scores, queries, ROWS)
            grad_values = dot(weights.astype(BF16), grads, ROWS)
            if head == 0:
                whole[index, :, :head_dim] = grad_keys
                whole[index, :, head_dim:] = grad_values
            else:
                whole[index, :, :head_dim] += grad_keys
                whole[index, :, head_dim:] += grad_values

        for at in range(planes):
            theirs = pl.multiple_of((at * 2 + 1 - core) * tokens, tokens)
            core_out[index, at] = whole[index, pl.ds(theirs, tokens)].astype(BF16)
        to_core(index).start()
        return carry

    lax.fori_loop(0, batch, one, 0)

    def mine(index, at):
        start = pl.multiple_of((at * 2 + core) * tokens, tokens)
        return whole[index, pl.ds(start, tokens)] + core_in[index, at].astype(F32)

    for index in range(batch):
        to_core(index).wait_recv()
        for step in range(1, planes):
            there = (plane + step) % planes
            z_out[index, there] = mine(index, there).astype(BF16)
            to_plane(index, there, plane).start()
        dkv_ref[index] = mine(index, plane)
    for index in range(batch):
        for step in range(1, planes):
            source = (plane + step) % planes
            to_plane(index, source, source).wait_recv()
            dkv_ref[index] += z_in[index, source].astype(F32)
        rows = slice(index * tokens, (index + 1) * tokens)
        width = heads * head_dim
        mixed_ref[rows, width : width + head_dim] = turned_back(dkv_ref[index, :, :head_dim], rows)
        mixed_ref[rows, width + head_dim :] = dkv_ref[index, :, head_dim:].astype(BF16)
    for index in range(batch):
        to_core(index).wait_send()
        for step in range(1, planes):
            to_plane(index, (plane + step) % planes, plane).wait_send()


def attend(mixed, tables, heads, blocks):
    cosine, sine, query_pos, key_pos, _ = tables
    batch, tokens = query_pos.shape
    head_dim = cosine.shape[1]
    query_width = heads * head_dim
    pair = 2 * head_dim
    planes = lax.axis_size("ctx") // 2
    keys = key_pos.shape[1]
    rows = batch * tokens
    if planes != 4:
        queries = rotate(
            mixed[:, :query_width].reshape(rows, heads, head_dim),
            cosine[:, None, :],
            sine[:, None, :],
        ).astype(BF16).reshape(rows, query_width)
        own_keys = rotate(mixed[:, query_width : query_width + head_dim], cosine, sine)
        kv = jnp.concatenate([own_keys, mixed[:, query_width + head_dim :]], axis=1).astype(BF16)
        kv_all = gather_ctx(kv.reshape(batch, tokens, pair), 1)
        split = queries.reshape(batch, tokens, heads, head_dim)
        scores = jnp.einsum(
            "bqhd,bkd->bqhk", split, kv_all[..., :head_dim], preferred_element_type=F32
        )
        allowed = query_pos[:, :, None, None] >= key_pos[:, None, None, :]
        scores = jnp.where(allowed, scores / math.sqrt(head_dim), -1e30)
        logs = jax.nn.logsumexp(scores, axis=-1)
        probs = jnp.exp(scores - logs[..., None]).astype(BF16)
        out = jnp.einsum(
            "bqhk,bkd->bqhd", probs, kv_all[..., head_dim:], preferred_element_type=F32
        ).reshape(queries.shape)
        shared = [share(part) for part in blocks]
        return out, out.astype(BF16), logs, kv_all, queries, *shared
    size = 2 * planes
    shape = jax.ShapeDtypeStruct
    dma = pltpu.SemaphoreType.DMA
    return pl.pallas_call(
        functools.partial(attend_kernel, planes, heads, len(blocks) > 0),
        out_shape=[
            shape((rows, query_width), F32),
            shape((rows, query_width), BF16),
            shape((rows, head_dim), F32),
            shape((batch, keys, pair), BF16),
            shape((rows, query_width), BF16),
        ]
        + [shape((2,) + part.shape, part.dtype) for part in blocks],
        in_specs=[VMEM] * 5 + [HBM] * len(blocks),
        out_specs=[VMEM] * 5 + [HBM] * len(blocks),
        scratch_shapes=[dma((planes,)), dma((planes,)), dma((planes,)), dma((planes,))]
        + ([dma((size,))] * 4 + [dma]) * len(blocks),
        compiler_params=pltpu.CompilerParams(
            collective_id=3 + 2 * len(blocks), has_side_effects=True, vmem_limit_bytes=48 << 20
        ),
        cost_estimate=pl.CostEstimate(
            flops=rows * keys, bytes_accessed=rows, transcendentals=0
        ),
        name="attend",
    )(mixed, cosine, signed(sine), query_pos[:, :, None], key_pos[:, None, :], *blocks)


def signed(sine):
    half = sine.shape[1] // 2
    return jnp.concatenate([-sine[:, :half], sine[:, half:]], axis=1)


def attend_backward(queries, kv_all, tables, grads, out, logs):
    cosine, sine, query_pos, key_pos, _ = tables
    batch, keys, pair = kv_all.shape
    head_dim = pair // 2
    heads = queries.shape[1] // head_dim
    rows = queries.shape[0]
    tokens = rows // batch
    planes = lax.axis_size("ctx") // 2
    if planes != 4:
        factor = 1.0 / math.sqrt(head_dim)
        k_all, v_all = kv_all[..., :head_dim], kv_all[..., head_dim:]
        split = queries.reshape(batch, tokens, heads, head_dim)
        grad_split = grads.reshape(split.shape)
        delta = jnp.sum(grad_split.astype(F32) * out.reshape(split.shape), axis=-1)
        scores = jnp.einsum("bqhd,bkd->bqhk", split, k_all, preferred_element_type=F32)
        allowed = query_pos[:, :, None, None] >= key_pos[:, None, None, :]
        scores = jnp.where(allowed, scores * factor, -1e30)
        probs = jnp.exp(scores - logs[..., None])
        grad_probs = jnp.einsum("bqhd,bkd->bqhk", grad_split, v_all, preferred_element_type=F32)
        grad_scores = (probs * (grad_probs - delta[..., None]) * factor).astype(BF16)
        dq = jnp.einsum("bqhk,bkd->bqhd", grad_scores, k_all, preferred_element_type=F32)
        dk = jnp.einsum("bqhk,bqhd->bkd", grad_scores, split, preferred_element_type=F32)
        dv = jnp.einsum(
            "bqhk,bqhd->bkd", probs.astype(BF16), grad_split, preferred_element_type=F32
        )
        dkv = lax.psum_scatter(
            jnp.concatenate([dk, dv], axis=-1).astype(BF16), "ctx", scatter_dimension=1, tiled=True
        )
        dkv = dkv.astype(F32).reshape(rows, pair)
        dq = unrotate(dq.reshape(rows, heads, head_dim), cosine[:, None, :], sine[:, None, :])
        dk = unrotate(dkv[:, :head_dim], cosine, sine)
        parts = [dq.reshape(queries.shape), dk, dkv[:, head_dim:]]
        return jnp.concatenate(parts, axis=1).astype(BF16)
    shape = jax.ShapeDtypeStruct
    dma = pltpu.SemaphoreType.DMA
    return pl.pallas_call(
        functools.partial(attend_back_kernel, planes, heads),
        out_shape=shape((rows, queries.shape[1] + pair), BF16),
        in_specs=[VMEM] * 9,
        out_specs=VMEM,
        scratch_shapes=[
            pltpu.VMEM((batch, tokens, pair), F32),
            pltpu.VMEM((batch, keys, pair), F32),
            pltpu.VMEM((batch, planes, tokens, pair), BF16),
            pltpu.VMEM((batch, planes, tokens, pair), BF16),
            pltpu.VMEM((batch, planes, tokens, pair), BF16),
            pltpu.VMEM((batch, planes, tokens, pair), BF16),
            dma((batch,)), dma((batch,)), dma((batch, planes)), dma((batch, planes)),
        ],
        compiler_params=pltpu.CompilerParams(
            collective_id=4, has_side_effects=True, vmem_limit_bytes=48 << 20
        ),
        cost_estimate=pl.CostEstimate(
            flops=rows * keys, bytes_accessed=rows, transcendentals=0
        ),
        name="attend_backward",
    )(
        queries,
        kv_all,
        query_pos[:, :, None],
        key_pos[:, None, :],
        grads,
        out,
        logs,
        cosine,
        signed(sine),
    )


def layer_forward(x_low, weights, tables, blocks, sooner, later):
    gain_attn, w_mixed, bias, w_project, gain_mlp, w_expand, w_reduce = weights
    cosine, sine, query_pos, key_pos, mine = tables
    count, width = x_low.shape
    query_width = w_project.shape[0]
    head_dim = (w_mixed.shape[1] - query_width) // 2
    heads = query_width // head_dim
    batch = query_pos.shape[0]
    tokens = count // batch
    x = x_low.astype(F32)
    root_attn = inverse_root(x)
    normed = (x * root_attn * gain_attn).astype(BF16)
    mixed = dot(normed, w_mixed) + bias
    mixed, sooner = lax.optimization_barrier((mixed, sooner))
    attended_full, attended, log_total, kv, queries, *shared = attend(
        mixed, tables, heads, blocks
    )
    if shared:
        w_expand = (shared[0].reshape((2, 2, width, -1)), 0)
    x_mine = lax.dynamic_slice_in_dim(x, mine * tokens, tokens, 0)
    middle = x_mine + tensor_scatter(dot(attended, w_project))
    root_mlp = inverse_root(middle)
    normed_mlp = (middle * root_mlp * gain_mlp).astype(BF16)
    normed_mlp, later = lax.optimization_barrier((normed_mlp, later))
    all_normed, branch, gate_slope, up_slope, hidden = feed_forward(
        normed_mlp, w_expand, w_reduce
    )
    result = middle + branch
    kept = (
        x_mine,
        lax.dynamic_slice_in_dim(root_attn, mine * tokens, tokens, 0),
        normed,
        queries,
        kv,
        attended_full,
        log_total,
        attended,
        middle,
        root_mlp,
        all_normed,
        gate_slope,
        up_slope,
        hidden,
    )
    return result.astype(BF16), kept, w_expand, sooner, later


def layer_backward(grad_out, grad_rows, kept, weights, tables, route, earlier, pinned):
    gain_attn, w_mixed, bias, w_project, gain_mlp, w_expand, w_reduce = weights
    cosine, sine, query_pos, key_pos, mine = tables
    (
        x_mine,
        root_attn,
        normed,
        queries,
        kv,
        attended_full,
        log_total,
        attended,
        middle,
        root_mlp,
        all_normed,
        gate_slope,
        up_slope,
        hidden,
    ) = kept
    count, query_width = queries.shape
    head_dim = (w_mixed.shape[1] - query_width) // 2
    heads = query_width // head_dim
    grad_normed_mlp, d_expand, d_reduce = feed_backward(
        grad_rows,
        w_expand,
        w_reduce,
        gate_slope,
        up_slope,
        all_normed,
        hidden,
    )
    grad_normed_mlp, earlier = lax.optimization_barrier((grad_normed_mlp, earlier))
    moved_reduce = lax.ppermute(d_reduce, "section", route)
    grad_middle, d_gain_mlp = norm_backward(middle, root_mlp, gain_mlp, grad_normed_mlp)
    grad_middle = grad_middle + grad_out
    grad_branch = tensor_pair(grad_middle.astype(BF16))
    d_project = dot(attended, grad_branch, ROWS)
    grad_attended = dot(grad_branch, w_project, LAST).astype(BF16)
    grad_mixed = attend_backward(
        queries, kv, tables, grad_attended, attended_full, log_total
    )
    grad_mixed, moved_reduce, pinned = lax.optimization_barrier(
        (grad_mixed, moved_reduce, pinned)
    )
    d_mixed = dot(normed, grad_mixed, ROWS)
    d_bias = jnp.sum(grad_mixed.astype(F32), axis=0)
    grad_normed = tensor_scatter(dot(grad_mixed, w_mixed, LAST))
    grad_x, d_gain_attn = norm_backward(x_mine, root_attn, gain_attn, grad_normed)
    grad_x = (grad_x + grad_middle).astype(BF16)
    vectors = (d_gain_attn, d_mixed, d_bias, d_project, d_gain_mlp)
    return grad_x, vectors, d_expand, (d_reduce, moved_reduce), earlier, pinned


def shards(
    block_input, positions, cotangent, norm_attn, w_qkv, b_qkv, w_out, norm_mlp, w_gate_up, w_down
):
    section = lax.axis_index("section")
    tensor = lax.axis_index("tensor")
    ctx = lax.axis_index("ctx")
    ctx_size = lax.axis_size("ctx")
    first = section == 0
    micro, tokens, width = block_input.shape
    half = micro // 2
    head_dim = w_qkv.shape[3] - w_out.shape[2] * ctx_size
    head_dim = head_dim // 2
    slice_width = norm_attn.shape[1]
    slice_bias = b_qkv.shape[2]
    units = w_down.shape[1]

    def plane_part(value):
        return lax.dynamic_slice_in_dim(value, section * half, half, 0)

    def layers(own, other):
        return jnp.where(first, own, other), jnp.where(first, other, own)

    x = plane_part(block_input).reshape(half * tokens, width)
    pos_local = plane_part(positions)
    cosine, sine = angles(pos_local.reshape(-1), head_dim)

    small = jnp.concatenate([norm_attn[0], norm_mlp[0], b_qkv[0, 0]])
    qkv, out = w_qkv[0, :, 0, :], w_out[0, 0]
    vectors = jnp.concatenate(layers(small, swap(small)))
    places = jnp.concatenate([pos_local // 64, pos_local % 64]).reshape(-1).astype(BF16)
    packed = gather_ctx(jnp.concatenate([vectors, places])[None], 0)
    places = packed[:, vectors.shape[0] :].astype(jnp.int32).reshape(ctx_size, 2, half, tokens)
    pos_all = jnp.swapaxes(places[:, 0] * 64 + places[:, 1], 0, 1).reshape(half, -1)
    tables = (cosine, sine, pos_local, pos_all, tensor)
    small_size = 2 * slice_width + slice_bias
    small0, small1 = packed[:, :small_size], packed[:, small_size : 2 * small_size]
    qkv0, qkv1 = layers(qkv, swap(qkv))
    out0, out1 = layers(out, swap(out))
    down_moved = swap(w_down[0])
    down0, down1 = layers(w_down[0], down_moved)
    expand = w_gate_up[0].reshape(slice_width, 2, ctx_size, units)
    blocks = jnp.transpose(expand, (1, 2, 0, 3))

    def whole(small, qkv, out, expand, down):
        return (
            small[:, :slice_width].reshape(1, width),
            gather_ctx(qkv, 0),
            small[:, 2 * slice_width :].reshape(1, slice_bias * ctx_size),
            gather_ctx(out, 0),
            small[:, slice_width : 2 * slice_width].reshape(1, width),
            expand,
            down,
        )

    weights0 = whole(small0, qkv0, out0, None, down0)

    result0, kept0, expand0, down_moved, (qkv1, out1) = layer_forward(
        x, weights0, tables, (blocks,), down_moved, (qkv1, out1)
    )
    weights0 = weights0[:5] + (expand0, down0)
    weights1 = whole(small1, qkv1, out1, (expand0[0], 1), down1)
    x1 = tensor_pair(result0)
    seeds, x1 = lax.optimization_barrier((plane_part(cotangent), x1))
    seed_rows = gather_ctx(seeds.reshape(half * tokens, width), 0)
    result1, kept1, *_ = layer_forward(x1, weights1, tables, (), (), ())
    out1_all = tensor_pair(result1)

    def exchange(layer0, layer1):
        kept_here = jnp.where(first, layer0, layer1)
        received = swap(jnp.where(first, layer1, layer0))
        low = jnp.where(first, kept_here, received)
        high = jnp.where(first, received, kept_here)
        both = jnp.concatenate([low, high], axis=0)
        return both.reshape(1, micro, tokens, width)

    seed = lax.dynamic_slice_in_dim(seeds, tensor, 1, 0)[0].astype(F32)
    def ctx_scatter(value):
        return lax.psum_scatter(
            value.astype(BF16), "ctx", scatter_dimension=0, tiled=True
        )

    group = w_qkv.shape[3]
    split_at = group - head_dim

    def with_vectors(grads):
        gain_attn, mixed, bias, project, gain_mlp = grads[:5]
        rows = jnp.concatenate(
            [
                bias[:split_at].reshape(ctx_size, -1),
                bias[split_at:].reshape(ctx_size, -1),
                gain_attn.reshape(ctx_size, slice_width),
                gain_mlp.reshape(ctx_size, slice_width),
            ],
            axis=1,
        )
        rows = jnp.pad(rows[:, None, :], ((0, 0), (0, 15), (0, group - rows.shape[1])))
        mixed = mixed.reshape(ctx_size, slice_width, group)
        both = jnp.concatenate([mixed.astype(BF16), rows.astype(BF16)], axis=1)
        return both.reshape(ctx_size * (slice_width + 16), group)

    grad1, d1, d_expand1, d_reduce1, _, out1_all = layer_backward(
        seed, seed_rows, kept1, weights1, tables, [(0, 1)], (), out1_all
    )
    section_output = exchange(x1, out1_all)
    slices1 = (ctx_scatter(with_vectors(d1)), ctx_scatter(d1[3]))
    grad1_all = tensor_pair(grad1)
    grad0, d0, d_expand0, d_reduce0, earlier, _ = layer_backward(
        grad1.astype(F32), grad1, kept0, weights0, tables, [(1, 0)], slices1 + (section_output, grad1_all), ()
    )
    slices1, (section_output, grad1_all) = earlier[:2], earlier[2:]

    def to_owner(part0, part1):
        received0 = lax.ppermute(part0.astype(BF16), "section", [(1, 0)])
        received1 = lax.ppermute(part1.astype(BF16), "section", [(0, 1)])
        own = jnp.where(first, part0, part1).astype(F32)
        return own + jnp.where(first, received0, received1).astype(F32)

    def of_owner(pair0, pair1):
        own, received = (jnp.where(first, low, high).astype(F32) for low, high in zip(pair0, pair1))
        return own + received

    blocks = (2, ctx_size, slice_width, units)
    grad0_all = tensor_pair(grad0)
    grad0_all, d_expand0 = lax.optimization_barrier((grad0_all, d_expand0))
    input_grad = exchange(grad0_all, grad1_all)
    total = collect(d_expand0.reshape(blocks), d_expand1.reshape(blocks), first)
    d_expand = lax.optimization_barrier(jnp.transpose(total, (2, 0, 1, 3)))
    d_expand = lax.optimization_barrier(d_expand.reshape(1, slice_width, 2, ctx_size * units))
    d_expand = d_expand.astype(F32)
    d_reduce = of_owner(d_reduce0, d_reduce1)

    d_mixed = to_owner(ctx_scatter(with_vectors(d0)), slices1[0])
    d_project = to_owner(ctx_scatter(d0[3]), slices1[1])
    vectors = d_mixed[slice_width]
    d_mixed = d_mixed[:slice_width]
    count_qk, count_v = split_at // ctx_size, head_dim // ctx_size
    bias_qk = vectors[:count_qk][None]
    bias_v = vectors[count_qk : count_qk + count_v][None]
    start = count_qk + count_v
    gains = vectors[start : start + 2 * slice_width].reshape(1, 2 * slice_width)
    gains = gains + lax.ppermute(gains, "tensor", SWAP)
    return (
        section_output,
        input_grad,
        gains[:, :slice_width],
        d_mixed[None, :, None, :],
        bias_qk[None],
        bias_v[None],
        d_project[None, None],
        gains[:, slice_width:],
        d_expand,
        d_reduce[None],
    )


def solution(mesh):
    in_specs = (
        P(None, "ctx", None),
        P(None, "ctx"),
        P(None, "ctx", None),
        P("section", "ctx"),
        P("section", "ctx", "tensor", None),
        P("section", "tensor", "ctx"),
        P("section", "tensor", "ctx", None),
        P("section", "ctx"),
        P("section", "ctx", None, "tensor"),
        P("section", ("tensor", "ctx"), None),
    )
    out_specs = (
        P("section", None, "ctx", None),
        P("section", None, "ctx", None),
        P("section", "ctx"),
        P("section", "ctx", "tensor", None),
        P("section", "tensor", "ctx"),
        P("section", "tensor", "ctx"),
        P("section", "tensor", "ctx", None),
        P("section", "ctx"),
        P("section", "ctx", None, "tensor"),
        P("section", ("tensor", "ctx"), None),
    )
    return jax.shard_map(shards, mesh=mesh, in_specs=in_specs, out_specs=out_specs, check_vma=False)
```

```python
import functools
import functools
import math

import jax
import jax.numpy as jnp
from jax import lax
from jax.experimental import pallas as pl
from jax.experimental.pallas import tpu as pltpu
from jax.sharding import PartitionSpec as P

EPSILON = 1e-06
ROPE_BASE = 1000000.0
ROWS = (((0,), (0,)), ((), ()))
LAST = (((1,), (1,)), ((), ()))
F32 = jnp.float32
BF16 = jnp.bfloat16
SWAP = [(0, 1), (1, 0)]
MESH = pl.DeviceIdType.MESH
VMEM = pl.BlockSpec(memory_space=pltpu.VMEM)
HBM = pl.BlockSpec(memory_space=pl.ANY)


def dot(a, b, dims=(((1,), (0,)), ((), ()))):
    return lax.dot_general(a, b, dims, preferred_element_type=F32)


def angles(positions, head_dim):
    half_dim = head_dim // 2
    frequency = ROPE_BASE ** (-(jnp.arange(half_dim, dtype=F32) * 2.0) / head_dim)
    phases = positions.astype(F32)[:, None] * frequency[None, :]
    phases = jnp.concatenate([phases, phases], axis=-1)
    return jnp.cos(phases), jnp.sin(phases)


def rotate(values, cosine, sine):
    half = values.shape[-1] // 2
    turned = jnp.concatenate([-values[..., half:], values[..., :half]], axis=-1)
    return values * cosine + turned * sine


def unrotate(grads, cosine, sine):
    half = grads.shape[-1] // 2
    twisted = grads * sine
    turned = jnp.concatenate([twisted[..., half:], -twisted[..., :half]], axis=-1)
    return grads * cosine + turned


def inverse_root(values):
    return lax.rsqrt(jnp.mean(values * values, axis=-1, keepdims=True) + EPSILON)


def norm_backward(values, root, gain, grad_normed):
    normal = values * root
    gain_grad = jnp.sum(grad_normed * normal, axis=0)
    scaled = grad_normed * gain
    mean = jnp.mean(scaled * normal, axis=-1, keepdims=True)
    return root * (scaled - normal * mean), gain_grad


def swap(value):
    return lax.ppermute(value, "section", SWAP)


def gather_ctx(value, axis):
    return lax.all_gather(value, "ctx", axis=axis, tiled=True)


def gather_tokens(rows):
    return lax.all_gather(rows, ("ctx", "tensor"), axis=0, tiled=True)


def scatter_tokens(rows):
    return lax.psum_scatter(rows, ("ctx", "tensor"), scatter_dimension=0, tiled=True).astype(F32)


def tensor_gather(rows):
    return lax.all_gather(rows, "tensor", axis=0, tiled=True)


def tensor_pair(rows):
    received = lax.ppermute(rows, "tensor", SWAP)
    mine = lax.axis_index("tensor") == 0
    return jnp.concatenate([jnp.where(mine, rows, received), jnp.where(mine, received, rows)])


def tensor_scatter(rows):
    mine = lax.axis_index("tensor")
    tokens = rows.shape[0] // 2
    own = lax.dynamic_slice_in_dim(rows, mine * tokens, tokens, 0)
    other = lax.dynamic_slice_in_dim(rows, (1 - mine) * tokens, tokens, 0)
    return own + lax.ppermute(other.astype(BF16), "tensor", SWAP).astype(F32)


def greet_all(size, me):
    barrier = pltpu.get_barrier_semaphore()
    for step in range(1, size):
        pl.semaphore_signal(
            barrier, inc=1, device_id={"ctx": (me + step) % size}, device_id_type=MESH
        )
    there = 1 - lax.axis_index("section")
    pl.semaphore_signal(barrier, inc=1, device_id={"section": there}, device_id_type=MESH)
    pl.semaphore_wait(barrier, size)


def by_distance(size):
    return sorted(range(size), key=lambda step: min(step, size - step))


def share_job(size, from_ref, all_ref, send, recv, over_send, over_recv, local):
    me = lax.axis_index("ctx")
    section = lax.axis_index("section")
    order = by_distance(size)[1:]

    def copy(there, source):
        return remote(
            from_ref.at[:, there],
            all_ref.at[section, :, source],
            send.at[there],
            recv.at[source],
            {"ctx": there},
        )

    def over(block, source):
        return remote(
            block,
            all_ref.at[section, :, source],
            over_send.at[source],
            over_recv.at[source],
            {"section": 1 - section},
        )

    def own():
        return pltpu.make_async_copy(from_ref.at[:, me], all_ref.at[section, :, me], local)

    def start():
        own().start()
        over(from_ref.at[:, me], me).start()
        for step in order[:2]:
            copy((me + step) % size, me).start()

    def stage(index):
        step = order[index]
        source = (me + size - step) % size
        copy(source, source).wait_recv()
        over(all_ref.at[section, :, source], source).start()
        copy((me + step) % size, me).wait_send()
        if index + 2 < len(order):
            copy((me + order[index + 2]) % size, me).start()

    def finish():
        own().wait()
        for step in range(size):
            source = (me + step) % size
            over(all_ref.at[section, :, source], source).wait()

    return start, stage, finish


def share(blocks):
    moved = lax.all_to_all(blocks, "ctx", split_axis=1, concat_axis=1, tiled=True)
    return lax.all_gather(moved, "section")


def collect_kernel(
    size, first_ref, second_ref, to_ref, own, other, send, recv, over_send, over_recv, local, store
):
    me = lax.axis_index("ctx")
    section = lax.axis_index("section")
    greet_all(size, me)
    order = by_distance(size)[::-1]

    def over(source_ref, at):
        return remote(
            source_ref.at[:, at], other.at[at], over_send.at[at], over_recv.at[at],
            {"section": 1 - section},
        )

    def load(source_ref, at):
        return pltpu.make_async_copy(source_ref.at[:, at], own.at[at], local.at[at])

    def copy(there, source):
        return remote(
            own.at[there], to_ref.at[:, source], send.at[there], recv.at[source], {"ctx": there}
        )

    def start(at):
        @pl.when(section == 0)
        def _():
            over(second_ref, at).start()
            load(first_ref, at).start()

        @pl.when(section == 1)
        def _():
            over(first_ref, at).start()
            load(second_ref, at).start()

    for index, step in enumerate(order):
        at = (me + step) % size
        if index == 0:
            start(at)
        if index + 1 < size:
            start((me + order[index + 1]) % size)
        over(first_ref, at).wait()
        load(first_ref, at).wait()
        own[at] = (own[at].astype(F32) + other[at].astype(F32)).astype(own.dtype)
        if step > 0:
            copy(at, me).start()
        else:
            mine = pltpu.make_async_copy(own.at[at], to_ref.at[:, me], store)
            mine.start()
            mine.wait()
    for step in order:
        at = (me + step) % size
        if step > 0:
            copy(at, at).wait_recv()
            copy(at, me).wait_send()


def collect(first, second, is_first):
    parts, size, rows, columns = first.shape
    if size != 8:
        received = lax.ppermute(jnp.where(is_first, second, first), "section", SWAP)
        total = jnp.where(is_first, first, second).astype(F32) + received.astype(F32)
        return lax.all_to_all(
            total.astype(BF16), "ctx", split_axis=1, concat_axis=1, tiled=True
        )
    dma = pltpu.SemaphoreType.DMA
    block = pltpu.VMEM((size, parts, rows, columns), first.dtype)
    return pl.pallas_call(
        functools.partial(collect_kernel, size),
        out_shape=jax.ShapeDtypeStruct(first.shape, first.dtype),
        in_specs=[HBM, HBM],
        out_specs=HBM,
        scratch_shapes=[block, block]
        + [dma((size,)), dma((size,)), dma((size,)), dma((size,)), dma((size,)), dma],
        compiler_params=pltpu.CompilerParams(
            collective_id=6, has_side_effects=True, vmem_limit_bytes=24 << 20
        ),
        cost_estimate=pl.CostEstimate(flops=first.size, bytes_accessed=1024, transcendentals=0),
        name="collect",
    )(first, second)


def remote(src, dst, send, recv, device):
    return pltpu.make_async_remote_copy(
        src_ref=src, dst_ref=dst, send_sem=send, recv_sem=recv, device_id=device, device_id_type=MESH
    )


def spread_kernel(
    chunk, piece, layer, planes, gathered, reduced, ins, outs, extra, own_ref, *refs
):
    in_refs, refs = refs[:ins], refs[ins:]
    all_ref, sum_ref = refs[:2]
    out_refs, refs = refs[2 : 2 + outs], refs[2 + outs :]
    work_refs, refs = refs[:extra], refs[extra:]
    (expand_w, load_sem), refs = refs[:2], refs[2:]
    load = pltpu.make_async_copy(in_refs[0].at[layer], expand_w, load_sem)
    load.start()
    in_refs = (expand_w,) + in_refs[1:]
    (land, core_out, core_in, y_out, y_in, z_out, z_in, both, kept,
     zs, zr, ys, yr, cs, cr, rcs, rcr, rys, ryr, rzs, rzr, local) = refs
    tensor = lax.axis_index("tensor")
    ctx = lax.axis_index("ctx")
    plane, core = ctx // 2, ctx % 2
    rows = own_ref.shape[0] // (4 * planes if gathered else 1)
    y_peer = {"tensor": 1 - tensor}
    core_peer = {"ctx": plane * 2 + 1 - core}

    barrier = pltpu.get_barrier_semaphore()
    pl.semaphore_signal(barrier, inc=1, device_id=y_peer, device_id_type=MESH)
    pl.semaphore_signal(barrier, inc=1, device_id=core_peer, device_id_type=MESH)
    for step in range(1, planes):
        there = (plane + step) % planes
        pl.semaphore_signal(barrier, inc=1, device_id={"ctx": there * 2 + core}, device_id_type=MESH)
    pl.semaphore_wait(barrier, planes + 1)

    def block(at, which_core, which_tensor):
        start = pl.multiple_of(((at * 2 + which_core) * 2 + which_tensor) * rows, rows)
        return land.at[pl.ds(start, rows)]

    def along(at, target, direction):
        ref = block(at, core, tensor)
        return remote(ref, ref, zs.at[at, direction], zr.at[at], {"ctx": target * 2 + core})

    def across(at, which_tensor):
        ref = block(at, core, which_tensor)
        return remote(ref, ref, ys.at[at], yr.at[at], y_peer)

    def beside(at, which_core, which_tensor, slot):
        ref = block(at, which_core, which_tensor)
        return remote(ref, ref, cs.at[at, slot], cr.at[at, slot], core_peer)

    if not gathered:
        start = pl.multiple_of(((plane * 2 + core) * 2 + tensor) * rows, rows)
        land[pl.ds(start, rows)] = own_ref[...]

        @pl.when(plane < planes - 1)
        def _():
            along(plane, plane + 1, 0).start()

        @pl.when(plane > 0)
        def _():
            along(plane, plane - 1, 1).start()

        across(plane, tensor).start()
        beside(plane, core, tensor, 0).start()

    def reduce_core(at):
        return remote(core_out.at[at], core_in.at[at], rcs.at[at], rcr.at[at], core_peer)

    def reduce_y(at):
        return remote(y_out.at[at], y_in.at[at], rys.at[at], ryr.at[at], y_peer)

    def reduce_z(at):
        return remote(z_out.at[at], z_in.at[plane], rzs.at[at], rzr.at[plane], {"ctx": at * 2 + core})

    def reduced_z(at):
        return remote(z_out.at[at], z_in.at[at], rzs.at[at], rzr.at[at], {"ctx": at * 2 + core})

    def save(at):
        span = pl.ds(pl.multiple_of(at * 4 * rows, 4 * rows), 4 * rows)
        return pltpu.make_async_copy(land.at[span], all_ref.at[span], local.at[at])

    def side_plane(distance, side):
        return plane + distance * (2 * side - 1)

    def inside(at):
        return jnp.logical_and(at >= 0, at < planes)

    def pass_on(distance, side):
        at = side_plane(distance, side)
        target = plane + 1 - 2 * side

        @pl.when(inside(at))
        def _():
            along(at, plane, 0).wait_recv()

            @pl.when(inside(target))
            def _():
                along(at, target, side).start()

            across(at, tensor).start()
            beside(at, core, tensor, 0).start()

    def pass_beside(distance, side):
        at = side_plane(distance, side)

        @pl.when(inside(at))
        def _():
            across(at, 1 - tensor).wait_recv()
            beside(at, core, 1 - tensor, 1).start()

    def fetch(at):
        span = pl.ds(pl.multiple_of(at * 4 * rows, 4 * rows), 4 * rows)
        return pltpu.make_async_copy(own_ref.at[span], land.at[span], local.at[at])

    if gathered:
        for at in range(planes):
            fetch(at).start()

    def step(index, carry):
        if gathered:
            index = 2 * planes - 2 - index
        distance = (index + 1) // 2
        at = side_plane(distance, 1 - index % 2)

        if not gathered:

            @pl.when(jnp.logical_or(index == 0, index % 2 == 1))
            def _():
                pass_on(distance + 1, 0)
                pass_on(distance + 1, 1)

                @pl.when(distance > 0)
                def _():
                    pass_beside(distance, 0)

                pass_beside(distance, 1)

        @pl.when(inside(at))
        def _():
            if gathered:
                fetch(at).wait()
            else:
                beside(at, 1 - core, tensor, 0).wait_recv()
                beside(at, 1 - core, 1 - tensor, 1).wait_recv()
            if piece is None:
                save(at).start()
            theirs = pl.multiple_of((at * 2 + 1 - core) * 2 * rows, 2 * rows)
            mine = pl.multiple_of((at * 2 + core) * 2 * rows, 2 * rows)
            if not reduced:
                for start in (theirs, mine):
                    part = chunk(land, start, 2 * rows, in_refs, out_refs, work_refs)
                    sum_ref[pl.ds(start, 2 * rows)] = part.astype(BF16)
                return
            core_out[at] = chunk(land, theirs, 2 * rows, in_refs, out_refs, work_refs).astype(BF16)
            reduce_core(at).start()
            both[...] = chunk(land, mine, 2 * rows, in_refs, out_refs, work_refs)
            reduce_core(at).wait_recv()
            both[...] += core_in[at].astype(F32)
            other = pl.multiple_of((1 - tensor) * rows, rows)
            own = pl.multiple_of(tensor * rows, rows)
            y_out[at] = both[pl.ds(other, rows)].astype(BF16)

            @pl.when(index > 0)
            def _():
                reduce_y(at).start()

            kept[at] = both[pl.ds(own, rows)]

        return carry

    load.wait()
    lax.fori_loop(0, 2 * planes - 1, step, 0)

    if reduced:
        reduce_y(plane).start()

        def collect(index, count):
            if gathered:
                index = 2 * planes - 3 - index
            at = side_plane((index + 2) // 2, index % 2)

            @pl.when(inside(at))
            def _():
                if piece is not None:
                    piece(land, count, planes, in_refs, out_refs, work_refs)
                reduce_y(at).wait_recv()
                z_out[at] = (kept[at] + y_in[at].astype(F32)).astype(BF16)
                reduce_z(at).start()

            return count + inside(at).astype(jnp.int32)

        count = lax.fori_loop(0, 2 * planes - 2, collect, 0)
        if piece is not None:
            piece(land, count, planes, in_refs, out_refs, work_refs)
        reduce_y(plane).wait_recv()
        sum_ref[...] = kept[plane] + y_in[plane].astype(F32)

        def finish(index, carry):
            at = (plane + 1 + index) % planes
            reduced_z(at).wait_recv()
            sum_ref[...] += z_in[at].astype(F32)
            return carry

        lax.fori_loop(0, planes - 1, finish, 0)

    if not gathered:
        @pl.when(plane < planes - 1)
        def _():
            along(plane, plane + 1, 0).wait_send()

        @pl.when(plane > 0)
        def _():
            along(plane, plane - 1, 1).wait_send()

    def drain(index, carry):
        distance = (index + 1) // 2
        side = 1 - index % 2
        at = side_plane(distance, side)
        target = plane + 1 - 2 * side

        @pl.when(inside(at))
        def _():
            if not gathered:

                @pl.when(jnp.logical_and(index > 0, inside(target)))
                def _():
                    along(at, target, side).wait_send()

                across(at, tensor).wait_send()
                beside(at, core, tensor, 0).wait_send()
                beside(at, core, 1 - tensor, 1).wait_send()
            if piece is None:
                save(at).wait()
            if reduced:
                reduce_core(at).wait_send()
                reduce_y(at).wait_send()

                @pl.when(index > 0)
                def _():
                    reduce_z(at).wait_send()

        return carry

    lax.fori_loop(0, 2 * planes - 1, drain, 0)


def spread(chunk, piece, own, inputs, layer, outputs, work, planes, ident, name, reduced=True):
    rows, width = own.shape
    gathered = rows == inputs[2].shape[0] if len(inputs) > 2 else False
    if gathered:
        rows //= 4 * planes
    count = planes * 4 * rows
    dma = pltpu.SemaphoreType.DMA
    shape = jax.ShapeDtypeStruct
    saved = (count, width) if piece is None else (16, width)
    total = shape((rows, width), F32) if reduced else shape((count, width), BF16)
    outs = [shape(saved, BF16), total] + list(outputs)
    held = planes if reduced else 1
    return pl.pallas_call(
        functools.partial(
            spread_kernel, chunk, piece, layer, planes, gathered, reduced, len(inputs), len(outputs), len(work)
        ),
        out_shape=outs,
        in_specs=[HBM if gathered else VMEM, HBM] + [VMEM] * (len(inputs) - 1),
        out_specs=[HBM, VMEM] + [VMEM] * len(outputs),
        scratch_shapes=list(work)
        + [
            pltpu.VMEM(inputs[0].shape[1:], BF16),
            pltpu.SemaphoreType.DMA,
            pltpu.VMEM((count, width), BF16),
            pltpu.VMEM((held, 2 * rows, width), BF16),
            pltpu.VMEM((held, 2 * rows, width), BF16),
            pltpu.VMEM((held, rows, width), BF16),
            pltpu.VMEM((held, rows, width), BF16),
            pltpu.VMEM((held, rows, width), BF16),
            pltpu.VMEM((held, rows, width), BF16),
            pltpu.VMEM((2 * rows, width), F32),
            pltpu.VMEM((held, rows, width), F32),
            dma((planes, 2)), dma((planes,)), dma((planes,)), dma((planes,)), dma((planes, 2)), dma((planes, 2)),
            dma((planes,)), dma((planes,)), dma((planes,)), dma((planes,)), dma((planes,)), dma((planes,)), dma((planes,)),
        ],
        compiler_params=pltpu.CompilerParams(collective_id=ident + 10 * layer, has_side_effects=True, vmem_limit_bytes=62 << 20),
        cost_estimate=pl.CostEstimate(
            flops=count * width, bytes_accessed=count, transcendentals=0
        ),
        name=name,
    )(own, *inputs)


def mlp_chunk(land, start, rows, in_refs, out_refs, work_refs):
    expand_w, down_w = in_refs
    gate_slope, up_slope, hidden_ref = out_refs
    span = pl.ds(start, rows)
    x = land[span]
    gate = dot(x, expand_w[0])
    up = dot(x, expand_w[1])
    sig = jax.nn.sigmoid(gate)
    silu = gate * sig
    hidden = (silu * up).astype(BF16)
    gate_slope[span] = (up * sig * (1.0 + gate * (1.0 - sig))).astype(BF16)
    up_slope[span] = silu.astype(BF16)
    hidden_ref[span] = hidden
    return dot(hidden, down_w[...])


def mlp_back_chunk(land, start, rows, in_refs, out_refs, work_refs):
    expand_w, down_w, gate_slope, up_slope = in_refs[:4]
    gate_ref, up_ref = work_refs
    span = pl.ds(start, rows)
    grad_hidden = dot(land[span], down_w[...], LAST)
    grad_gate = (grad_hidden * gate_slope[span].astype(F32)).astype(BF16)
    grad_up = (grad_hidden * up_slope[span].astype(F32)).astype(BF16)
    gate_ref[span] = grad_gate
    up_ref[span] = grad_up
    return dot(grad_gate, expand_w[0], LAST) + dot(grad_up, expand_w[1], LAST)


def mlp_back_piece(land, index, pieces, in_refs, out_refs, work_refs):
    normed, hidden = in_refs[4:]
    gate_ref, up_ref = work_refs
    d_expand, d_down = out_refs
    size = d_expand.shape[1] // pieces
    span = pl.ds(pl.multiple_of(index * size, size), size)
    rows = normed[:, span]
    d_expand[0, span] = dot(rows, gate_ref[...], ROWS).astype(BF16)
    d_expand[1, span] = dot(rows, up_ref[...], ROWS).astype(BF16)
    d_down[:, span] = dot(hidden[...], land[:, span], ROWS).astype(BF16)


def mlp_forward(own, expand, layer, down_w, planes):
    count = planes * 4 * own.shape[0]
    shape = jax.ShapeDtypeStruct((count, down_w.shape[0]), BF16)
    return spread(
        mlp_chunk,
        None,
        own,
        (expand, down_w),
        layer,
        (shape,) * 3,
        (),
        planes,
        1,
        "mlp_forward",
        layer == 0,
    )


def mlp_backward(own, expand, layer, down_w, gate_slope, up_slope, normed, hidden, planes):
    d_expand = jax.ShapeDtypeStruct(expand.shape[1:], BF16)
    reduce = jax.ShapeDtypeStruct(down_w.shape, BF16)
    work = pltpu.VMEM(gate_slope.shape, BF16)
    return spread(
        mlp_back_chunk,
        mlp_back_piece,
        own,
        (expand, down_w, gate_slope, up_slope, normed, hidden),
        layer,
        (d_expand, reduce),
        (work, work),
        planes,
        2,
        "mlp_backward",
    )[1:]


def feed_forward(own, expand_layer, down_w):
    planes = lax.axis_size("ctx") // 2
    if planes == 4:
        rows, total, *kept = mlp_forward(own, *expand_layer, down_w, planes)
        return rows, total if expand_layer[1] == 0 else scatter_tokens(total), *kept
    expand = expand_layer[0][expand_layer[1]]
    rows = gather_tokens(own)
    gate, up = dot(rows, expand[0]), dot(rows, expand[1])
    sig = jax.nn.sigmoid(gate)
    silu = gate * sig
    hidden = (silu * up).astype(BF16)
    gate_slope = (up * sig * (1.0 + gate * (1.0 - sig))).astype(BF16)
    total = scatter_tokens(dot(hidden, down_w).astype(BF16))
    return rows, total, gate_slope, silu.astype(BF16), hidden


def feed_backward(own, expand_layer, down_w, gate_slope, up_slope, normed, hidden):
    planes = lax.axis_size("ctx") // 2
    if planes == 4:
        return mlp_backward(
            own, *expand_layer, down_w, gate_slope, up_slope, normed, hidden, planes
        )
    expand = expand_layer[0][expand_layer[1]]
    rows = own if own.shape[0] == normed.shape[0] else gather_tokens(own)
    grad_hidden = dot(rows, down_w, LAST)
    grad_gate = (grad_hidden * gate_slope.astype(F32)).astype(BF16)
    grad_up = (grad_hidden * up_slope.astype(F32)).astype(BF16)
    part = dot(grad_gate, expand[0], LAST) + dot(grad_up, expand[1], LAST)
    return (
        scatter_tokens(part.astype(BF16)),
        jnp.stack([dot(normed, grad_gate, ROWS), dot(normed, grad_up, ROWS)]).astype(BF16),
        dot(hidden, rows, ROWS).astype(BF16),
    )


def greet_line(planes, plane, core):
    barrier = pltpu.get_barrier_semaphore()
    pl.semaphore_signal(
        barrier, inc=1, device_id={"ctx": plane * 2 + 1 - core}, device_id_type=MESH
    )
    for step in range(1, planes):
        there = (plane + step) % planes
        pl.semaphore_signal(
            barrier, inc=1, device_id={"ctx": there * 2 + core}, device_id_type=MESH
        )
    pl.semaphore_wait(barrier, planes)


def attend_kernel(planes, heads, with_job, *refs):
    mixed_ref, cosine_ref, sine_ref, qpos_ref, kpos_ref = refs[:5]
    if with_job:
        out_ref, low_ref, log_ref, all_ref, q_ref = refs[6:11]
        zs, zr, cs, cr = refs[12:16]
        start, stage, finish = share_job(2 * planes, refs[5], refs[11], *refs[16:])
    else:
        out_ref, low_ref, log_ref, all_ref, q_ref, zs, zr, cs, cr = refs[5:]
    ctx = lax.axis_index("ctx")
    plane, core = ctx // 2, ctx % 2
    batch, tokens = qpos_ref.shape[:2]
    head_dim = cosine_ref.shape[1]
    query_width = heads * head_dim
    factor = 1.0 / math.sqrt(head_dim)
    if with_job:
        greet_all(2 * planes, ctx)
    else:
        greet_line(planes, plane, core)
    core_peer = {"ctx": plane * 2 + 1 - core}

    def block(at):
        return all_ref.at[:, pl.ds(pl.multiple_of(at * tokens, tokens), tokens)]

    def along(there, source):
        ref = block(source * 2 + core)
        return remote(ref, ref, zs.at[there], zr.at[source], {"ctx": there * 2 + core})

    def beside(source, which):
        ref = block(source * 2 + which)
        return remote(ref, ref, cs.at[source], cr.at[source], core_peer)

    def turned(rows, span):
        values = mixed_ref[rows, span]
        return values * cosine_ref[rows] + pltpu.roll(values, head_dim // 2, 1) * sine_ref[rows]

    own = pl.ds(pl.multiple_of(ctx * tokens, tokens), tokens)
    for index in range(batch):
        rows = slice(index * tokens, (index + 1) * tokens)
        keys = turned(rows, slice(query_width, query_width + head_dim))
        all_ref[index, own, :head_dim] = keys.astype(BF16)
        all_ref[index, own, head_dim:] = mixed_ref[rows, query_width + head_dim :].astype(BF16)
    for step in range(1, planes):
        along((plane + step) % planes, plane).start()
    beside(plane, core).start()
    if with_job:
        start()
    for step in range(1, planes):
        source = (plane + step) % planes
        along(source, source).wait_recv()
        beside(source, core).start()
    for step in range(planes):
        beside((plane + step) % planes, 1 - core).wait_recv()

    def one(index, carry):
        rows = pl.ds(pl.multiple_of(index * tokens, tokens), tokens)
        keys = all_ref[index, :, :head_dim]
        values = all_ref[index, :, head_dim:]
        allowed = qpos_ref[index] >= kpos_ref[index]
        lane = lax.broadcasted_iota(jnp.int32, (tokens, head_dim), 1)
        logs = jnp.zeros((tokens, head_dim), F32)
        for head in range(heads):
            span = slice(head * head_dim, (head + 1) * head_dim)
            queries = turned(rows, span).astype(BF16)
            q_ref[rows, span] = queries
            scores = dot(queries, keys, LAST)
            scores = jnp.where(allowed, scores * factor, -1e30)
            top = jnp.max(scores, axis=1, keepdims=True)
            weights = jnp.exp(scores - top)
            total = jnp.sum(weights, axis=1, keepdims=True)
            logs = jnp.where(lane == head, top + jnp.log(total), logs)
            out = dot((weights * (1.0 / total)).astype(BF16), values)
            out_ref[rows, span] = out
            low_ref[rows, span] = out.astype(BF16)
        log_ref[rows] = logs
        return carry

    if with_job:
        stages = 2 * planes - 1
        for index in range(batch):
            stage(index)
            one(index, 0)
        for index in range(batch, stages):
            stage(index)
        finish()
    else:
        lax.fori_loop(0, batch, one, 0)
    for step in range(1, planes):
        along((plane + step) % planes, plane).wait_send()
        beside((plane + step) % planes, core).wait_send()
    beside(plane, core).wait_send()


def attend_back_kernel(
    planes, heads, q_ref, kv_ref, qpos_ref, kpos_ref, grad_ref, out_ref, log_ref, cosine_ref,
    sine_ref, mixed_ref, dkv_ref, whole, core_out, core_in, z_out, z_in, cs, cr, zs, zr,
):
    ctx = lax.axis_index("ctx")
    plane, core = ctx // 2, ctx % 2
    batch = qpos_ref.shape[0]
    tokens = q_ref.shape[0] // batch
    head_dim = kv_ref.shape[2] // 2
    factor = 1.0 / math.sqrt(head_dim)
    greet_line(planes, plane, core)
    core_peer = {"ctx": plane * 2 + 1 - core}

    def turned_back(grads, rows):
        rolled = pltpu.roll(grads, head_dim // 2, 1)
        return (grads * cosine_ref[rows] - rolled * sine_ref[rows]).astype(BF16)

    def to_core(index):
        return remote(core_out.at[index], core_in.at[index], cs.at[index], cr.at[index], core_peer)

    def to_plane(index, there, source):
        return remote(
            z_out.at[index, there],
            z_in.at[index, source],
            zs.at[index, there],
            zr.at[index, source],
            {"ctx": there * 2 + core},
        )

    def one(index, carry):
        rows = pl.ds(pl.multiple_of(index * tokens, tokens), tokens)
        keys = kv_ref[index, :, :head_dim]
        values = kv_ref[index, :, head_dim:]
        allowed = qpos_ref[index] >= kpos_ref[index]
        logs = log_ref[rows]
        for head in range(heads):
            span = slice(head * head_dim, (head + 1) * head_dim)
            queries = q_ref[rows, span]
            grads = grad_ref[rows, span]
            delta = jnp.sum(grads.astype(F32) * out_ref[rows, span], axis=1, keepdims=True)
            scores = jnp.where(allowed, dot(queries, keys, LAST) * factor, -1e30)
            weights = jnp.exp(scores - logs[:, head : head + 1])
            grad_scores = (weights * (dot(grads, values, LAST) - delta) * factor).astype(BF16)
            mixed_ref[rows, span] = turned_back(dot(grad_scores, keys), rows)
            grad_keys = dot(grad_scores, queries, ROWS)
            grad_values = dot(weights.astype(BF16), grads, ROWS)
            if head == 0:
                whole[index, :, :head_dim] = grad_keys
                whole[index, :, head_dim:] = grad_values
            else:
                whole[index, :, :head_dim] += grad_keys
                whole[index, :, head_dim:] += grad_values

        for at in range(planes):
            theirs = pl.multiple_of((at * 2 + 1 - core) * tokens, tokens)
            core_out[index, at] = whole[index, pl.ds(theirs, tokens)].astype(BF16)
        to_core(index).start()
        return carry

    lax.fori_loop(0, batch, one, 0)

    def mine(index, at):
        start = pl.multiple_of((at * 2 + core) * tokens, tokens)
        return whole[index, pl.ds(start, tokens)] + core_in[index, at].astype(F32)

    for index in range(batch):
        to_core(index).wait_recv()
        for step in range(1, planes):
            there = (plane + step) % planes
            z_out[index, there] = mine(index, there).astype(BF16)
            to_plane(index, there, plane).start()
        dkv_ref[index] = mine(index, plane)
    for index in range(batch):
        for step in range(1, planes):
            source = (plane + step) % planes
            to_plane(index, source, source).wait_recv()
            dkv_ref[index] += z_in[index, source].astype(F32)
        rows = slice(index * tokens, (index + 1) * tokens)
        width = heads * head_dim
        mixed_ref[rows, width : width + head_dim] = turned_back(dkv_ref[index, :, :head_dim], rows)
        mixed_ref[rows, width + head_dim :] = dkv_ref[index, :, head_dim:].astype(BF16)
    for index in range(batch):
        to_core(index).wait_send()
        for step in range(1, planes):
            to_plane(index, (plane + step) % planes, plane).wait_send()


def attend(mixed, tables, heads, blocks):
    cosine, sine, query_pos, key_pos, _ = tables
    batch, tokens = query_pos.shape
    head_dim = cosine.shape[1]
    query_width = heads * head_dim
    pair = 2 * head_dim
    planes = lax.axis_size("ctx") // 2
    keys = key_pos.shape[1]
    rows = batch * tokens
    if planes != 4:
        queries = rotate(
            mixed[:, :query_width].reshape(rows, heads, head_dim),
            cosine[:, None, :],
            sine[:, None, :],
        ).astype(BF16).reshape(rows, query_width)
        own_keys = rotate(mixed[:, query_width : query_width + head_dim], cosine, sine)
        kv = jnp.concatenate([own_keys, mixed[:, query_width + head_dim :]], axis=1).astype(BF16)
        kv_all = gather_ctx(kv.reshape(batch, tokens, pair), 1)
        split = queries.reshape(batch, tokens, heads, head_dim)
        scores = jnp.einsum(
            "bqhd,bkd->bqhk", split, kv_all[..., :head_dim], preferred_element_type=F32
        )
        allowed = query_pos[:, :, None, None] >= key_pos[:, None, None, :]
        scores = jnp.where(allowed, scores / math.sqrt(head_dim), -1e30)
        logs = jax.nn.logsumexp(scores, axis=-1)
        probs = jnp.exp(scores - logs[..., None]).astype(BF16)
        out = jnp.einsum(
            "bqhk,bkd->bqhd", probs, kv_all[..., head_dim:], preferred_element_type=F32
        ).reshape(queries.shape)
        shared = [share(part) for part in blocks]
        return out, out.astype(BF16), logs, kv_all, queries, *shared
    size = 2 * planes
    shape = jax.ShapeDtypeStruct
    dma = pltpu.SemaphoreType.DMA
    return pl.pallas_call(
        functools.partial(attend_kernel, planes, heads, len(blocks) > 0),
        out_shape=[
            shape((rows, query_width), F32),
            shape((rows, query_width), BF16),
            shape((rows, head_dim), F32),
            shape((batch, keys, pair), BF16),
            shape((rows, query_width), BF16),
        ]
        + [shape((2,) + part.shape, part.dtype) for part in blocks],
        in_specs=[VMEM] * 5 + [HBM] * len(blocks),
        out_specs=[VMEM] * 5 + [HBM] * len(blocks),
        scratch_shapes=[dma((planes,)), dma((planes,)), dma((planes,)), dma((planes,))]
        + ([dma((size,))] * 4 + [dma]) * len(blocks),
        compiler_params=pltpu.CompilerParams(
            collective_id=3 + 2 * len(blocks), has_side_effects=True, vmem_limit_bytes=48 << 20
        ),
        cost_estimate=pl.CostEstimate(
            flops=rows * keys, bytes_accessed=rows, transcendentals=0
        ),
        name="attend",
    )(mixed, cosine, signed(sine), query_pos[:, :, None], key_pos[:, None, :], *blocks)


def signed(sine):
    half = sine.shape[1] // 2
    return jnp.concatenate([-sine[:, :half], sine[:, half:]], axis=1)


def attend_backward(queries, kv_all, tables, grads, out, logs):
    cosine, sine, query_pos, key_pos, _ = tables
    batch, keys, pair = kv_all.shape
    head_dim = pair // 2
    heads = queries.shape[1] // head_dim
    rows = queries.shape[0]
    tokens = rows // batch
    planes = lax.axis_size("ctx") // 2
    if planes != 4:
        factor = 1.0 / math.sqrt(head_dim)
        k_all, v_all = kv_all[..., :head_dim], kv_all[..., head_dim:]
        split = queries.reshape(batch, tokens, heads, head_dim)
        grad_split = grads.reshape(split.shape)
        delta = jnp.sum(grad_split.astype(F32) * out.reshape(split.shape), axis=-1)
        scores = jnp.einsum("bqhd,bkd->bqhk", split, k_all, preferred_element_type=F32)
        allowed = query_pos[:, :, None, None] >= key_pos[:, None, None, :]
        scores = jnp.where(allowed, scores * factor, -1e30)
        probs = jnp.exp(scores - logs[..., None])
        grad_probs = jnp.einsum("bqhd,bkd->bqhk", grad_split, v_all, preferred_element_type=F32)
        grad_scores = (probs * (grad_probs - delta[..., None]) * factor).astype(BF16)
        dq = jnp.einsum("bqhk,bkd->bqhd", grad_scores, k_all, preferred_element_type=F32)
        dk = jnp.einsum("bqhk,bqhd->bkd", grad_scores, split, preferred_element_type=F32)
        dv = jnp.einsum(
            "bqhk,bqhd->bkd", probs.astype(BF16), grad_split, preferred_element_type=F32
        )
        dkv = lax.psum_scatter(
            jnp.concatenate([dk, dv], axis=-1).astype(BF16), "ctx", scatter_dimension=1, tiled=True
        )
        dkv = dkv.astype(F32).reshape(rows, pair)
        dq = unrotate(dq.reshape(rows, heads, head_dim), cosine[:, None, :], sine[:, None, :])
        dk = unrotate(dkv[:, :head_dim], cosine, sine)
        parts = [dq.reshape(queries.shape), dk, dkv[:, head_dim:]]
        return jnp.concatenate(parts, axis=1).astype(BF16)
    shape = jax.ShapeDtypeStruct
    dma = pltpu.SemaphoreType.DMA
    return pl.pallas_call(
        functools.partial(attend_back_kernel, planes, heads),
        out_shape=shape((rows, queries.shape[1] + pair), BF16),
        in_specs=[VMEM] * 9,
        out_specs=VMEM,
        scratch_shapes=[
            pltpu.VMEM((batch, tokens, pair), F32),
            pltpu.VMEM((batch, keys, pair), F32),
            pltpu.VMEM((batch, planes, tokens, pair), BF16),
            pltpu.VMEM((batch, planes, tokens, pair), BF16),
            pltpu.VMEM((batch, planes, tokens, pair), BF16),
            pltpu.VMEM((batch, planes, tokens, pair), BF16),
            dma((batch,)), dma((batch,)), dma((batch, planes)), dma((batch, planes)),
        ],
        compiler_params=pltpu.CompilerParams(
            collective_id=4, has_side_effects=True, vmem_limit_bytes=48 << 20
        ),
        cost_estimate=pl.CostEstimate(
            flops=rows * keys, bytes_accessed=rows, transcendentals=0
        ),
        name="attend_backward",
    )(
        queries,
        kv_all,
        query_pos[:, :, None],
        key_pos[:, None, :],
        grads,
        out,
        logs,
        cosine,
        signed(sine),
    )


def layer_forward(x_low, weights, tables, blocks, sooner, later):
    gain_attn, w_mixed, bias, w_project, gain_mlp, w_expand, w_reduce = weights
    cosine, sine, query_pos, key_pos, mine = tables
    count, width = x_low.shape
    query_width = w_project.shape[0]
    head_dim = (w_mixed.shape[1] - query_width) // 2
    heads = query_width // head_dim
    batch = query_pos.shape[0]
    tokens = count // batch
    x = x_low.astype(F32)
    root_attn = inverse_root(x)
    normed = (x * root_attn * gain_attn).astype(BF16)
    mixed = dot(normed, w_mixed) + bias
    mixed, sooner = lax.optimization_barrier((mixed, sooner))
    attended_full, attended, log_total, kv, queries, *shared = attend(
        mixed, tables, heads, blocks
    )
    if shared:
        w_expand = (shared[0].reshape((2, 2, width, -1)), 0)
    x_mine = lax.dynamic_slice_in_dim(x, mine * tokens, tokens, 0)
    middle = x_mine + tensor_scatter(dot(attended, w_project))
    root_mlp = inverse_root(middle)
    normed_mlp = (middle * root_mlp * gain_mlp).astype(BF16)
    normed_mlp, later = lax.optimization_barrier((normed_mlp, later))
    all_normed, branch, gate_slope, up_slope, hidden = feed_forward(
        normed_mlp, w_expand, w_reduce
    )
    result = middle + branch
    kept = (
        x_mine,
        lax.dynamic_slice_in_dim(root_attn, mine * tokens, tokens, 0),
        normed,
        queries,
        kv,
        attended_full,
        log_total,
        attended,
        middle,
        root_mlp,
        all_normed,
        gate_slope,
        up_slope,
        hidden,
    )
    return result.astype(BF16), kept, w_expand, sooner, later


def layer_backward(grad_out, grad_rows, kept, weights, tables, route, earlier, pinned):
    gain_attn, w_mixed, bias, w_project, gain_mlp, w_expand, w_reduce = weights
    cosine, sine, query_pos, key_pos, mine = tables
    (
        x_mine,
        root_attn,
        normed,
        queries,
        kv,
        attended_full,
        log_total,
        attended,
        middle,
        root_mlp,
        all_normed,
        gate_slope,
        up_slope,
        hidden,
    ) = kept
    count, query_width = queries.shape
    head_dim = (w_mixed.shape[1] - query_width) // 2
    heads = query_width // head_dim
    grad_normed_mlp, d_expand, d_reduce = feed_backward(
        grad_rows,
        w_expand,
        w_reduce,
        gate_slope,
        up_slope,
        all_normed,
        hidden,
    )
    grad_normed_mlp, earlier = lax.optimization_barrier((grad_normed_mlp, earlier))
    moved_reduce = lax.ppermute(d_reduce, "section", route)
    grad_middle, d_gain_mlp = norm_backward(middle, root_mlp, gain_mlp, grad_normed_mlp)
    grad_middle = grad_middle + grad_out
    grad_branch = tensor_pair(grad_middle.astype(BF16))
    grad_attended = dot(grad_branch, w_project, LAST).astype(BF16)
    grad_mixed = attend_backward(
        queries, kv, tables, grad_attended, attended_full, log_total
    )
    if earlier:
        d_project = dot(attended, grad_branch, ROWS)
    grad_mixed, moved_reduce, pinned, late_branch = lax.optimization_barrier(
        (grad_mixed, moved_reduce, pinned, grad_branch)
    )
    if not earlier:
        d_project = dot(attended, late_branch, ROWS)
    d_mixed = dot(normed, grad_mixed, ROWS)
    d_bias = jnp.sum(grad_mixed.astype(F32), axis=0)
    grad_normed = tensor_scatter(dot(grad_mixed, w_mixed, LAST))
    grad_x, d_gain_attn = norm_backward(x_mine, root_attn, gain_attn, grad_normed)
    grad_x = (grad_x + grad_middle).astype(BF16)
    vectors = (d_gain_attn, d_mixed, d_bias, d_project, d_gain_mlp)
    return grad_x, vectors, d_expand, (d_reduce, moved_reduce), earlier, pinned


def shards(
    block_input, positions, cotangent, norm_attn, w_qkv, b_qkv, w_out, norm_mlp, w_gate_up, w_down
):
    section = lax.axis_index("section")
    tensor = lax.axis_index("tensor")
    ctx = lax.axis_index("ctx")
    ctx_size = lax.axis_size("ctx")
    first = section == 0
    micro, tokens, width = block_input.shape
    half = micro // 2
    head_dim = w_qkv.shape[3] - w_out.shape[2] * ctx_size
    head_dim = head_dim // 2
    slice_width = norm_attn.shape[1]
    slice_bias = b_qkv.shape[2]
    units = w_down.shape[1]

    def plane_part(value):
        return lax.dynamic_slice_in_dim(value, section * half, half, 0)

    def layers(own, other):
        return jnp.where(first, own, other), jnp.where(first, other, own)

    x = plane_part(block_input).reshape(half * tokens, width)
    pos_local = plane_part(positions)
    cosine, sine = angles(pos_local.reshape(-1), head_dim)

    small = jnp.concatenate([norm_attn[0], norm_mlp[0], b_qkv[0, 0]])
    qkv, out = w_qkv[0, :, 0, :], w_out[0, 0]
    vectors = jnp.concatenate(layers(small, swap(small)))
    places = jnp.concatenate([pos_local // 64, pos_local % 64]).reshape(-1).astype(BF16)
    packed = gather_ctx(jnp.concatenate([vectors, places])[None], 0)
    places = packed[:, vectors.shape[0] :].astype(jnp.int32).reshape(ctx_size, 2, half, tokens)
    pos_all = jnp.swapaxes(places[:, 0] * 64 + places[:, 1], 0, 1).reshape(half, -1)
    tables = (cosine, sine, pos_local, pos_all, tensor)
    small_size = 2 * slice_width + slice_bias
    small0, small1 = packed[:, :small_size], packed[:, small_size : 2 * small_size]
    qkv0, qkv1 = layers(qkv, swap(qkv))
    out0, out1 = layers(out, swap(out))
    down_moved = swap(w_down[0])
    down0, down1 = layers(w_down[0], down_moved)
    expand = w_gate_up[0].reshape(slice_width, 2, ctx_size, units)
    blocks = jnp.transpose(expand, (1, 2, 0, 3))

    def whole(small, qkv, out, expand, down):
        return (
            small[:, :slice_width].reshape(1, width),
            gather_ctx(qkv, 0),
            small[:, 2 * slice_width :].reshape(1, slice_bias * ctx_size),
            gather_ctx(out, 0),
            small[:, slice_width : 2 * slice_width].reshape(1, width),
            expand,
            down,
        )

    weights0 = whole(small0, qkv0, out0, None, down0)

    result0, kept0, expand0, down_moved, (qkv1, out1) = layer_forward(
        x, weights0, tables, (blocks,), down_moved, (qkv1, out1)
    )
    weights0 = weights0[:5] + (expand0, down0)
    weights1 = whole(small1, qkv1, out1, (expand0[0], 1), down1)
    x1 = tensor_pair(result0)
    seeds, x1 = lax.optimization_barrier((plane_part(cotangent), x1))
    seed_rows = gather_ctx(seeds.reshape(half * tokens, width), 0)
    result1, kept1, *_ = layer_forward(x1, weights1, tables, (), (), ())
    out1_all = tensor_pair(result1)

    def exchange(layer0, layer1):
        kept_here = jnp.where(first, layer0, layer1)
        received = swap(jnp.where(first, layer1, layer0))
        low = jnp.where(first, kept_here, received)
        high = jnp.where(first, received, kept_here)
        both = jnp.concatenate([low, high], axis=0)
        return both.reshape(1, micro, tokens, width)

    seed = lax.dynamic_slice_in_dim(seeds, tensor, 1, 0)[0].astype(F32)
    def ctx_scatter(value):
        return lax.psum_scatter(
            value.astype(BF16), "ctx", scatter_dimension=0, tiled=True
        )

    group = w_qkv.shape[3]
    split_at = group - head_dim

    def with_vectors(grads):
        gain_attn, mixed, bias, project, gain_mlp = grads[:5]
        rows = jnp.concatenate(
            [
                bias[:split_at].reshape(ctx_size, -1),
                bias[split_at:].reshape(ctx_size, -1),
                gain_attn.reshape(ctx_size, slice_width),
                gain_mlp.reshape(ctx_size, slice_width),
            ],
            axis=1,
        )
        rows = jnp.pad(rows[:, None, :], ((0, 0), (0, 15), (0, group - rows.shape[1])))
        mixed = mixed.reshape(ctx_size, slice_width, group)
        both = jnp.concatenate([mixed.astype(BF16), rows.astype(BF16)], axis=1)
        return both.reshape(ctx_size * (slice_width + 16), group)

    grad1, d1, d_expand1, d_reduce1, _, out1_all = layer_backward(
        seed, seed_rows, kept1, weights1, tables, [(0, 1)], (), out1_all
    )
    section_output = exchange(x1, out1_all)
    slices1 = (ctx_scatter(with_vectors(d1)), ctx_scatter(d1[3]))
    grad1_all = tensor_pair(grad1)
    grad0, d0, d_expand0, d_reduce0, earlier, _ = layer_backward(
        grad1.astype(F32), grad1, kept0, weights0, tables, [(1, 0)], slices1 + (section_output, grad1_all), ()
    )
    slices1, (section_output, grad1_all) = earlier[:2], earlier[2:]

    def to_owner(part0, part1):
        received0 = lax.ppermute(part0.astype(BF16), "section", [(1, 0)])
        received1 = lax.ppermute(part1.astype(BF16), "section", [(0, 1)])
        own = jnp.where(first, part0, part1).astype(F32)
        return own + jnp.where(first, received0, received1).astype(F32)

    def of_owner(pair0, pair1):
        own, received = (jnp.where(first, low, high).astype(F32) for low, high in zip(pair0, pair1))
        return own + received

    blocks = (2, ctx_size, slice_width, units)
    grad0_all = tensor_pair(grad0)
    grad0_all, d_expand0 = lax.optimization_barrier((grad0_all, d_expand0))
    input_grad = exchange(grad0_all, grad1_all)
    total = collect(d_expand0.reshape(blocks), d_expand1.reshape(blocks), first)
    d_expand = lax.optimization_barrier(jnp.transpose(total, (2, 0, 1, 3)))
    d_expand = lax.optimization_barrier(d_expand.reshape(1, slice_width, 2, ctx_size * units))
    d_expand = d_expand.astype(F32)
    d_reduce = of_owner(d_reduce0, d_reduce1)

    d_mixed = to_owner(ctx_scatter(with_vectors(d0)), slices1[0])
    d_project = to_owner(ctx_scatter(d0[3]), slices1[1])
    vectors = d_mixed[slice_width]
    d_mixed = d_mixed[:slice_width]
    count_qk, count_v = split_at // ctx_size, head_dim // ctx_size
    bias_qk = vectors[:count_qk][None]
    bias_v = vectors[count_qk : count_qk + count_v][None]
    start = count_qk + count_v
    gains = vectors[start : start + 2 * slice_width].reshape(1, 2 * slice_width)
    gains = gains + lax.ppermute(gains, "tensor", SWAP)
    return (
        section_output,
        input_grad,
        gains[:, :slice_width],
        d_mixed[None, :, None, :],
        bias_qk[None],
        bias_v[None],
        d_project[None, None],
        gains[:, slice_width:],
        d_expand,
        d_reduce[None],
    )


def solution(mesh):
    in_specs = (
        P(None, "ctx", None),
        P(None, "ctx"),
        P(None, "ctx", None),
        P("section", "ctx"),
        P("section", "ctx", "tensor", None),
        P("section", "tensor", "ctx"),
        P("section", "tensor", "ctx", None),
        P("section", "ctx"),
        P("section", "ctx", None, "tensor"),
        P("section", ("tensor", "ctx"), None),
    )
    out_specs = (
        P("section", None, "ctx", None),
        P("section", None, "ctx", None),
        P("section", "ctx"),
        P("section", "ctx", "tensor", None),
        P("section", "tensor", "ctx"),
        P("section", "tensor", "ctx"),
        P("section", "tensor", "ctx", None),
        P("section", "ctx"),
        P("section", "ctx", None, "tensor"),
        P("section", ("tensor", "ctx"), None),
    )
    return jax.shard_map(shards, mesh=mesh, in_specs=in_specs, out_specs=out_specs, check_vma=False)
```

```python
import functools
import functools
import math

import jax
import jax.numpy as jnp
from jax import lax
from jax.experimental import pallas as pl
from jax.experimental.pallas import tpu as pltpu
from jax.sharding import PartitionSpec as P

EPSILON = 1e-06
ROPE_BASE = 1000000.0
ROWS = (((0,), (0,)), ((), ()))
LAST = (((1,), (1,)), ((), ()))
F32 = jnp.float32
BF16 = jnp.bfloat16
SWAP = [(0, 1), (1, 0)]
MESH = pl.DeviceIdType.MESH
VMEM = pl.BlockSpec(memory_space=pltpu.VMEM)
HBM = pl.BlockSpec(memory_space=pl.ANY)


def dot(a, b, dims=(((1,), (0,)), ((), ()))):
    return lax.dot_general(a, b, dims, preferred_element_type=F32)


def angles(positions, head_dim):
    half_dim = head_dim // 2
    frequency = ROPE_BASE ** (-(jnp.arange(half_dim, dtype=F32) * 2.0) / head_dim)
    phases = positions.astype(F32)[:, None] * frequency[None, :]
    phases = jnp.concatenate([phases, phases], axis=-1)
    return jnp.cos(phases), jnp.sin(phases)


def rotate(values, cosine, sine):
    half = values.shape[-1] // 2
    turned = jnp.concatenate([-values[..., half:], values[..., :half]], axis=-1)
    return values * cosine + turned * sine


def unrotate(grads, cosine, sine):
    half = grads.shape[-1] // 2
    twisted = grads * sine
    turned = jnp.concatenate([twisted[..., half:], -twisted[..., :half]], axis=-1)
    return grads * cosine + turned


def inverse_root(values):
    return lax.rsqrt(jnp.mean(values * values, axis=-1, keepdims=True) + EPSILON)


def norm_backward(values, root, gain, grad_normed):
    normal = values * root
    gain_grad = jnp.sum(grad_normed * normal, axis=0)
    scaled = grad_normed * gain
    mean = jnp.mean(scaled * normal, axis=-1, keepdims=True)
    return root * (scaled - normal * mean), gain_grad


def swap(value):
    return lax.ppermute(value, "section", SWAP)


def gather_ctx(value, axis):
    return lax.all_gather(value, "ctx", axis=axis, tiled=True)


def gather_tokens(rows):
    return lax.all_gather(rows, ("ctx", "tensor"), axis=0, tiled=True)


def scatter_tokens(rows):
    return lax.psum_scatter(rows, ("ctx", "tensor"), scatter_dimension=0, tiled=True).astype(F32)


def tensor_gather(rows):
    return lax.all_gather(rows, "tensor", axis=0, tiled=True)


def tensor_pair(rows):
    received = lax.ppermute(rows, "tensor", SWAP)
    mine = lax.axis_index("tensor") == 0
    return jnp.concatenate([jnp.where(mine, rows, received), jnp.where(mine, received, rows)])


def tensor_scatter(rows):
    mine = lax.axis_index("tensor")
    tokens = rows.shape[0] // 2
    own = lax.dynamic_slice_in_dim(rows, mine * tokens, tokens, 0)
    other = lax.dynamic_slice_in_dim(rows, (1 - mine) * tokens, tokens, 0)
    return own + lax.ppermute(other.astype(BF16), "tensor", SWAP).astype(F32)


def greet_all(size, me):
    barrier = pltpu.get_barrier_semaphore()
    for step in range(1, size):
        pl.semaphore_signal(
            barrier, inc=1, device_id={"ctx": (me + step) % size}, device_id_type=MESH
        )
    there = 1 - lax.axis_index("section")
    pl.semaphore_signal(barrier, inc=1, device_id={"section": there}, device_id_type=MESH)
    pl.semaphore_wait(barrier, size)


def by_distance(size):
    return sorted(range(size), key=lambda step: min(step, size - step))


def share_job(size, from_ref, all_ref, send, recv, over_send, over_recv, local):
    me = lax.axis_index("ctx")
    section = lax.axis_index("section")
    order = by_distance(size)[1:]

    def copy(there, source):
        return remote(
            from_ref.at[:, there],
            all_ref.at[section, :, source],
            send.at[there],
            recv.at[source],
            {"ctx": there},
        )

    def over(block, source):
        return remote(
            block,
            all_ref.at[section, :, source],
            over_send.at[source],
            over_recv.at[source],
            {"section": 1 - section},
        )

    def own():
        return pltpu.make_async_copy(from_ref.at[:, me], all_ref.at[section, :, me], local)

    def start():
        own().start()
        over(from_ref.at[:, me], me).start()
        for step in order[:2]:
            copy((me + step) % size, me).start()

    def stage(index):
        step = order[index]
        source = (me + size - step) % size
        copy(source, source).wait_recv()
        over(all_ref.at[section, :, source], source).start()
        copy((me + step) % size, me).wait_send()
        if index + 2 < len(order):
            copy((me + order[index + 2]) % size, me).start()

    def finish():
        own().wait()
        for step in range(size):
            source = (me + step) % size
            over(all_ref.at[section, :, source], source).wait()

    return start, stage, finish


def share(blocks):
    moved = lax.all_to_all(blocks, "ctx", split_axis=1, concat_axis=1, tiled=True)
    return lax.all_gather(moved, "section")


def collect_kernel(
    size, first_ref, second_ref, to_ref, own, other, send, recv, over_send, over_recv, local, store
):
    me = lax.axis_index("ctx")
    section = lax.axis_index("section")
    greet_all(size, me)
    order = by_distance(size)[::-1]

    def over(source_ref, at):
        return remote(
            source_ref.at[:, at], other.at[at], over_send.at[at], over_recv.at[at],
            {"section": 1 - section},
        )

    def load(source_ref, at):
        return pltpu.make_async_copy(source_ref.at[:, at], own.at[at], local.at[at])

    def copy(there, source):
        return remote(
            own.at[there], to_ref.at[:, source], send.at[there], recv.at[source], {"ctx": there}
        )

    def start(at):
        @pl.when(section == 0)
        def _():
            over(second_ref, at).start()
            load(first_ref, at).start()

        @pl.when(section == 1)
        def _():
            over(first_ref, at).start()
            load(second_ref, at).start()

    for index, step in enumerate(order):
        at = (me + step) % size
        if index == 0:
            start(at)
        if index + 1 < size:
            start((me + order[index + 1]) % size)
        over(first_ref, at).wait()
        load(first_ref, at).wait()
        own[at] = (own[at].astype(F32) + other[at].astype(F32)).astype(own.dtype)
        if step > 0:
            copy(at, me).start()
        else:
            mine = pltpu.make_async_copy(own.at[at], to_ref.at[:, me], store)
            mine.start()
            mine.wait()
    for step in order:
        at = (me + step) % size
        if step > 0:
            copy(at, at).wait_recv()
            copy(at, me).wait_send()


def collect(first, second, is_first):
    parts, size, rows, columns = first.shape
    if size != 8:
        received = lax.ppermute(jnp.where(is_first, second, first), "section", SWAP)
        total = jnp.where(is_first, first, second).astype(F32) + received.astype(F32)
        return lax.all_to_all(
            total.astype(BF16), "ctx", split_axis=1, concat_axis=1, tiled=True
        )
    dma = pltpu.SemaphoreType.DMA
    block = pltpu.VMEM((size, parts, rows, columns), first.dtype)
    return pl.pallas_call(
        functools.partial(collect_kernel, size),
        out_shape=jax.ShapeDtypeStruct(first.shape, first.dtype),
        in_specs=[HBM, HBM],
        out_specs=HBM,
        scratch_shapes=[block, block]
        + [dma((size,)), dma((size,)), dma((size,)), dma((size,)), dma((size,)), dma],
        compiler_params=pltpu.CompilerParams(
            collective_id=6, has_side_effects=True, vmem_limit_bytes=24 << 20
        ),
        cost_estimate=pl.CostEstimate(flops=first.size, bytes_accessed=1024, transcendentals=0),
        name="collect",
    )(first, second)


def join_kernel(blocks_ref, out_ref):
    parts, size = blocks_ref.shape[:2]
    for part in range(parts):
        pieces = [blocks_ref[part, index].astype(F32) for index in range(size)]
        out_ref[:, part, :] = jnp.concatenate(pieces, axis=1)


def join(blocks):
    parts, size, rows, columns = blocks.shape
    if size != 8:
        joined = jnp.transpose(blocks, (2, 0, 1, 3))
        return joined.reshape(rows, parts, size * columns).astype(F32)
    tile = 32
    return pl.pallas_call(
        join_kernel,
        grid=(rows // tile,),
        out_shape=jax.ShapeDtypeStruct((rows, parts, size * columns), F32),
        in_specs=[pl.BlockSpec((parts, size, tile, columns), lambda index: (0, 0, index, 0))],
        out_specs=pl.BlockSpec((tile, parts, size * columns), lambda index: (index, 0, 0)),
        compiler_params=pltpu.CompilerParams(vmem_limit_bytes=32 << 20),
        name="join",
    )(blocks)


def cut_kernel(rows_ref, out_ref):
    parts, size = out_ref.shape[:2]
    columns = out_ref.shape[3]
    for part in range(parts):
        values = rows_ref[:, part, :]
        for index in range(size):
            out_ref[part, index] = values[:, index * columns : (index + 1) * columns]


def cut(values, size):
    rows, parts, columns = values.shape
    columns //= size
    if size != 8:
        return jnp.transpose(values.reshape(rows, parts, size, columns), (1, 2, 0, 3))
    tile = 32
    return pl.pallas_call(
        cut_kernel,
        grid=(rows // tile,),
        out_shape=jax.ShapeDtypeStruct((parts, size, rows, columns), values.dtype),
        in_specs=[pl.BlockSpec((tile, parts, size * columns), lambda index: (index, 0, 0))],
        out_specs=pl.BlockSpec((parts, size, tile, columns), lambda index: (0, 0, index, 0)),
        compiler_params=pltpu.CompilerParams(vmem_limit_bytes=32 << 20),
        name="cut",
    )(values)


def remote(src, dst, send, recv, device):
    return pltpu.make_async_remote_copy(
        src_ref=src, dst_ref=dst, send_sem=send, recv_sem=recv, device_id=device, device_id_type=MESH
    )


def spread_kernel(
    chunk, piece, layer, planes, gathered, reduced, ins, outs, extra, own_ref, *refs
):
    in_refs, refs = refs[:ins], refs[ins:]
    all_ref, sum_ref = refs[:2]
    out_refs, refs = refs[2 : 2 + outs], refs[2 + outs :]
    work_refs, refs = refs[:extra], refs[extra:]
    (expand_w, load_sem), refs = refs[:2], refs[2:]
    load = pltpu.make_async_copy(in_refs[0].at[layer], expand_w, load_sem)
    load.start()
    in_refs = (expand_w,) + in_refs[1:]
    (land, core_out, core_in, y_out, y_in, z_out, z_in, both, kept,
     zs, zr, ys, yr, cs, cr, rcs, rcr, rys, ryr, rzs, rzr, local) = refs
    tensor = lax.axis_index("tensor")
    ctx = lax.axis_index("ctx")
    plane, core = ctx // 2, ctx % 2
    rows = own_ref.shape[0] // (4 * planes if gathered else 1)
    y_peer = {"tensor": 1 - tensor}
    core_peer = {"ctx": plane * 2 + 1 - core}

    barrier = pltpu.get_barrier_semaphore()
    pl.semaphore_signal(barrier, inc=1, device_id=y_peer, device_id_type=MESH)
    pl.semaphore_signal(barrier, inc=1, device_id=core_peer, device_id_type=MESH)
    for step in range(1, planes):
        there = (plane + step) % planes
        pl.semaphore_signal(barrier, inc=1, device_id={"ctx": there * 2 + core}, device_id_type=MESH)
    pl.semaphore_wait(barrier, planes + 1)

    def block(at, which_core, which_tensor):
        start = pl.multiple_of(((at * 2 + which_core) * 2 + which_tensor) * rows, rows)
        return land.at[pl.ds(start, rows)]

    def along(at, target, direction):
        ref = block(at, core, tensor)
        return remote(ref, ref, zs.at[at, direction], zr.at[at], {"ctx": target * 2 + core})

    def across(at, which_tensor):
        ref = block(at, core, which_tensor)
        return remote(ref, ref, ys.at[at], yr.at[at], y_peer)

    def beside(at, which_core, which_tensor, slot):
        ref = block(at, which_core, which_tensor)
        return remote(ref, ref, cs.at[at, slot], cr.at[at, slot], core_peer)

    if not gathered:
        start = pl.multiple_of(((plane * 2 + core) * 2 + tensor) * rows, rows)
        land[pl.ds(start, rows)] = own_ref[...]

        @pl.when(plane < planes - 1)
        def _():
            along(plane, plane + 1, 0).start()

        @pl.when(plane > 0)
        def _():
            along(plane, plane - 1, 1).start()

        across(plane, tensor).start()
        beside(plane, core, tensor, 0).start()

    def reduce_core(at):
        return remote(core_out.at[at], core_in.at[at], rcs.at[at], rcr.at[at], core_peer)

    def reduce_y(at):
        return remote(y_out.at[at], y_in.at[at], rys.at[at], ryr.at[at], y_peer)

    def reduce_z(at):
        return remote(z_out.at[at], z_in.at[plane], rzs.at[at], rzr.at[plane], {"ctx": at * 2 + core})

    def reduced_z(at):
        return remote(z_out.at[at], z_in.at[at], rzs.at[at], rzr.at[at], {"ctx": at * 2 + core})

    def save(at):
        span = pl.ds(pl.multiple_of(at * 4 * rows, 4 * rows), 4 * rows)
        return pltpu.make_async_copy(land.at[span], all_ref.at[span], local.at[at])

    def side_plane(distance, side):
        return plane + distance * (2 * side - 1)

    def inside(at):
        return jnp.logical_and(at >= 0, at < planes)

    def pass_on(distance, side):
        at = side_plane(distance, side)
        target = plane + 1 - 2 * side

        @pl.when(inside(at))
        def _():
            along(at, plane, 0).wait_recv()

            @pl.when(inside(target))
            def _():
                along(at, target, side).start()

            across(at, tensor).start()
            beside(at, core, tensor, 0).start()

    def pass_beside(distance, side):
        at = side_plane(distance, side)

        @pl.when(inside(at))
        def _():
            across(at, 1 - tensor).wait_recv()
            beside(at, core, 1 - tensor, 1).start()

    def fetch(at):
        span = pl.ds(pl.multiple_of(at * 4 * rows, 4 * rows), 4 * rows)
        return pltpu.make_async_copy(own_ref.at[span], land.at[span], local.at[at])

    if gathered:
        for at in range(planes):
            fetch(at).start()

    def step(index, carry):
        if gathered:
            index = 2 * planes - 2 - index
        distance = (index + 1) // 2
        at = side_plane(distance, 1 - index % 2)

        if not gathered:

            @pl.when(jnp.logical_or(index == 0, index % 2 == 1))
            def _():
                pass_on(distance + 1, 0)
                pass_on(distance + 1, 1)

                @pl.when(distance > 0)
                def _():
                    pass_beside(distance, 0)

                pass_beside(distance, 1)

        @pl.when(inside(at))
        def _():
            if gathered:
                fetch(at).wait()
            else:
                beside(at, 1 - core, tensor, 0).wait_recv()
                beside(at, 1 - core, 1 - tensor, 1).wait_recv()
            if piece is None:
                save(at).start()
            theirs = pl.multiple_of((at * 2 + 1 - core) * 2 * rows, 2 * rows)
            mine = pl.multiple_of((at * 2 + core) * 2 * rows, 2 * rows)
            if not reduced:
                for start in (theirs, mine):
                    part = chunk(land, start, 2 * rows, in_refs, out_refs, work_refs)
                    sum_ref[pl.ds(start, 2 * rows)] = part.astype(BF16)
                return
            core_out[at] = chunk(land, theirs, 2 * rows, in_refs, out_refs, work_refs).astype(BF16)
            reduce_core(at).start()
            both[...] = chunk(land, mine, 2 * rows, in_refs, out_refs, work_refs)
            reduce_core(at).wait_recv()
            both[...] += core_in[at].astype(F32)
            other = pl.multiple_of((1 - tensor) * rows, rows)
            own = pl.multiple_of(tensor * rows, rows)
            y_out[at] = both[pl.ds(other, rows)].astype(BF16)

            @pl.when(index > 0)
            def _():
                reduce_y(at).start()

            kept[at] = both[pl.ds(own, rows)]

        return carry

    load.wait()
    lax.fori_loop(0, 2 * planes - 1, step, 0)

    if reduced:
        reduce_y(plane).start()

        def collect(index, count):
            if gathered:
                index = 2 * planes - 3 - index
            at = side_plane((index + 2) // 2, index % 2)

            @pl.when(inside(at))
            def _():
                if piece is not None:
                    piece(land, count, planes, in_refs, out_refs, work_refs)
                reduce_y(at).wait_recv()
                z_out[at] = (kept[at] + y_in[at].astype(F32)).astype(BF16)
                reduce_z(at).start()

            return count + inside(at).astype(jnp.int32)

        count = lax.fori_loop(0, 2 * planes - 2, collect, 0)
        if piece is not None:
            piece(land, count, planes, in_refs, out_refs, work_refs)
        reduce_y(plane).wait_recv()
        sum_ref[...] = kept[plane] + y_in[plane].astype(F32)

        def finish(index, carry):
            at = (plane + 1 + index) % planes
            reduced_z(at).wait_recv()
            sum_ref[...] += z_in[at].astype(F32)
            return carry

        lax.fori_loop(0, planes - 1, finish, 0)

    if not gathered:
        @pl.when(plane < planes - 1)
        def _():
            along(plane, plane + 1, 0).wait_send()

        @pl.when(plane > 0)
        def _():
            along(plane, plane - 1, 1).wait_send()

    def drain(index, carry):
        distance = (index + 1) // 2
        side = 1 - index % 2
        at = side_plane(distance, side)
        target = plane + 1 - 2 * side

        @pl.when(inside(at))
        def _():
            if not gathered:

                @pl.when(jnp.logical_and(index > 0, inside(target)))
                def _():
                    along(at, target, side).wait_send()

                across(at, tensor).wait_send()
                beside(at, core, tensor, 0).wait_send()
                beside(at, core, 1 - tensor, 1).wait_send()
            if piece is None:
                save(at).wait()
            if reduced:
                reduce_core(at).wait_send()
                reduce_y(at).wait_send()

                @pl.when(index > 0)
                def _():
                    reduce_z(at).wait_send()

        return carry

    lax.fori_loop(0, 2 * planes - 1, drain, 0)


def spread(chunk, piece, own, inputs, layer, outputs, work, planes, ident, name, reduced=True):
    rows, width = own.shape
    gathered = rows == inputs[2].shape[0] if len(inputs) > 2 else False
    if gathered:
        rows //= 4 * planes
    count = planes * 4 * rows
    dma = pltpu.SemaphoreType.DMA
    shape = jax.ShapeDtypeStruct
    saved = (count, width) if piece is None else (16, width)
    total = shape((rows, width), F32) if reduced else shape((count, width), BF16)
    outs = [shape(saved, BF16), total] + list(outputs)
    held = planes if reduced else 1
    return pl.pallas_call(
        functools.partial(
            spread_kernel, chunk, piece, layer, planes, gathered, reduced, len(inputs), len(outputs), len(work)
        ),
        out_shape=outs,
        in_specs=[HBM if gathered else VMEM, HBM] + [VMEM] * (len(inputs) - 1),
        out_specs=[HBM, VMEM] + [VMEM] * len(outputs),
        scratch_shapes=list(work)
        + [
            pltpu.VMEM(inputs[0].shape[1:], BF16),
            pltpu.SemaphoreType.DMA,
            pltpu.VMEM((count, width), BF16),
            pltpu.VMEM((held, 2 * rows, width), BF16),
            pltpu.VMEM((held, 2 * rows, width), BF16),
            pltpu.VMEM((held, rows, width), BF16),
            pltpu.VMEM((held, rows, width), BF16),
            pltpu.VMEM((held, rows, width), BF16),
            pltpu.VMEM((held, rows, width), BF16),
            pltpu.VMEM((2 * rows, width), F32),
            pltpu.VMEM((held, rows, width), F32),
            dma((planes, 2)), dma((planes,)), dma((planes,)), dma((planes,)), dma((planes, 2)), dma((planes, 2)),
            dma((planes,)), dma((planes,)), dma((planes,)), dma((planes,)), dma((planes,)), dma((planes,)), dma((planes,)),
        ],
        compiler_params=pltpu.CompilerParams(collective_id=ident + 10 * layer, has_side_effects=True, vmem_limit_bytes=62 << 20),
        cost_estimate=pl.CostEstimate(
            flops=count * width, bytes_accessed=count, transcendentals=0
        ),
        name=name,
    )(own, *inputs)


def mlp_chunk(land, start, rows, in_refs, out_refs, work_refs):
    expand_w, down_w = in_refs
    gate_slope, up_slope, hidden_ref = out_refs
    span = pl.ds(start, rows)
    x = land[span]
    gate = dot(x, expand_w[0])
    up = dot(x, expand_w[1])
    sig = jax.nn.sigmoid(gate)
    silu = gate * sig
    hidden = (silu * up).astype(BF16)
    gate_slope[span] = (up * sig * (1.0 + gate * (1.0 - sig))).astype(BF16)
    up_slope[span] = silu.astype(BF16)
    hidden_ref[span] = hidden
    return dot(hidden, down_w[...])


def mlp_back_chunk(land, start, rows, in_refs, out_refs, work_refs):
    expand_w, down_w, gate_slope, up_slope = in_refs[:4]
    gate_ref, up_ref = work_refs
    span = pl.ds(start, rows)
    grad_hidden = dot(land[span], down_w[...], LAST)
    grad_gate = (grad_hidden * gate_slope[span].astype(F32)).astype(BF16)
    grad_up = (grad_hidden * up_slope[span].astype(F32)).astype(BF16)
    gate_ref[span] = grad_gate
    up_ref[span] = grad_up
    return dot(grad_gate, expand_w[0], LAST) + dot(grad_up, expand_w[1], LAST)


def mlp_back_piece(land, index, pieces, in_refs, out_refs, work_refs):
    normed, hidden = in_refs[4:]
    gate_ref, up_ref = work_refs
    d_expand, d_down = out_refs
    size = d_expand.shape[1] // pieces
    span = pl.ds(pl.multiple_of(index * size, size), size)
    rows = normed[:, span]
    d_expand[0, span] = dot(rows, gate_ref[...], ROWS).astype(BF16)
    d_expand[1, span] = dot(rows, up_ref[...], ROWS).astype(BF16)
    d_down[:, span] = dot(hidden[...], land[:, span], ROWS).astype(BF16)


def mlp_forward(own, expand, layer, down_w, planes):
    count = planes * 4 * own.shape[0]
    shape = jax.ShapeDtypeStruct((count, down_w.shape[0]), BF16)
    return spread(
        mlp_chunk,
        None,
        own,
        (expand, down_w),
        layer,
        (shape,) * 3,
        (),
        planes,
        1,
        "mlp_forward",
        layer == 0,
    )


def mlp_backward(own, expand, layer, down_w, gate_slope, up_slope, normed, hidden, planes):
    d_expand = jax.ShapeDtypeStruct(expand.shape[1:], BF16)
    reduce = jax.ShapeDtypeStruct(down_w.shape, BF16)
    work = pltpu.VMEM(gate_slope.shape, BF16)
    return spread(
        mlp_back_chunk,
        mlp_back_piece,
        own,
        (expand, down_w, gate_slope, up_slope, normed, hidden),
        layer,
        (d_expand, reduce),
        (work, work),
        planes,
        2,
        "mlp_backward",
    )[1:]


def feed_forward(own, expand_layer, down_w):
    planes = lax.axis_size("ctx") // 2
    if planes == 4:
        rows, total, *kept = mlp_forward(own, *expand_layer, down_w, planes)
        return rows, total if expand_layer[1] == 0 else scatter_tokens(total), *kept
    expand = expand_layer[0][expand_layer[1]]
    rows = gather_tokens(own)
    gate, up = dot(rows, expand[0]), dot(rows, expand[1])
    sig = jax.nn.sigmoid(gate)
    silu = gate * sig
    hidden = (silu * up).astype(BF16)
    gate_slope = (up * sig * (1.0 + gate * (1.0 - sig))).astype(BF16)
    total = scatter_tokens(dot(hidden, down_w).astype(BF16))
    return rows, total, gate_slope, silu.astype(BF16), hidden


def feed_backward(own, expand_layer, down_w, gate_slope, up_slope, normed, hidden):
    planes = lax.axis_size("ctx") // 2
    if planes == 4:
        return mlp_backward(
            own, *expand_layer, down_w, gate_slope, up_slope, normed, hidden, planes
        )
    expand = expand_layer[0][expand_layer[1]]
    rows = own if own.shape[0] == normed.shape[0] else gather_tokens(own)
    grad_hidden = dot(rows, down_w, LAST)
    grad_gate = (grad_hidden * gate_slope.astype(F32)).astype(BF16)
    grad_up = (grad_hidden * up_slope.astype(F32)).astype(BF16)
    part = dot(grad_gate, expand[0], LAST) + dot(grad_up, expand[1], LAST)
    return (
        scatter_tokens(part.astype(BF16)),
        jnp.stack([dot(normed, grad_gate, ROWS), dot(normed, grad_up, ROWS)]).astype(BF16),
        dot(hidden, rows, ROWS).astype(BF16),
    )


def greet_line(planes, plane, core):
    barrier = pltpu.get_barrier_semaphore()
    pl.semaphore_signal(
        barrier, inc=1, device_id={"ctx": plane * 2 + 1 - core}, device_id_type=MESH
    )
    for step in range(1, planes):
        there = (plane + step) % planes
        pl.semaphore_signal(
            barrier, inc=1, device_id={"ctx": there * 2 + core}, device_id_type=MESH
        )
    pl.semaphore_wait(barrier, planes)


def attend_kernel(planes, heads, with_job, *refs):
    mixed_ref, cosine_ref, sine_ref, qpos_ref, kpos_ref = refs[:5]
    if with_job:
        out_ref, low_ref, log_ref, all_ref, q_ref = refs[6:11]
        zs, zr, cs, cr = refs[12:16]
        start, stage, finish = share_job(2 * planes, refs[5], refs[11], *refs[16:])
    else:
        out_ref, low_ref, log_ref, all_ref, q_ref, zs, zr, cs, cr = refs[5:]
    ctx = lax.axis_index("ctx")
    plane, core = ctx // 2, ctx % 2
    batch, tokens = qpos_ref.shape[:2]
    head_dim = cosine_ref.shape[1]
    query_width = heads * head_dim
    factor = 1.0 / math.sqrt(head_dim)
    if with_job:
        greet_all(2 * planes, ctx)
    else:
        greet_line(planes, plane, core)
    core_peer = {"ctx": plane * 2 + 1 - core}

    def block(at):
        return all_ref.at[:, pl.ds(pl.multiple_of(at * tokens, tokens), tokens)]

    def along(there, source):
        ref = block(source * 2 + core)
        return remote(ref, ref, zs.at[there], zr.at[source], {"ctx": there * 2 + core})

    def beside(source, which):
        ref = block(source * 2 + which)
        return remote(ref, ref, cs.at[source], cr.at[source], core_peer)

    def turned(rows, span):
        values = mixed_ref[rows, span]
        return values * cosine_ref[rows] + pltpu.roll(values, head_dim // 2, 1) * sine_ref[rows]

    own = pl.ds(pl.multiple_of(ctx * tokens, tokens), tokens)
    for index in range(batch):
        rows = slice(index * tokens, (index + 1) * tokens)
        keys = turned(rows, slice(query_width, query_width + head_dim))
        all_ref[index, own, :head_dim] = keys.astype(BF16)
        all_ref[index, own, head_dim:] = mixed_ref[rows, query_width + head_dim :].astype(BF16)
    for step in range(1, planes):
        along((plane + step) % planes, plane).start()
    beside(plane, core).start()
    if with_job:
        start()
    for step in range(1, planes):
        source = (plane + step) % planes
        along(source, source).wait_recv()
        beside(source, core).start()
    for step in range(planes):
        beside((plane + step) % planes, 1 - core).wait_recv()

    def one(index, carry):
        rows = pl.ds(pl.multiple_of(index * tokens, tokens), tokens)
        keys = all_ref[index, :, :head_dim]
        values = all_ref[index, :, head_dim:]
        allowed = qpos_ref[index] >= kpos_ref[index]
        lane = lax.broadcasted_iota(jnp.int32, (tokens, head_dim), 1)
        logs = jnp.zeros((tokens, head_dim), F32)
        for head in range(heads):
            span = slice(head * head_dim, (head + 1) * head_dim)
            queries = turned(rows, span).astype(BF16)
            q_ref[rows, span] = queries
            scores = dot(queries, keys, LAST)
            scores = jnp.where(allowed, scores * factor, -1e30)
            top = jnp.max(scores, axis=1, keepdims=True)
            weights = jnp.exp(scores - top)
            total = jnp.sum(weights, axis=1, keepdims=True)
            logs = jnp.where(lane == head, top + jnp.log(total), logs)
            out = dot((weights * (1.0 / total)).astype(BF16), values)
            out_ref[rows, span] = out
            low_ref[rows, span] = out.astype(BF16)
        log_ref[rows] = logs
        return carry

    if with_job:
        stages = 2 * planes - 1
        for index in range(batch):
            stage(index)
            one(index, 0)
        for index in range(batch, stages):
            stage(index)
        finish()
    else:
        lax.fori_loop(0, batch, one, 0)
    for step in range(1, planes):
        along((plane + step) % planes, plane).wait_send()
        beside((plane + step) % planes, core).wait_send()
    beside(plane, core).wait_send()


def attend_back_kernel(
    planes, heads, q_ref, kv_ref, qpos_ref, kpos_ref, grad_ref, out_ref, log_ref, cosine_ref,
    sine_ref, mixed_ref, dkv_ref, whole, core_out, core_in, z_out, z_in, cs, cr, zs, zr,
):
    ctx = lax.axis_index("ctx")
    plane, core = ctx // 2, ctx % 2
    batch = qpos_ref.shape[0]
    tokens = q_ref.shape[0] // batch
    head_dim = kv_ref.shape[2] // 2
    factor = 1.0 / math.sqrt(head_dim)
    greet_line(planes, plane, core)
    core_peer = {"ctx": plane * 2 + 1 - core}

    def turned_back(grads, rows):
        rolled = pltpu.roll(grads, head_dim // 2, 1)
        return (grads * cosine_ref[rows] - rolled * sine_ref[rows]).astype(BF16)

    def to_core(index):
        return remote(core_out.at[index], core_in.at[index], cs.at[index], cr.at[index], core_peer)

    def to_plane(index, there, source):
        return remote(
            z_out.at[index, there],
            z_in.at[index, source],
            zs.at[index, there],
            zr.at[index, source],
            {"ctx": there * 2 + core},
        )

    def one(index, carry):
        rows = pl.ds(pl.multiple_of(index * tokens, tokens), tokens)
        keys = kv_ref[index, :, :head_dim]
        values = kv_ref[index, :, head_dim:]
        allowed = qpos_ref[index] >= kpos_ref[index]
        logs = log_ref[rows]
        for head in range(heads):
            span = slice(head * head_dim, (head + 1) * head_dim)
            queries = q_ref[rows, span]
            grads = grad_ref[rows, span]
            delta = jnp.sum(grads.astype(F32) * out_ref[rows, span], axis=1, keepdims=True)
            scores = jnp.where(allowed, dot(queries, keys, LAST) * factor, -1e30)
            weights = jnp.exp(scores - logs[:, head : head + 1])
            grad_scores = (weights * (dot(grads, values, LAST) - delta) * factor).astype(BF16)
            mixed_ref[rows, span] = turned_back(dot(grad_scores, keys), rows)
            grad_keys = dot(grad_scores, queries, ROWS)
            grad_values = dot(weights.astype(BF16), grads, ROWS)
            if head == 0:
                whole[index, :, :head_dim] = grad_keys
                whole[index, :, head_dim:] = grad_values
            else:
                whole[index, :, :head_dim] += grad_keys
                whole[index, :, head_dim:] += grad_values

        for at in range(planes):
            theirs = pl.multiple_of((at * 2 + 1 - core) * tokens, tokens)
            core_out[index, at] = whole[index, pl.ds(theirs, tokens)].astype(BF16)
        to_core(index).start()
        return carry

    lax.fori_loop(0, batch, one, 0)

    def mine(index, at):
        start = pl.multiple_of((at * 2 + core) * tokens, tokens)
        return whole[index, pl.ds(start, tokens)] + core_in[index, at].astype(F32)

    for index in range(batch):
        to_core(index).wait_recv()
        for step in range(1, planes):
            there = (plane + step) % planes
            z_out[index, there] = mine(index, there).astype(BF16)
            to_plane(index, there, plane).start()
        dkv_ref[index] = mine(index, plane)
    for index in range(batch):
        for step in range(1, planes):
            source = (plane + step) % planes
            to_plane(index, source, source).wait_recv()
            dkv_ref[index] += z_in[index, source].astype(F32)
        rows = slice(index * tokens, (index + 1) * tokens)
        width = heads * head_dim
        mixed_ref[rows, width : width + head_dim] = turned_back(dkv_ref[index, :, :head_dim], rows)
        mixed_ref[rows, width + head_dim :] = dkv_ref[index, :, head_dim:].astype(BF16)
    for index in range(batch):
        to_core(index).wait_send()
        for step in range(1, planes):
            to_plane(index, (plane + step) % planes, plane).wait_send()


def attend(mixed, tables, heads, blocks):
    cosine, sine, query_pos, key_pos, _ = tables
    batch, tokens = query_pos.shape
    head_dim = cosine.shape[1]
    query_width = heads * head_dim
    pair = 2 * head_dim
    planes = lax.axis_size("ctx") // 2
    keys = key_pos.shape[1]
    rows = batch * tokens
    if planes != 4:
        queries = rotate(
            mixed[:, :query_width].reshape(rows, heads, head_dim),
            cosine[:, None, :],
            sine[:, None, :],
        ).astype(BF16).reshape(rows, query_width)
        own_keys = rotate(mixed[:, query_width : query_width + head_dim], cosine, sine)
        kv = jnp.concatenate([own_keys, mixed[:, query_width + head_dim :]], axis=1).astype(BF16)
        kv_all = gather_ctx(kv.reshape(batch, tokens, pair), 1)
        split = queries.reshape(batch, tokens, heads, head_dim)
        scores = jnp.einsum(
            "bqhd,bkd->bqhk", split, kv_all[..., :head_dim], preferred_element_type=F32
        )
        allowed = query_pos[:, :, None, None] >= key_pos[:, None, None, :]
        scores = jnp.where(allowed, scores / math.sqrt(head_dim), -1e30)
        logs = jax.nn.logsumexp(scores, axis=-1)
        probs = jnp.exp(scores - logs[..., None]).astype(BF16)
        out = jnp.einsum(
            "bqhk,bkd->bqhd", probs, kv_all[..., head_dim:], preferred_element_type=F32
        ).reshape(queries.shape)
        shared = [share(part) for part in blocks]
        return out, out.astype(BF16), logs, kv_all, queries, *shared
    size = 2 * planes
    shape = jax.ShapeDtypeStruct
    dma = pltpu.SemaphoreType.DMA
    return pl.pallas_call(
        functools.partial(attend_kernel, planes, heads, len(blocks) > 0),
        out_shape=[
            shape((rows, query_width), F32),
            shape((rows, query_width), BF16),
            shape((rows, head_dim), F32),
            shape((batch, keys, pair), BF16),
            shape((rows, query_width), BF16),
        ]
        + [shape((2,) + part.shape, part.dtype) for part in blocks],
        in_specs=[VMEM] * 5 + [HBM] * len(blocks),
        out_specs=[VMEM] * 5 + [HBM] * len(blocks),
        scratch_shapes=[dma((planes,)), dma((planes,)), dma((planes,)), dma((planes,))]
        + ([dma((size,))] * 4 + [dma]) * len(blocks),
        compiler_params=pltpu.CompilerParams(
            collective_id=3 + 2 * len(blocks), has_side_effects=True, vmem_limit_bytes=48 << 20
        ),
        cost_estimate=pl.CostEstimate(
            flops=rows * keys, bytes_accessed=rows, transcendentals=0
        ),
        name="attend",
    )(mixed, cosine, signed(sine), query_pos[:, :, None], key_pos[:, None, :], *blocks)


def signed(sine):
    half = sine.shape[1] // 2
    return jnp.concatenate([-sine[:, :half], sine[:, half:]], axis=1)


def attend_backward(queries, kv_all, tables, grads, out, logs):
    cosine, sine, query_pos, key_pos, _ = tables
    batch, keys, pair = kv_all.shape
    head_dim = pair // 2
    heads = queries.shape[1] // head_dim
    rows = queries.shape[0]
    tokens = rows // batch
    planes = lax.axis_size("ctx") // 2
    if planes != 4:
        factor = 1.0 / math.sqrt(head_dim)
        k_all, v_all = kv_all[..., :head_dim], kv_all[..., head_dim:]
        split = queries.reshape(batch, tokens, heads, head_dim)
        grad_split = grads.reshape(split.shape)
        delta = jnp.sum(grad_split.astype(F32) * out.reshape(split.shape), axis=-1)
        scores = jnp.einsum("bqhd,bkd->bqhk", split, k_all, preferred_element_type=F32)
        allowed = query_pos[:, :, None, None] >= key_pos[:, None, None, :]
        scores = jnp.where(allowed, scores * factor, -1e30)
        probs = jnp.exp(scores - logs[..., None])
        grad_probs = jnp.einsum("bqhd,bkd->bqhk", grad_split, v_all, preferred_element_type=F32)
        grad_scores = (probs * (grad_probs - delta[..., None]) * factor).astype(BF16)
        dq = jnp.einsum("bqhk,bkd->bqhd", grad_scores, k_all, preferred_element_type=F32)
        dk = jnp.einsum("bqhk,bqhd->bkd", grad_scores, split, preferred_element_type=F32)
        dv = jnp.einsum(
            "bqhk,bqhd->bkd", probs.astype(BF16), grad_split, preferred_element_type=F32
        )
        dkv = lax.psum_scatter(
            jnp.concatenate([dk, dv], axis=-1).astype(BF16), "ctx", scatter_dimension=1, tiled=True
        )
        dkv = dkv.astype(F32).reshape(rows, pair)
        dq = unrotate(dq.reshape(rows, heads, head_dim), cosine[:, None, :], sine[:, None, :])
        dk = unrotate(dkv[:, :head_dim], cosine, sine)
        parts = [dq.reshape(queries.shape), dk, dkv[:, head_dim:]]
        return jnp.concatenate(parts, axis=1).astype(BF16)
    shape = jax.ShapeDtypeStruct
    dma = pltpu.SemaphoreType.DMA
    return pl.pallas_call(
        functools.partial(attend_back_kernel, planes, heads),
        out_shape=shape((rows, queries.shape[1] + pair), BF16),
        in_specs=[VMEM] * 9,
        out_specs=VMEM,
        scratch_shapes=[
            pltpu.VMEM((batch, tokens, pair), F32),
            pltpu.VMEM((batch, keys, pair), F32),
            pltpu.VMEM((batch, planes, tokens, pair), BF16),
            pltpu.VMEM((batch, planes, tokens, pair), BF16),
            pltpu.VMEM((batch, planes, tokens, pair), BF16),
            pltpu.VMEM((batch, planes, tokens, pair), BF16),
            dma((batch,)), dma((batch,)), dma((batch, planes)), dma((batch, planes)),
        ],
        compiler_params=pltpu.CompilerParams(
            collective_id=4, has_side_effects=True, vmem_limit_bytes=48 << 20
        ),
        cost_estimate=pl.CostEstimate(
            flops=rows * keys, bytes_accessed=rows, transcendentals=0
        ),
        name="attend_backward",
    )(
        queries,
        kv_all,
        query_pos[:, :, None],
        key_pos[:, None, :],
        grads,
        out,
        logs,
        cosine,
        signed(sine),
    )


def layer_forward(x_low, weights, tables, blocks, sooner, later):
    gain_attn, w_mixed, bias, w_project, gain_mlp, w_expand, w_reduce = weights
    cosine, sine, query_pos, key_pos, mine = tables
    count, width = x_low.shape
    query_width = w_project.shape[0]
    head_dim = (w_mixed.shape[1] - query_width) // 2
    heads = query_width // head_dim
    batch = query_pos.shape[0]
    tokens = count // batch
    x = x_low.astype(F32)
    root_attn = inverse_root(x)
    normed = (x * root_attn * gain_attn).astype(BF16)
    mixed = dot(normed, w_mixed) + bias
    mixed, sooner = lax.optimization_barrier((mixed, sooner))
    attended_full, attended, log_total, kv, queries, *shared = attend(
        mixed, tables, heads, blocks
    )
    if shared:
        w_expand = (shared[0].reshape((2, 2, width, -1)), 0)
    x_mine = lax.dynamic_slice_in_dim(x, mine * tokens, tokens, 0)
    middle = x_mine + tensor_scatter(dot(attended, w_project))
    root_mlp = inverse_root(middle)
    normed_mlp = (middle * root_mlp * gain_mlp).astype(BF16)
    normed_mlp, later = lax.optimization_barrier((normed_mlp, later))
    all_normed, branch, gate_slope, up_slope, hidden = feed_forward(
        normed_mlp, w_expand, w_reduce
    )
    result = middle + branch
    kept = (
        x_mine,
        lax.dynamic_slice_in_dim(root_attn, mine * tokens, tokens, 0),
        normed,
        queries,
        kv,
        attended_full,
        log_total,
        attended,
        middle,
        root_mlp,
        all_normed,
        gate_slope,
        up_slope,
        hidden,
    )
    return result.astype(BF16), kept, w_expand, sooner, later


def layer_backward(grad_out, grad_rows, kept, weights, tables, route, earlier, pinned):
    gain_attn, w_mixed, bias, w_project, gain_mlp, w_expand, w_reduce = weights
    cosine, sine, query_pos, key_pos, mine = tables
    (
        x_mine,
        root_attn,
        normed,
        queries,
        kv,
        attended_full,
        log_total,
        attended,
        middle,
        root_mlp,
        all_normed,
        gate_slope,
        up_slope,
        hidden,
    ) = kept
    count, query_width = queries.shape
    head_dim = (w_mixed.shape[1] - query_width) // 2
    heads = query_width // head_dim
    grad_normed_mlp, d_expand, d_reduce = feed_backward(
        grad_rows,
        w_expand,
        w_reduce,
        gate_slope,
        up_slope,
        all_normed,
        hidden,
    )
    grad_normed_mlp, earlier = lax.optimization_barrier((grad_normed_mlp, earlier))
    moved_reduce = lax.ppermute(d_reduce, "section", route)
    grad_middle, d_gain_mlp = norm_backward(middle, root_mlp, gain_mlp, grad_normed_mlp)
    grad_middle = grad_middle + grad_out
    grad_branch = tensor_pair(grad_middle.astype(BF16))
    grad_attended = dot(grad_branch, w_project, LAST).astype(BF16)
    grad_mixed = attend_backward(
        queries, kv, tables, grad_attended, attended_full, log_total
    )
    if earlier:
        d_project = dot(attended, grad_branch, ROWS)
    grad_mixed, moved_reduce, pinned, late_branch = lax.optimization_barrier(
        (grad_mixed, moved_reduce, pinned, grad_branch)
    )
    if not earlier:
        d_project = dot(attended, late_branch, ROWS)
    d_mixed = dot(normed, grad_mixed, ROWS)
    d_bias = jnp.sum(grad_mixed.astype(F32), axis=0)
    grad_normed = tensor_scatter(dot(grad_mixed, w_mixed, LAST))
    grad_x, d_gain_attn = norm_backward(x_mine, root_attn, gain_attn, grad_normed)
    grad_x = (grad_x + grad_middle).astype(BF16)
    vectors = (d_gain_attn, d_mixed, d_bias, d_project, d_gain_mlp)
    return grad_x, vectors, d_expand, (d_reduce, moved_reduce), earlier, pinned


def shards(
    block_input, positions, cotangent, norm_attn, w_qkv, b_qkv, w_out, norm_mlp, w_gate_up, w_down
):
    section = lax.axis_index("section")
    tensor = lax.axis_index("tensor")
    ctx = lax.axis_index("ctx")
    ctx_size = lax.axis_size("ctx")
    first = section == 0
    micro, tokens, width = block_input.shape
    half = micro // 2
    head_dim = w_qkv.shape[3] - w_out.shape[2] * ctx_size
    head_dim = head_dim // 2
    slice_width = norm_attn.shape[1]
    slice_bias = b_qkv.shape[2]
    units = w_down.shape[1]

    def plane_part(value):
        return lax.dynamic_slice_in_dim(value, section * half, half, 0)

    def layers(own, other):
        return jnp.where(first, own, other), jnp.where(first, other, own)

    x = plane_part(block_input).reshape(half * tokens, width)
    pos_local = plane_part(positions)
    cosine, sine = angles(pos_local.reshape(-1), head_dim)

    small = jnp.concatenate([norm_attn[0], norm_mlp[0], b_qkv[0, 0]])
    qkv, out = w_qkv[0, :, 0, :], w_out[0, 0]
    vectors = jnp.concatenate(layers(small, swap(small)))
    places = jnp.concatenate([pos_local // 64, pos_local % 64]).reshape(-1).astype(BF16)
    packed = gather_ctx(jnp.concatenate([vectors, places])[None], 0)
    places = packed[:, vectors.shape[0] :].astype(jnp.int32).reshape(ctx_size, 2, half, tokens)
    pos_all = jnp.swapaxes(places[:, 0] * 64 + places[:, 1], 0, 1).reshape(half, -1)
    tables = (cosine, sine, pos_local, pos_all, tensor)
    small_size = 2 * slice_width + slice_bias
    small0, small1 = packed[:, :small_size], packed[:, small_size : 2 * small_size]
    qkv0, qkv1 = layers(qkv, swap(qkv))
    out0, out1 = layers(out, swap(out))
    down_moved = swap(w_down[0])
    down0, down1 = layers(w_down[0], down_moved)
    blocks = cut(w_gate_up[0], ctx_size)

    def whole(small, qkv, out, expand, down):
        return (
            small[:, :slice_width].reshape(1, width),
            gather_ctx(qkv, 0),
            small[:, 2 * slice_width :].reshape(1, slice_bias * ctx_size),
            gather_ctx(out, 0),
            small[:, slice_width : 2 * slice_width].reshape(1, width),
            expand,
            down,
        )

    weights0 = whole(small0, qkv0, out0, None, down0)

    result0, kept0, expand0, down_moved, (qkv1, out1) = layer_forward(
        x, weights0, tables, (blocks,), down_moved, (qkv1, out1)
    )
    weights0 = weights0[:5] + (expand0, down0)
    weights1 = whole(small1, qkv1, out1, (expand0[0], 1), down1)
    x1 = tensor_pair(result0)
    seeds, x1 = lax.optimization_barrier((plane_part(cotangent), x1))
    seed_rows = gather_ctx(seeds.reshape(half * tokens, width), 0)
    result1, kept1, *_ = layer_forward(x1, weights1, tables, (), (), ())
    out1_all = tensor_pair(result1)

    def exchange(layer0, layer1):
        kept_here = jnp.where(first, layer0, layer1)
        received = swap(jnp.where(first, layer1, layer0))
        low = jnp.where(first, kept_here, received)
        high = jnp.where(first, received, kept_here)
        both = jnp.concatenate([low, high], axis=0)
        return both.reshape(1, micro, tokens, width)

    seed = lax.dynamic_slice_in_dim(seeds, tensor, 1, 0)[0].astype(F32)
    def ctx_scatter(value):
        return lax.psum_scatter(
            value.astype(BF16), "ctx", scatter_dimension=0, tiled=True
        )

    group = w_qkv.shape[3]
    split_at = group - head_dim

    def with_vectors(grads):
        gain_attn, mixed, bias, project, gain_mlp = grads[:5]
        rows = jnp.concatenate(
            [
                bias[:split_at].reshape(ctx_size, -1),
                bias[split_at:].reshape(ctx_size, -1),
                gain_attn.reshape(ctx_size, slice_width),
                gain_mlp.reshape(ctx_size, slice_width),
            ],
            axis=1,
        )
        rows = jnp.pad(rows[:, None, :], ((0, 0), (0, 15), (0, group - rows.shape[1])))
        mixed = mixed.reshape(ctx_size, slice_width, group)
        both = jnp.concatenate([mixed.astype(BF16), rows.astype(BF16)], axis=1)
        return both.reshape(ctx_size * (slice_width + 16), group)

    grad1, d1, d_expand1, d_reduce1, _, out1_all = layer_backward(
        seed, seed_rows, kept1, weights1, tables, [(0, 1)], (), out1_all
    )
    section_output = exchange(x1, out1_all)
    slices1 = (ctx_scatter(with_vectors(d1)), ctx_scatter(d1[3]))
    grad1_all = tensor_pair(grad1)
    grad0, d0, d_expand0, d_reduce0, earlier, _ = layer_backward(
        grad1.astype(F32), grad1, kept0, weights0, tables, [(1, 0)], slices1 + (section_output, grad1_all), ()
    )
    slices1, (section_output, grad1_all) = earlier[:2], earlier[2:]

    def to_owner(part0, part1):
        received0 = lax.ppermute(part0.astype(BF16), "section", [(1, 0)])
        received1 = lax.ppermute(part1.astype(BF16), "section", [(0, 1)])
        own = jnp.where(first, part0, part1).astype(F32)
        return own + jnp.where(first, received0, received1).astype(F32)

    def of_owner(pair0, pair1):
        own, received = (jnp.where(first, low, high).astype(F32) for low, high in zip(pair0, pair1))
        return own + received

    blocks = (2, ctx_size, slice_width, units)
    grad0_all = tensor_pair(grad0)
    grad0_all, d_expand0 = lax.optimization_barrier((grad0_all, d_expand0))
    input_grad = exchange(grad0_all, grad1_all)
    total = collect(d_expand0.reshape(blocks), d_expand1.reshape(blocks), first)
    d_expand = join(total)[None]
    d_reduce = of_owner(d_reduce0, d_reduce1)

    d_mixed = to_owner(ctx_scatter(with_vectors(d0)), slices1[0])
    d_project = to_owner(ctx_scatter(d0[3]), slices1[1])
    vectors = d_mixed[slice_width]
    d_mixed = d_mixed[:slice_width]
    count_qk, count_v = split_at // ctx_size, head_dim // ctx_size
    bias_qk = vectors[:count_qk][None]
    bias_v = vectors[count_qk : count_qk + count_v][None]
    start = count_qk + count_v
    gains = vectors[start : start + 2 * slice_width].reshape(1, 2 * slice_width)
    gains = gains + lax.ppermute(gains, "tensor", SWAP)
    return (
        section_output,
        input_grad,
        gains[:, :slice_width],
        d_mixed[None, :, None, :],
        bias_qk[None],
        bias_v[None],
        d_project[None, None],
        gains[:, slice_width:],
        d_expand,
        d_reduce[None],
    )


def solution(mesh):
    in_specs = (
        P(None, "ctx", None),
        P(None, "ctx"),
        P(None, "ctx", None),
        P("section", "ctx"),
        P("section", "ctx", "tensor", None),
        P("section", "tensor", "ctx"),
        P("section", "tensor", "ctx", None),
        P("section", "ctx"),
        P("section", "ctx", None, "tensor"),
        P("section", ("tensor", "ctx"), None),
    )
    out_specs = (
        P("section", None, "ctx", None),
        P("section", None, "ctx", None),
        P("section", "ctx"),
        P("section", "ctx", "tensor", None),
        P("section", "tensor", "ctx"),
        P("section", "tensor", "ctx"),
        P("section", "tensor", "ctx", None),
        P("section", "ctx"),
        P("section", "ctx", None, "tensor"),
        P("section", ("tensor", "ctx"), None),
    )
    return jax.shard_map(shards, mesh=mesh, in_specs=in_specs, out_specs=out_specs, check_vma=False)
```

```python
import functools
import functools
import math

import jax
import jax.numpy as jnp
from jax import lax
from jax.experimental import pallas as pl
from jax.experimental.pallas import tpu as pltpu
from jax.sharding import PartitionSpec as P

EPSILON = 1e-06
ROPE_BASE = 1000000.0
ROWS = (((0,), (0,)), ((), ()))
LAST = (((1,), (1,)), ((), ()))
F32 = jnp.float32
BF16 = jnp.bfloat16
SWAP = [(0, 1), (1, 0)]
MESH = pl.DeviceIdType.MESH
VMEM = pl.BlockSpec(memory_space=pltpu.VMEM)
HBM = pl.BlockSpec(memory_space=pl.ANY)


def dot(a, b, dims=(((1,), (0,)), ((), ()))):
    return lax.dot_general(a, b, dims, preferred_element_type=F32)


def angles(positions, head_dim):
    half_dim = head_dim // 2
    frequency = ROPE_BASE ** (-(jnp.arange(half_dim, dtype=F32) * 2.0) / head_dim)
    phases = positions.astype(F32)[:, None] * frequency[None, :]
    phases = jnp.concatenate([phases, phases], axis=-1)
    return jnp.cos(phases), jnp.sin(phases)


def rotate(values, cosine, sine):
    half = values.shape[-1] // 2
    turned = jnp.concatenate([-values[..., half:], values[..., :half]], axis=-1)
    return values * cosine + turned * sine


def unrotate(grads, cosine, sine):
    half = grads.shape[-1] // 2
    twisted = grads * sine
    turned = jnp.concatenate([twisted[..., half:], -twisted[..., :half]], axis=-1)
    return grads * cosine + turned


def inverse_root(values):
    return lax.rsqrt(jnp.mean(values * values, axis=-1, keepdims=True) + EPSILON)


def norm_backward(values, root, gain, grad_normed):
    normal = values * root
    gain_grad = jnp.sum(grad_normed * normal, axis=0)
    scaled = grad_normed * gain
    mean = jnp.mean(scaled * normal, axis=-1, keepdims=True)
    return root * (scaled - normal * mean), gain_grad


def swap(value):
    return lax.ppermute(value, "section", SWAP)


def gather_ctx(value, axis):
    return lax.all_gather(value, "ctx", axis=axis, tiled=True)


def gather_tokens(rows):
    return lax.all_gather(rows, ("ctx", "tensor"), axis=0, tiled=True)


def scatter_tokens(rows):
    return lax.psum_scatter(rows, ("ctx", "tensor"), scatter_dimension=0, tiled=True).astype(F32)


def tensor_gather(rows):
    return lax.all_gather(rows, "tensor", axis=0, tiled=True)


def tensor_pair(rows):
    received = lax.ppermute(rows, "tensor", SWAP)
    mine = lax.axis_index("tensor") == 0
    return jnp.concatenate([jnp.where(mine, rows, received), jnp.where(mine, received, rows)])


def tensor_scatter(rows):
    mine = lax.axis_index("tensor")
    tokens = rows.shape[0] // 2
    own = lax.dynamic_slice_in_dim(rows, mine * tokens, tokens, 0)
    other = lax.dynamic_slice_in_dim(rows, (1 - mine) * tokens, tokens, 0)
    return own + lax.ppermute(other.astype(BF16), "tensor", SWAP).astype(F32)


def greet_all(size, me):
    barrier = pltpu.get_barrier_semaphore()
    for step in range(1, size):
        pl.semaphore_signal(
            barrier, inc=1, device_id={"ctx": (me + step) % size}, device_id_type=MESH
        )
    there = 1 - lax.axis_index("section")
    pl.semaphore_signal(barrier, inc=1, device_id={"section": there}, device_id_type=MESH)
    pl.semaphore_wait(barrier, size)


def by_distance(size):
    return sorted(range(size), key=lambda step: min(step, size - step))


def share_job(size, from_ref, all_ref, send, recv, over_send, over_recv, local):
    me = lax.axis_index("ctx")
    section = lax.axis_index("section")
    order = by_distance(size)[1:]

    def copy(there, source):
        return remote(
            from_ref.at[:, there],
            all_ref.at[section, :, source],
            send.at[there],
            recv.at[source],
            {"ctx": there},
        )

    def over(block, source):
        return remote(
            block,
            all_ref.at[section, :, source],
            over_send.at[source],
            over_recv.at[source],
            {"section": 1 - section},
        )

    def own():
        return pltpu.make_async_copy(from_ref.at[:, me], all_ref.at[section, :, me], local)

    def start():
        own().start()
        over(from_ref.at[:, me], me).start()
        for step in order[:2]:
            copy((me + step) % size, me).start()

    def stage(index):
        step = order[index]
        source = (me + size - step) % size
        copy(source, source).wait_recv()
        over(all_ref.at[section, :, source], source).start()
        copy((me + step) % size, me).wait_send()
        if index + 2 < len(order):
            copy((me + order[index + 2]) % size, me).start()

    def finish():
        own().wait()
        for step in range(size):
            source = (me + step) % size
            over(all_ref.at[section, :, source], source).wait()

    return start, stage, finish


def share(blocks):
    moved = lax.all_to_all(blocks, "ctx", split_axis=1, concat_axis=1, tiled=True)
    return lax.all_gather(moved, "section")


def collect_kernel(
    size, first_ref, second_ref, to_ref, own, other, send, recv, over_send, over_recv, local, store
):
    me = lax.axis_index("ctx")
    section = lax.axis_index("section")
    greet_all(size, me)
    order = by_distance(size)[::-1]

    def over(source_ref, at):
        return remote(
            source_ref.at[:, at], other.at[at], over_send.at[at], over_recv.at[at],
            {"section": 1 - section},
        )

    def load(source_ref, at):
        return pltpu.make_async_copy(source_ref.at[:, at], own.at[at], local.at[at])

    def copy(there, source):
        return remote(
            own.at[there], to_ref.at[:, source], send.at[there], recv.at[source], {"ctx": there}
        )

    def start(at):
        @pl.when(section == 0)
        def _():
            over(second_ref, at).start()
            load(first_ref, at).start()

        @pl.when(section == 1)
        def _():
            over(first_ref, at).start()
            load(second_ref, at).start()

    for index, step in enumerate(order):
        at = (me + step) % size
        if index == 0:
            start(at)
        if index + 1 < size:
            start((me + order[index + 1]) % size)
        over(first_ref, at).wait()
        load(first_ref, at).wait()
        own[at] = (own[at].astype(F32) + other[at].astype(F32)).astype(own.dtype)
        if step > 0:
            copy(at, me).start()
        else:
            mine = pltpu.make_async_copy(own.at[at], to_ref.at[:, me], store)
            mine.start()
            mine.wait()
    for step in order:
        at = (me + step) % size
        if step > 0:
            copy(at, at).wait_recv()
            copy(at, me).wait_send()


def collect(first, second, is_first):
    parts, size, rows, columns = first.shape
    if size != 8:
        received = lax.ppermute(jnp.where(is_first, second, first), "section", SWAP)
        total = jnp.where(is_first, first, second).astype(F32) + received.astype(F32)
        return lax.all_to_all(
            total.astype(BF16), "ctx", split_axis=1, concat_axis=1, tiled=True
        )
    dma = pltpu.SemaphoreType.DMA
    block = pltpu.VMEM((size, parts, rows, columns), first.dtype)
    return pl.pallas_call(
        functools.partial(collect_kernel, size),
        out_shape=jax.ShapeDtypeStruct(first.shape, first.dtype),
        in_specs=[HBM, HBM],
        out_specs=HBM,
        scratch_shapes=[block, block]
        + [dma((size,)), dma((size,)), dma((size,)), dma((size,)), dma((size,)), dma],
        compiler_params=pltpu.CompilerParams(
            collective_id=6, has_side_effects=True, vmem_limit_bytes=24 << 20
        ),
        cost_estimate=pl.CostEstimate(flops=first.size, bytes_accessed=1024, transcendentals=0),
        name="collect",
    )(first, second)


def join_kernel(blocks_ref, out_ref):
    parts, size = blocks_ref.shape[:2]
    for part in range(parts):
        pieces = [blocks_ref[part, index].astype(F32) for index in range(size)]
        out_ref[:, part, :] = jnp.concatenate(pieces, axis=1)


def join(blocks):
    parts, size, rows, columns = blocks.shape
    if size != 8:
        joined = jnp.transpose(blocks, (2, 0, 1, 3))
        return joined.reshape(rows, parts, size * columns).astype(F32)
    tile = 32
    return pl.pallas_call(
        join_kernel,
        grid=(rows // tile,),
        out_shape=jax.ShapeDtypeStruct((rows, parts, size * columns), F32),
        in_specs=[pl.BlockSpec((parts, size, tile, columns), lambda index: (0, 0, index, 0))],
        out_specs=pl.BlockSpec((tile, parts, size * columns), lambda index: (index, 0, 0)),
        compiler_params=pltpu.CompilerParams(vmem_limit_bytes=32 << 20),
        name="join",
    )(blocks)


def cut_kernel(rows_ref, out_ref):
    parts, size = out_ref.shape[:2]
    columns = out_ref.shape[3]
    for part in range(parts):
        values = rows_ref[:, part, :]
        for index in range(size):
            out_ref[part, index] = values[:, index * columns : (index + 1) * columns]


def cut(values, size):
    rows, parts, columns = values.shape
    columns //= size
    if size != 8:
        return jnp.transpose(values.reshape(rows, parts, size, columns), (1, 2, 0, 3))
    tile = 32
    return pl.pallas_call(
        cut_kernel,
        grid=(rows // tile,),
        out_shape=jax.ShapeDtypeStruct((parts, size, rows, columns), values.dtype),
        in_specs=[pl.BlockSpec((tile, parts, size * columns), lambda index: (index, 0, 0))],
        out_specs=pl.BlockSpec((parts, size, tile, columns), lambda index: (0, 0, index, 0)),
        compiler_params=pltpu.CompilerParams(vmem_limit_bytes=32 << 20),
        name="cut",
    )(values)


def remote(src, dst, send, recv, device):
    return pltpu.make_async_remote_copy(
        src_ref=src, dst_ref=dst, send_sem=send, recv_sem=recv, device_id=device, device_id_type=MESH
    )


def spread_kernel(
    chunk, piece, layer, planes, gathered, reduced, ins, outs, extra, own_ref, *refs
):
    in_refs, refs = refs[:ins], refs[ins:]
    all_ref, sum_ref = refs[:2]
    out_refs, refs = refs[2 : 2 + outs], refs[2 + outs :]
    work_refs, refs = refs[:extra], refs[extra:]
    (expand_w, load_sem), refs = refs[:2], refs[2:]
    load = pltpu.make_async_copy(in_refs[0].at[layer], expand_w, load_sem)
    load.start()
    in_refs = (expand_w,) + in_refs[1:]
    (land, core_out, core_in, y_out, y_in, z_out, z_in, both, kept,
     zs, zr, ys, yr, cs, cr, rcs, rcr, rys, ryr, rzs, rzr, local) = refs
    tensor = lax.axis_index("tensor")
    ctx = lax.axis_index("ctx")
    plane, core = ctx // 2, ctx % 2
    rows = own_ref.shape[0] // (4 * planes if gathered else 1)
    y_peer = {"tensor": 1 - tensor}
    core_peer = {"ctx": plane * 2 + 1 - core}

    barrier = pltpu.get_barrier_semaphore()
    pl.semaphore_signal(barrier, inc=1, device_id=y_peer, device_id_type=MESH)
    pl.semaphore_signal(barrier, inc=1, device_id=core_peer, device_id_type=MESH)
    for step in range(1, planes):
        there = (plane + step) % planes
        pl.semaphore_signal(barrier, inc=1, device_id={"ctx": there * 2 + core}, device_id_type=MESH)
    pl.semaphore_wait(barrier, planes + 1)

    def block(at, which_core, which_tensor):
        start = pl.multiple_of(((at * 2 + which_core) * 2 + which_tensor) * rows, rows)
        return land.at[pl.ds(start, rows)]

    def along(at, target, direction):
        ref = block(at, core, tensor)
        return remote(ref, ref, zs.at[at, direction], zr.at[at], {"ctx": target * 2 + core})

    def across(at, which_tensor):
        ref = block(at, core, which_tensor)
        return remote(ref, ref, ys.at[at], yr.at[at], y_peer)

    def beside(at, which_core, which_tensor, slot):
        ref = block(at, which_core, which_tensor)
        return remote(ref, ref, cs.at[at, slot], cr.at[at, slot], core_peer)

    if not gathered:
        start = pl.multiple_of(((plane * 2 + core) * 2 + tensor) * rows, rows)
        land[pl.ds(start, rows)] = own_ref[...]

        @pl.when(plane < planes - 1)
        def _():
            along(plane, plane + 1, 0).start()

        @pl.when(plane > 0)
        def _():
            along(plane, plane - 1, 1).start()

        across(plane, tensor).start()
        beside(plane, core, tensor, 0).start()

    def reduce_core(at):
        return remote(core_out.at[at], core_in.at[at], rcs.at[at], rcr.at[at], core_peer)

    def reduce_y(at):
        return remote(y_out.at[at], y_in.at[at], rys.at[at], ryr.at[at], y_peer)

    def reduce_z(at):
        return remote(z_out.at[at], z_in.at[plane], rzs.at[at], rzr.at[plane], {"ctx": at * 2 + core})

    def reduced_z(at):
        return remote(z_out.at[at], z_in.at[at], rzs.at[at], rzr.at[at], {"ctx": at * 2 + core})

    def save(at):
        span = pl.ds(pl.multiple_of(at * 4 * rows, 4 * rows), 4 * rows)
        return pltpu.make_async_copy(land.at[span], all_ref.at[span], local.at[at])

    def side_plane(distance, side):
        return plane + distance * (2 * side - 1)

    def inside(at):
        return jnp.logical_and(at >= 0, at < planes)

    def pass_on(distance, side):
        at = side_plane(distance, side)
        target = plane + 1 - 2 * side

        @pl.when(inside(at))
        def _():
            along(at, plane, 0).wait_recv()

            @pl.when(inside(target))
            def _():
                along(at, target, side).start()

            across(at, tensor).start()
            beside(at, core, tensor, 0).start()

    def pass_beside(distance, side):
        at = side_plane(distance, side)

        @pl.when(inside(at))
        def _():
            across(at, 1 - tensor).wait_recv()
            beside(at, core, 1 - tensor, 1).start()

    def fetch(at):
        span = pl.ds(pl.multiple_of(at * 4 * rows, 4 * rows), 4 * rows)
        return pltpu.make_async_copy(own_ref.at[span], land.at[span], local.at[at])

    if gathered:
        for at in range(planes):
            fetch(at).start()

    def step(index, carry):
        if gathered:
            index = 2 * planes - 2 - index
        distance = (index + 1) // 2
        at = side_plane(distance, 1 - index % 2)

        if not gathered:

            @pl.when(jnp.logical_or(index == 0, index % 2 == 1))
            def _():
                pass_on(distance + 1, 0)
                pass_on(distance + 1, 1)

                @pl.when(distance > 0)
                def _():
                    pass_beside(distance, 0)

                pass_beside(distance, 1)

        @pl.when(inside(at))
        def _():
            if gathered:
                fetch(at).wait()
            else:
                beside(at, 1 - core, tensor, 0).wait_recv()
                beside(at, 1 - core, 1 - tensor, 1).wait_recv()
            if piece is None:
                save(at).start()
            theirs = pl.multiple_of((at * 2 + 1 - core) * 2 * rows, 2 * rows)
            mine = pl.multiple_of((at * 2 + core) * 2 * rows, 2 * rows)
            if not reduced:
                for start in (theirs, mine):
                    part = chunk(land, start, 2 * rows, in_refs, out_refs, work_refs)
                    sum_ref[pl.ds(start, 2 * rows)] = part.astype(BF16)
                return
            core_out[at] = chunk(land, theirs, 2 * rows, in_refs, out_refs, work_refs).astype(BF16)
            reduce_core(at).start()
            both[...] = chunk(land, mine, 2 * rows, in_refs, out_refs, work_refs)
            reduce_core(at).wait_recv()
            both[...] += core_in[at].astype(F32)
            other = pl.multiple_of((1 - tensor) * rows, rows)
            own = pl.multiple_of(tensor * rows, rows)
            y_out[at] = both[pl.ds(other, rows)].astype(BF16)

            @pl.when(index > 0)
            def _():
                reduce_y(at).start()

            kept[at] = both[pl.ds(own, rows)]

        return carry

    load.wait()
    lax.fori_loop(0, 2 * planes - 1, step, 0)

    if reduced:
        reduce_y(plane).start()

        def collect(index, count):
            if gathered:
                index = 2 * planes - 3 - index
            at = side_plane((index + 2) // 2, index % 2)

            @pl.when(inside(at))
            def _():
                if piece is not None:
                    piece(land, count, planes, in_refs, out_refs, work_refs)
                reduce_y(at).wait_recv()
                z_out[at] = (kept[at] + y_in[at].astype(F32)).astype(BF16)
                reduce_z(at).start()

            return count + inside(at).astype(jnp.int32)

        count = lax.fori_loop(0, 2 * planes - 2, collect, 0)
        if piece is not None:
            piece(land, count, planes, in_refs, out_refs, work_refs)
        reduce_y(plane).wait_recv()
        sum_ref[...] = kept[plane] + y_in[plane].astype(F32)

        def finish(index, carry):
            at = (plane + 1 + index) % planes
            reduced_z(at).wait_recv()
            sum_ref[...] += z_in[at].astype(F32)
            return carry

        lax.fori_loop(0, planes - 1, finish, 0)

    if not gathered:
        @pl.when(plane < planes - 1)
        def _():
            along(plane, plane + 1, 0).wait_send()

        @pl.when(plane > 0)
        def _():
            along(plane, plane - 1, 1).wait_send()

    def drain(index, carry):
        distance = (index + 1) // 2
        side = 1 - index % 2
        at = side_plane(distance, side)
        target = plane + 1 - 2 * side

        @pl.when(inside(at))
        def _():
            if not gathered:

                @pl.when(jnp.logical_and(index > 0, inside(target)))
                def _():
                    along(at, target, side).wait_send()

                across(at, tensor).wait_send()
                beside(at, core, tensor, 0).wait_send()
                beside(at, core, 1 - tensor, 1).wait_send()
            if piece is None:
                save(at).wait()
            if reduced:
                reduce_core(at).wait_send()
                reduce_y(at).wait_send()

                @pl.when(index > 0)
                def _():
                    reduce_z(at).wait_send()

        return carry

    lax.fori_loop(0, 2 * planes - 1, drain, 0)


def spread(chunk, piece, own, inputs, layer, outputs, work, planes, ident, name, reduced=True):
    rows, width = own.shape
    gathered = rows == inputs[2].shape[0] if len(inputs) > 2 else False
    if gathered:
        rows //= 4 * planes
    count = planes * 4 * rows
    dma = pltpu.SemaphoreType.DMA
    shape = jax.ShapeDtypeStruct
    saved = (count, width) if piece is None else (16, width)
    total = shape((rows, width), F32) if reduced else shape((count, width), BF16)
    outs = [shape(saved, BF16), total] + list(outputs)
    held = planes if reduced else 1
    return pl.pallas_call(
        functools.partial(
            spread_kernel, chunk, piece, layer, planes, gathered, reduced, len(inputs), len(outputs), len(work)
        ),
        out_shape=outs,
        in_specs=[HBM if gathered else VMEM, HBM] + [VMEM] * (len(inputs) - 1),
        out_specs=[HBM, VMEM] + [VMEM] * len(outputs),
        scratch_shapes=list(work)
        + [
            pltpu.VMEM(inputs[0].shape[1:], BF16),
            pltpu.SemaphoreType.DMA,
            pltpu.VMEM((count, width), BF16),
            pltpu.VMEM((held, 2 * rows, width), BF16),
            pltpu.VMEM((held, 2 * rows, width), BF16),
            pltpu.VMEM((held, rows, width), BF16),
            pltpu.VMEM((held, rows, width), BF16),
            pltpu.VMEM((held, rows, width), BF16),
            pltpu.VMEM((held, rows, width), BF16),
            pltpu.VMEM((2 * rows, width), F32),
            pltpu.VMEM((held, rows, width), F32),
            dma((planes, 2)), dma((planes,)), dma((planes,)), dma((planes,)), dma((planes, 2)), dma((planes, 2)),
            dma((planes,)), dma((planes,)), dma((planes,)), dma((planes,)), dma((planes,)), dma((planes,)), dma((planes,)),
        ],
        compiler_params=pltpu.CompilerParams(collective_id=ident + 10 * layer, has_side_effects=True, vmem_limit_bytes=62 << 20),
        cost_estimate=pl.CostEstimate(
            flops=count * width, bytes_accessed=count, transcendentals=0
        ),
        name=name,
    )(own, *inputs)


def mlp_chunk(land, start, rows, in_refs, out_refs, work_refs):
    expand_w, down_w = in_refs
    gate_slope, up_slope, hidden_ref = out_refs
    span = pl.ds(start, rows)
    x = land[span]
    gate = dot(x, expand_w[0])
    up = dot(x, expand_w[1])
    sig = jax.nn.sigmoid(gate)
    silu = gate * sig
    hidden = (silu * up).astype(BF16)
    gate_slope[span] = (up * sig * (1.0 + gate * (1.0 - sig))).astype(BF16)
    up_slope[span] = silu.astype(BF16)
    hidden_ref[span] = hidden
    return dot(hidden, down_w[...])


def mlp_back_chunk(land, start, rows, in_refs, out_refs, work_refs):
    expand_w, down_w, gate_slope, up_slope = in_refs[:4]
    gate_ref, up_ref = work_refs
    span = pl.ds(start, rows)
    grad_hidden = dot(land[span], down_w[...], LAST)
    grad_gate = (grad_hidden * gate_slope[span].astype(F32)).astype(BF16)
    grad_up = (grad_hidden * up_slope[span].astype(F32)).astype(BF16)
    gate_ref[span] = grad_gate
    up_ref[span] = grad_up
    return dot(grad_gate, expand_w[0], LAST) + dot(grad_up, expand_w[1], LAST)


def mlp_back_piece(land, index, pieces, in_refs, out_refs, work_refs):
    normed, hidden = in_refs[4:]
    gate_ref, up_ref = work_refs
    d_expand, d_down = out_refs
    size = d_expand.shape[1] // pieces
    span = pl.ds(pl.multiple_of(index * size, size), size)
    rows = normed[:, span]
    d_expand[0, span] = dot(rows, gate_ref[...], ROWS).astype(BF16)
    d_expand[1, span] = dot(rows, up_ref[...], ROWS).astype(BF16)
    d_down[:, span] = dot(hidden[...], land[:, span], ROWS).astype(BF16)


def mlp_forward(own, expand, layer, down_w, planes):
    count = planes * 4 * own.shape[0]
    shape = jax.ShapeDtypeStruct((count, down_w.shape[0]), BF16)
    return spread(
        mlp_chunk,
        None,
        own,
        (expand, down_w),
        layer,
        (shape,) * 3,
        (),
        planes,
        1,
        "mlp_forward",
        layer == 0,
    )


def mlp_backward(own, expand, layer, down_w, gate_slope, up_slope, normed, hidden, planes):
    d_expand = jax.ShapeDtypeStruct(expand.shape[1:], BF16)
    reduce = jax.ShapeDtypeStruct(down_w.shape, BF16)
    work = pltpu.VMEM(gate_slope.shape, BF16)
    return spread(
        mlp_back_chunk,
        mlp_back_piece,
        own,
        (expand, down_w, gate_slope, up_slope, normed, hidden),
        layer,
        (d_expand, reduce),
        (work, work),
        planes,
        2,
        "mlp_backward",
    )[1:]


def feed_forward(own, expand_layer, down_w):
    planes = lax.axis_size("ctx") // 2
    if planes == 4:
        rows, total, *kept = mlp_forward(own, *expand_layer, down_w, planes)
        return rows, total if expand_layer[1] == 0 else scatter_tokens(total), *kept
    expand = expand_layer[0][expand_layer[1]]
    rows = gather_tokens(own)
    gate, up = dot(rows, expand[0]), dot(rows, expand[1])
    sig = jax.nn.sigmoid(gate)
    silu = gate * sig
    hidden = (silu * up).astype(BF16)
    gate_slope = (up * sig * (1.0 + gate * (1.0 - sig))).astype(BF16)
    total = scatter_tokens(dot(hidden, down_w).astype(BF16))
    return rows, total, gate_slope, silu.astype(BF16), hidden


def feed_backward(own, expand_layer, down_w, gate_slope, up_slope, normed, hidden):
    planes = lax.axis_size("ctx") // 2
    if planes == 4:
        return mlp_backward(
            own, *expand_layer, down_w, gate_slope, up_slope, normed, hidden, planes
        )
    expand = expand_layer[0][expand_layer[1]]
    rows = own if own.shape[0] == normed.shape[0] else gather_tokens(own)
    grad_hidden = dot(rows, down_w, LAST)
    grad_gate = (grad_hidden * gate_slope.astype(F32)).astype(BF16)
    grad_up = (grad_hidden * up_slope.astype(F32)).astype(BF16)
    part = dot(grad_gate, expand[0], LAST) + dot(grad_up, expand[1], LAST)
    return (
        scatter_tokens(part.astype(BF16)),
        jnp.stack([dot(normed, grad_gate, ROWS), dot(normed, grad_up, ROWS)]).astype(BF16),
        dot(hidden, rows, ROWS).astype(BF16),
    )


def greet_line(planes, plane, core):
    barrier = pltpu.get_barrier_semaphore()
    pl.semaphore_signal(
        barrier, inc=1, device_id={"ctx": plane * 2 + 1 - core}, device_id_type=MESH
    )
    for step in range(1, planes):
        there = (plane + step) % planes
        pl.semaphore_signal(
            barrier, inc=1, device_id={"ctx": there * 2 + core}, device_id_type=MESH
        )
    pl.semaphore_wait(barrier, planes)


def attend_kernel(planes, heads, with_job, *refs):
    mixed_ref, cosine_ref, sine_ref, qpos_ref, kpos_ref = refs[:5]
    if with_job:
        out_ref, low_ref, log_ref, all_ref, q_ref = refs[6:11]
        zs, zr, cs, cr = refs[12:16]
        start, stage, finish = share_job(2 * planes, refs[5], refs[11], *refs[16:])
    else:
        out_ref, low_ref, log_ref, all_ref, q_ref, zs, zr, cs, cr = refs[5:]
    ctx = lax.axis_index("ctx")
    plane, core = ctx // 2, ctx % 2
    batch, tokens = qpos_ref.shape[:2]
    head_dim = cosine_ref.shape[1]
    query_width = heads * head_dim
    factor = 1.0 / math.sqrt(head_dim)
    if with_job:
        greet_all(2 * planes, ctx)
    else:
        greet_line(planes, plane, core)
    core_peer = {"ctx": plane * 2 + 1 - core}

    def block(at):
        return all_ref.at[:, pl.ds(pl.multiple_of(at * tokens, tokens), tokens)]

    def along(there, source):
        ref = block(source * 2 + core)
        return remote(ref, ref, zs.at[there], zr.at[source], {"ctx": there * 2 + core})

    def beside(source, which):
        ref = block(source * 2 + which)
        return remote(ref, ref, cs.at[source], cr.at[source], core_peer)

    def turned(rows, span):
        values = mixed_ref[rows, span]
        return values * cosine_ref[rows] + pltpu.roll(values, head_dim // 2, 1) * sine_ref[rows]

    own = pl.ds(pl.multiple_of(ctx * tokens, tokens), tokens)
    for index in range(batch):
        rows = slice(index * tokens, (index + 1) * tokens)
        keys = turned(rows, slice(query_width, query_width + head_dim))
        all_ref[index, own, :head_dim] = keys.astype(BF16)
        all_ref[index, own, head_dim:] = mixed_ref[rows, query_width + head_dim :].astype(BF16)
    for step in range(1, planes):
        along((plane + step) % planes, plane).start()
    beside(plane, core).start()
    if with_job:
        start()
    for step in range(1, planes):
        source = (plane + step) % planes
        along(source, source).wait_recv()
        beside(source, core).start()
    for step in range(planes):
        beside((plane + step) % planes, 1 - core).wait_recv()

    def one(index, carry):
        rows = pl.ds(pl.multiple_of(index * tokens, tokens), tokens)
        keys = all_ref[index, :, :head_dim]
        values = all_ref[index, :, head_dim:]
        allowed = qpos_ref[index] >= kpos_ref[index]
        lane = lax.broadcasted_iota(jnp.int32, (tokens, head_dim), 1)
        logs = jnp.zeros((tokens, head_dim), F32)
        for head in range(heads):
            span = slice(head * head_dim, (head + 1) * head_dim)
            queries = turned(rows, span).astype(BF16)
            q_ref[rows, span] = queries
            scores = dot(queries, keys, LAST)
            scores = jnp.where(allowed, scores * factor, -1e30)
            top = jnp.max(scores, axis=1, keepdims=True)
            weights = jnp.exp(scores - top)
            total = jnp.sum(weights, axis=1, keepdims=True)
            logs = jnp.where(lane == head, top + jnp.log(total), logs)
            out = dot((weights * (1.0 / total)).astype(BF16), values)
            out_ref[rows, span] = out
            low_ref[rows, span] = out.astype(BF16)
        log_ref[rows] = logs
        return carry

    if with_job:
        stages = 2 * planes - 1
        for index in range(batch):
            stage(index)
            one(index, 0)
        for index in range(batch, stages):
            stage(index)
        finish()
    else:
        lax.fori_loop(0, batch, one, 0)
    for step in range(1, planes):
        along((plane + step) % planes, plane).wait_send()
        beside((plane + step) % planes, core).wait_send()
    beside(plane, core).wait_send()


def attend_back_kernel(
    planes, heads, q_ref, kv_ref, qpos_ref, kpos_ref, grad_ref, out_ref, log_ref, cosine_ref,
    sine_ref, mixed_ref, dkv_ref, whole, core_out, core_in, z_out, z_in, cs, cr, zs, zr,
):
    ctx = lax.axis_index("ctx")
    plane, core = ctx // 2, ctx % 2
    batch = qpos_ref.shape[0]
    tokens = q_ref.shape[0] // batch
    head_dim = kv_ref.shape[2] // 2
    factor = 1.0 / math.sqrt(head_dim)
    greet_line(planes, plane, core)
    core_peer = {"ctx": plane * 2 + 1 - core}

    def turned_back(grads, rows):
        rolled = pltpu.roll(grads, head_dim // 2, 1)
        return (grads * cosine_ref[rows] - rolled * sine_ref[rows]).astype(BF16)

    def to_core(index):
        return remote(core_out.at[index], core_in.at[index], cs.at[index], cr.at[index], core_peer)

    def to_plane(index, there, source):
        return remote(
            z_out.at[index, there],
            z_in.at[index, source],
            zs.at[index, there],
            zr.at[index, source],
            {"ctx": there * 2 + core},
        )

    def one(index, carry):
        rows = pl.ds(pl.multiple_of(index * tokens, tokens), tokens)
        keys = kv_ref[index, :, :head_dim]
        values = kv_ref[index, :, head_dim:]
        allowed = qpos_ref[index] >= kpos_ref[index]
        logs = log_ref[rows]
        for head in range(heads):
            span = slice(head * head_dim, (head + 1) * head_dim)
            queries = q_ref[rows, span]
            grads = grad_ref[rows, span]
            delta = jnp.sum(grads.astype(F32) * out_ref[rows, span], axis=1, keepdims=True)
            scores = jnp.where(allowed, dot(queries, keys, LAST) * factor, -1e30)
            weights = jnp.exp(scores - logs[:, head : head + 1])
            grad_scores = (weights * (dot(grads, values, LAST) - delta) * factor).astype(BF16)
            mixed_ref[rows, span] = turned_back(dot(grad_scores, keys), rows)
            grad_keys = dot(grad_scores, queries, ROWS)
            grad_values = dot(weights.astype(BF16), grads, ROWS)
            if head == 0:
                whole[index, :, :head_dim] = grad_keys
                whole[index, :, head_dim:] = grad_values
            else:
                whole[index, :, :head_dim] += grad_keys
                whole[index, :, head_dim:] += grad_values

        for at in range(planes):
            theirs = pl.multiple_of((at * 2 + 1 - core) * tokens, tokens)
            core_out[index, at] = whole[index, pl.ds(theirs, tokens)].astype(BF16)
        to_core(index).start()
        return carry

    lax.fori_loop(0, batch, one, 0)

    def mine(index, at):
        start = pl.multiple_of((at * 2 + core) * tokens, tokens)
        return whole[index, pl.ds(start, tokens)] + core_in[index, at].astype(F32)

    for index in range(batch):
        to_core(index).wait_recv()
        for step in range(1, planes):
            there = (plane + step) % planes
            z_out[index, there] = mine(index, there).astype(BF16)
            to_plane(index, there, plane).start()
        dkv_ref[index] = mine(index, plane)
    for index in range(batch):
        for step in range(1, planes):
            source = (plane + step) % planes
            to_plane(index, source, source).wait_recv()
            dkv_ref[index] += z_in[index, source].astype(F32)
        rows = slice(index * tokens, (index + 1) * tokens)
        width = heads * head_dim
        mixed_ref[rows, width : width + head_dim] = turned_back(dkv_ref[index, :, :head_dim], rows)
        mixed_ref[rows, width + head_dim :] = dkv_ref[index, :, head_dim:].astype(BF16)
    for index in range(batch):
        to_core(index).wait_send()
        for step in range(1, planes):
            to_plane(index, (plane + step) % planes, plane).wait_send()


def attend(mixed, tables, heads, blocks):
    cosine, sine, query_pos, key_pos, _ = tables
    batch, tokens = query_pos.shape
    head_dim = cosine.shape[1]
    query_width = heads * head_dim
    pair = 2 * head_dim
    planes = lax.axis_size("ctx") // 2
    keys = key_pos.shape[1]
    rows = batch * tokens
    if planes != 4:
        queries = rotate(
            mixed[:, :query_width].reshape(rows, heads, head_dim),
            cosine[:, None, :],
            sine[:, None, :],
        ).astype(BF16).reshape(rows, query_width)
        own_keys = rotate(mixed[:, query_width : query_width + head_dim], cosine, sine)
        kv = jnp.concatenate([own_keys, mixed[:, query_width + head_dim :]], axis=1).astype(BF16)
        kv_all = gather_ctx(kv.reshape(batch, tokens, pair), 1)
        split = queries.reshape(batch, tokens, heads, head_dim)
        scores = jnp.einsum(
            "bqhd,bkd->bqhk", split, kv_all[..., :head_dim], preferred_element_type=F32
        )
        allowed = query_pos[:, :, None, None] >= key_pos[:, None, None, :]
        scores = jnp.where(allowed, scores / math.sqrt(head_dim), -1e30)
        logs = jax.nn.logsumexp(scores, axis=-1)
        probs = jnp.exp(scores - logs[..., None]).astype(BF16)
        out = jnp.einsum(
            "bqhk,bkd->bqhd", probs, kv_all[..., head_dim:], preferred_element_type=F32
        ).reshape(queries.shape)
        shared = [share(part) for part in blocks]
        return out, out.astype(BF16), logs, kv_all, queries, *shared
    size = 2 * planes
    shape = jax.ShapeDtypeStruct
    dma = pltpu.SemaphoreType.DMA
    return pl.pallas_call(
        functools.partial(attend_kernel, planes, heads, len(blocks) > 0),
        out_shape=[
            shape((rows, query_width), F32),
            shape((rows, query_width), BF16),
            shape((rows, head_dim), F32),
            shape((batch, keys, pair), BF16),
            shape((rows, query_width), BF16),
        ]
        + [shape((2,) + part.shape, part.dtype) for part in blocks],
        in_specs=[VMEM] * 5 + [HBM] * len(blocks),
        out_specs=[VMEM] * 5 + [HBM] * len(blocks),
        scratch_shapes=[dma((planes,)), dma((planes,)), dma((planes,)), dma((planes,))]
        + ([dma((size,))] * 4 + [dma]) * len(blocks),
        compiler_params=pltpu.CompilerParams(
            collective_id=3 + 2 * len(blocks), has_side_effects=True, vmem_limit_bytes=48 << 20
        ),
        cost_estimate=pl.CostEstimate(
            flops=rows * keys, bytes_accessed=rows, transcendentals=0
        ),
        name="attend",
    )(mixed, cosine, signed(sine), query_pos[:, :, None], key_pos[:, None, :], *blocks)


def signed(sine):
    half = sine.shape[1] // 2
    return jnp.concatenate([-sine[:, :half], sine[:, half:]], axis=1)


def attend_backward(queries, kv_all, tables, grads, out, logs):
    cosine, sine, query_pos, key_pos, _ = tables
    batch, keys, pair = kv_all.shape
    head_dim = pair // 2
    heads = queries.shape[1] // head_dim
    rows = queries.shape[0]
    tokens = rows // batch
    planes = lax.axis_size("ctx") // 2
    if planes != 4:
        factor = 1.0 / math.sqrt(head_dim)
        k_all, v_all = kv_all[..., :head_dim], kv_all[..., head_dim:]
        split = queries.reshape(batch, tokens, heads, head_dim)
        grad_split = grads.reshape(split.shape)
        delta = jnp.sum(grad_split.astype(F32) * out.reshape(split.shape), axis=-1)
        scores = jnp.einsum("bqhd,bkd->bqhk", split, k_all, preferred_element_type=F32)
        allowed = query_pos[:, :, None, None] >= key_pos[:, None, None, :]
        scores = jnp.where(allowed, scores * factor, -1e30)
        probs = jnp.exp(scores - logs[..., None])
        grad_probs = jnp.einsum("bqhd,bkd->bqhk", grad_split, v_all, preferred_element_type=F32)
        grad_scores = (probs * (grad_probs - delta[..., None]) * factor).astype(BF16)
        dq = jnp.einsum("bqhk,bkd->bqhd", grad_scores, k_all, preferred_element_type=F32)
        dk = jnp.einsum("bqhk,bqhd->bkd", grad_scores, split, preferred_element_type=F32)
        dv = jnp.einsum(
            "bqhk,bqhd->bkd", probs.astype(BF16), grad_split, preferred_element_type=F32
        )
        dkv = lax.psum_scatter(
            jnp.concatenate([dk, dv], axis=-1).astype(BF16), "ctx", scatter_dimension=1, tiled=True
        )
        dkv = dkv.astype(F32).reshape(rows, pair)
        dq = unrotate(dq.reshape(rows, heads, head_dim), cosine[:, None, :], sine[:, None, :])
        dk = unrotate(dkv[:, :head_dim], cosine, sine)
        parts = [dq.reshape(queries.shape), dk, dkv[:, head_dim:]]
        return jnp.concatenate(parts, axis=1).astype(BF16)
    shape = jax.ShapeDtypeStruct
    dma = pltpu.SemaphoreType.DMA
    return pl.pallas_call(
        functools.partial(attend_back_kernel, planes, heads),
        out_shape=shape((rows, queries.shape[1] + pair), BF16),
        in_specs=[VMEM] * 9,
        out_specs=VMEM,
        scratch_shapes=[
            pltpu.VMEM((batch, tokens, pair), F32),
            pltpu.VMEM((batch, keys, pair), F32),
            pltpu.VMEM((batch, planes, tokens, pair), BF16),
            pltpu.VMEM((batch, planes, tokens, pair), BF16),
            pltpu.VMEM((batch, planes, tokens, pair), BF16),
            pltpu.VMEM((batch, planes, tokens, pair), BF16),
            dma((batch,)), dma((batch,)), dma((batch, planes)), dma((batch, planes)),
        ],
        compiler_params=pltpu.CompilerParams(
            collective_id=4, has_side_effects=True, vmem_limit_bytes=48 << 20
        ),
        cost_estimate=pl.CostEstimate(
            flops=rows * keys, bytes_accessed=rows, transcendentals=0
        ),
        name="attend_backward",
    )(
        queries,
        kv_all,
        query_pos[:, :, None],
        key_pos[:, None, :],
        grads,
        out,
        logs,
        cosine,
        signed(sine),
    )


def layer_forward(x_low, weights, tables, blocks, sooner, later):
    gain_attn, w_mixed, bias, w_project, gain_mlp, w_expand, w_reduce = weights
    cosine, sine, query_pos, key_pos, mine = tables
    count, width = x_low.shape
    query_width = w_project.shape[0]
    head_dim = (w_mixed.shape[1] - query_width) // 2
    heads = query_width // head_dim
    batch = query_pos.shape[0]
    tokens = count // batch
    x = x_low.astype(F32)
    root_attn = inverse_root(x)
    normed = (x * root_attn * gain_attn).astype(BF16)
    mixed = dot(normed, w_mixed) + bias
    mixed, sooner = lax.optimization_barrier((mixed, sooner))
    attended_full, attended, log_total, kv, queries, *shared = attend(
        mixed, tables, heads, blocks
    )
    if shared:
        w_expand = (shared[0].reshape((2, 2, width, -1)), 0)
    x_mine = lax.dynamic_slice_in_dim(x, mine * tokens, tokens, 0)
    middle = x_mine + tensor_scatter(dot(attended, w_project))
    root_mlp = inverse_root(middle)
    normed_mlp = (middle * root_mlp * gain_mlp).astype(BF16)
    normed_mlp, later = lax.optimization_barrier((normed_mlp, later))
    all_normed, branch, gate_slope, up_slope, hidden = feed_forward(
        normed_mlp, w_expand, w_reduce
    )
    result = middle + branch
    kept = (
        x_mine,
        lax.dynamic_slice_in_dim(root_attn, mine * tokens, tokens, 0),
        normed,
        queries,
        kv,
        attended_full,
        log_total,
        attended,
        middle,
        root_mlp,
        all_normed,
        gate_slope,
        up_slope,
        hidden,
    )
    return result.astype(BF16), kept, w_expand, sooner, later


def layer_backward(grad_out, grad_rows, kept, weights, tables, route, earlier, pinned):
    gain_attn, w_mixed, bias, w_project, gain_mlp, w_expand, w_reduce = weights
    cosine, sine, query_pos, key_pos, mine = tables
    (
        x_mine,
        root_attn,
        normed,
        queries,
        kv,
        attended_full,
        log_total,
        attended,
        middle,
        root_mlp,
        all_normed,
        gate_slope,
        up_slope,
        hidden,
    ) = kept
    count, query_width = queries.shape
    head_dim = (w_mixed.shape[1] - query_width) // 2
    heads = query_width // head_dim
    grad_normed_mlp, d_expand, d_reduce = feed_backward(
        grad_rows,
        w_expand,
        w_reduce,
        gate_slope,
        up_slope,
        all_normed,
        hidden,
    )
    grad_normed_mlp, earlier = lax.optimization_barrier((grad_normed_mlp, earlier))
    if earlier:
        pinned = tuple(lax.ppermute(part, "section", SWAP[:1]) for part in earlier[:2])
    moved_reduce = lax.ppermute(d_reduce, "section", route)
    grad_middle, d_gain_mlp = norm_backward(middle, root_mlp, gain_mlp, grad_normed_mlp)
    grad_middle = grad_middle + grad_out
    grad_branch = tensor_pair(grad_middle.astype(BF16))
    grad_attended = dot(grad_branch, w_project, LAST).astype(BF16)
    grad_mixed = attend_backward(
        queries, kv, tables, grad_attended, attended_full, log_total
    )
    if earlier:
        d_project = dot(attended, grad_branch, ROWS)
    grad_mixed, moved_reduce, pinned, late_branch = lax.optimization_barrier(
        (grad_mixed, moved_reduce, pinned, grad_branch)
    )
    if not earlier:
        d_project = dot(attended, late_branch, ROWS)
    d_mixed = dot(normed, grad_mixed, ROWS)
    d_bias = jnp.sum(grad_mixed.astype(F32), axis=0)
    grad_normed = tensor_scatter(dot(grad_mixed, w_mixed, LAST))
    grad_x, d_gain_attn = norm_backward(x_mine, root_attn, gain_attn, grad_normed)
    grad_x = (grad_x + grad_middle).astype(BF16)
    vectors = (d_gain_attn, d_mixed, d_bias, d_project, d_gain_mlp)
    return grad_x, vectors, d_expand, (d_reduce, moved_reduce), earlier, pinned


def shards(
    block_input, positions, cotangent, norm_attn, w_qkv, b_qkv, w_out, norm_mlp, w_gate_up, w_down
):
    section = lax.axis_index("section")
    tensor = lax.axis_index("tensor")
    ctx = lax.axis_index("ctx")
    ctx_size = lax.axis_size("ctx")
    first = section == 0
    micro, tokens, width = block_input.shape
    half = micro // 2
    head_dim = w_qkv.shape[3] - w_out.shape[2] * ctx_size
    head_dim = head_dim // 2
    slice_width = norm_attn.shape[1]
    slice_bias = b_qkv.shape[2]
    units = w_down.shape[1]

    def plane_part(value):
        return lax.dynamic_slice_in_dim(value, section * half, half, 0)

    def layers(own, other):
        return jnp.where(first, own, other), jnp.where(first, other, own)

    x = plane_part(block_input).reshape(half * tokens, width)
    pos_local = plane_part(positions)
    cosine, sine = angles(pos_local.reshape(-1), head_dim)

    small = jnp.concatenate([norm_attn[0], norm_mlp[0], b_qkv[0, 0]])
    qkv, out = w_qkv[0, :, 0, :], w_out[0, 0]
    vectors = jnp.concatenate(layers(small, swap(small)))
    places = jnp.concatenate([pos_local // 64, pos_local % 64]).reshape(-1).astype(BF16)
    packed = gather_ctx(jnp.concatenate([vectors, places])[None], 0)
    places = packed[:, vectors.shape[0] :].astype(jnp.int32).reshape(ctx_size, 2, half, tokens)
    pos_all = jnp.swapaxes(places[:, 0] * 64 + places[:, 1], 0, 1).reshape(half, -1)
    tables = (cosine, sine, pos_local, pos_all, tensor)
    small_size = 2 * slice_width + slice_bias
    small0, small1 = packed[:, :small_size], packed[:, small_size : 2 * small_size]
    qkv0, qkv1 = layers(qkv, swap(qkv))
    out0, out1 = layers(out, swap(out))
    down_moved = swap(w_down[0])
    down0, down1 = layers(w_down[0], down_moved)
    blocks = cut(w_gate_up[0], ctx_size)

    def whole(small, qkv, out, expand, down):
        return (
            small[:, :slice_width].reshape(1, width),
            gather_ctx(qkv, 0),
            small[:, 2 * slice_width :].reshape(1, slice_bias * ctx_size),
            gather_ctx(out, 0),
            small[:, slice_width : 2 * slice_width].reshape(1, width),
            expand,
            down,
        )

    weights0 = whole(small0, qkv0, out0, None, down0)

    result0, kept0, expand0, down_moved, (qkv1, out1) = layer_forward(
        x, weights0, tables, (blocks,), down_moved, (qkv1, out1)
    )
    weights0 = weights0[:5] + (expand0, down0)
    weights1 = whole(small1, qkv1, out1, (expand0[0], 1), down1)
    x1 = tensor_pair(result0)
    seeds, x1 = lax.optimization_barrier((plane_part(cotangent), x1))
    seed_rows = gather_ctx(seeds.reshape(half * tokens, width), 0)
    result1, kept1, *_ = layer_forward(x1, weights1, tables, (), (), ())
    out1_all = tensor_pair(result1)

    def exchange(layer0, layer1):
        kept_here = jnp.where(first, layer0, layer1)
        received = swap(jnp.where(first, layer1, layer0))
        low = jnp.where(first, kept_here, received)
        high = jnp.where(first, received, kept_here)
        both = jnp.concatenate([low, high], axis=0)
        return both.reshape(1, micro, tokens, width)

    seed = lax.dynamic_slice_in_dim(seeds, tensor, 1, 0)[0].astype(F32)
    def ctx_scatter(value):
        return lax.psum_scatter(
            value.astype(BF16), "ctx", scatter_dimension=0, tiled=True
        )

    group = w_qkv.shape[3]
    split_at = group - head_dim

    def with_vectors(grads):
        gain_attn, mixed, bias, project, gain_mlp = grads[:5]
        rows = jnp.concatenate(
            [
                bias[:split_at].reshape(ctx_size, -1),
                bias[split_at:].reshape(ctx_size, -1),
                gain_attn.reshape(ctx_size, slice_width),
                gain_mlp.reshape(ctx_size, slice_width),
            ],
            axis=1,
        )
        rows = jnp.pad(rows[:, None, :], ((0, 0), (0, 15), (0, group - rows.shape[1])))
        mixed = mixed.reshape(ctx_size, slice_width, group)
        both = jnp.concatenate([mixed.astype(BF16), rows.astype(BF16)], axis=1)
        return both.reshape(ctx_size * (slice_width + 16), group)

    grad1, d1, d_expand1, d_reduce1, _, out1_all = layer_backward(
        seed, seed_rows, kept1, weights1, tables, [(0, 1)], (), out1_all
    )
    section_output = exchange(x1, out1_all)
    slices1 = (ctx_scatter(with_vectors(d1)), ctx_scatter(d1[3]))
    grad1_all = tensor_pair(grad1)
    grad0, d0, d_expand0, d_reduce0, earlier, moved1 = layer_backward(
        grad1.astype(F32), grad1, kept0, weights0, tables, [(1, 0)], slices1 + (section_output, grad1_all), ()
    )
    slices1, (section_output, grad1_all) = earlier[:2], earlier[2:]

    def to_owner(part0, part1, received1):
        received0 = lax.ppermute(part0.astype(BF16), "section", [(1, 0)])
        own = jnp.where(first, part0, part1).astype(F32)
        return own + jnp.where(first, received0, received1).astype(F32)

    def of_owner(pair0, pair1):
        own, received = (jnp.where(first, low, high).astype(F32) for low, high in zip(pair0, pair1))
        return own + received

    blocks = (2, ctx_size, slice_width, units)
    grad0_all = tensor_pair(grad0)
    grad0_all, d_expand0 = lax.optimization_barrier((grad0_all, d_expand0))
    input_grad = exchange(grad0_all, grad1_all)
    total = collect(d_expand0.reshape(blocks), d_expand1.reshape(blocks), first)
    d_expand = join(total)[None]
    d_reduce = of_owner(d_reduce0, d_reduce1)

    d_mixed = to_owner(ctx_scatter(with_vectors(d0)), slices1[0], moved1[0])
    d_project = to_owner(ctx_scatter(d0[3]), slices1[1], moved1[1])
    vectors = d_mixed[slice_width]
    d_mixed = d_mixed[:slice_width]
    count_qk, count_v = split_at // ctx_size, head_dim // ctx_size
    bias_qk = vectors[:count_qk][None]
    bias_v = vectors[count_qk : count_qk + count_v][None]
    start = count_qk + count_v
    gains = vectors[start : start + 2 * slice_width].reshape(1, 2 * slice_width)
    gains = gains + lax.ppermute(gains, "tensor", SWAP)
    return (
        section_output,
        input_grad,
        gains[:, :slice_width],
        d_mixed[None, :, None, :],
        bias_qk[None],
        bias_v[None],
        d_project[None, None],
        gains[:, slice_width:],
        d_expand,
        d_reduce[None],
    )


def solution(mesh):
    in_specs = (
        P(None, "ctx", None),
        P(None, "ctx"),
        P(None, "ctx", None),
        P("section", "ctx"),
        P("section", "ctx", "tensor", None),
        P("section", "tensor", "ctx"),
        P("section", "tensor", "ctx", None),
        P("section", "ctx"),
        P("section", "ctx", None, "tensor"),
        P("section", ("tensor", "ctx"), None),
    )
    out_specs = (
        P("section", None, "ctx", None),
        P("section", None, "ctx", None),
        P("section", "ctx"),
        P("section", "ctx", "tensor", None),
        P("section", "tensor", "ctx"),
        P("section", "tensor", "ctx"),
        P("section", "tensor", "ctx", None),
        P("section", "ctx"),
        P("section", "ctx", None, "tensor"),
        P("section", ("tensor", "ctx"), None),
    )
    return jax.shard_map(shards, mesh=mesh, in_specs=in_specs, out_specs=out_specs, check_vma=False)
```
